32 devices in a mesh: row: 4 (over y, core), col: 8 (over z, x).
Axes of the slice: x: 2, y: 2, z: 4, core: 2. Of those that a mesh axis runs over, the one named last changes fastest.
Arguments:
- solution: float32 [4, 8, 16, 128, 128], P('row', 'col'), may hold values from -6 to 6
- residual: float32 [4, 8, 16, 128, 128], P('row', 'col'), may hold values from -6 to 6, as said below
- prev_direction: float32 [4, 8, 16, 128, 128], P('row', 'col'), may hold values from -6 to 6, as said below
- prev_dot: float32 [128], replicated, may hold values from 32768 to 131072
- face_lists: int32 [4, 8, 4, 4], P('row', 'col'), may hold values from 0 to 16, as said below
- multiplicity: int32 [4, 8, 16], P('row', 'col'), may hold values from 1 to 2, as said below
- block_pattern: int32 [4, 8, 16, 3], P('row', 'col'), may hold values from 0 to 15, as said below
- schur: float32 [4, 8, 16, 3, 128, 128], P('row', 'col'), may hold values from -1 to 4, as said below
- neumann_inverse: float32 [4, 8, 16, 3, 128, 128], P('row', 'col'), may hold values from 0 to 2, as said below
- coarse_basis: float32 [4, 8, 8, 2048], P('row', 'col'), may hold values from -0.25 to 0.25
- primal_map: int32 [4, 8, 8], P('row', 'col'), may hold values from 0 to 255, all different within a row
- coarse_inverse: float32 [256, 256], P('col'), may hold values from -1 to 1, as said below
Outputs:
- new_solution: float32 [4, 8, 16, 128, 128], P('row', 'col')
- new_residual: float32 [4, 8, 16, 128, 128], P('row', 'col')
- direction: float32 [4, 8, 16, 128, 128], P('row', 'col')
The draws below stay inside these ranges and needn't reach their ends.
Inputs may be any that keep to these rules, and one draw needn't show every extreme that they name: face_lists[i, j, f, k] names the interface blocks that subdomain (i, j) shares with its neighbour across face f (0 toward row i-1, 1 toward row i+1, 2 toward column j-1, 3 toward column j+1); slot k of a face names the same unknowns as slot k of the neighbour's list for the facing face, and both lists have the same length, 1 to 4 blocks, none on faces at the grid's edge; unused slots hold 16; no block lies on two faces; some face holds 4 blocks. multiplicity is 2 for blocks named in face_lists and 1 for the others. block_pattern[i, j, b, 0] = b; the two other entries of block row b are two other blocks, each of which lists b in turn. `schur`: each subdomain's Schur complement is symmetric positive definite, with positive diagonal and no positive entry off it. `neumann_inverse`: each subdomain's local solve matrix is symmetric positive definite. `coarse_inverse`: symmetric positive definite. `residual`: copies of an unknown held by two subdomains (slot k of facing lists) are equal. `prev_direction`: copies of an unknown held by two subdomains (slot k of facing lists) are equal.
All inputs are finite; a program needn't handle non-finite values.
Results may differ from the reference program's by a relative error of at most 0.0003.
Values sent between devices are 32-bit elements; how exact they have to be, the bound alone decides.
No kernel may reach another device: no remote copies, remote signals or barrier semaphores. Data moves between devices by JAX's collectives and lax.ppermute only.
A program may use at most 128 MiB of HBM per device.

```python
import math
import jax
import jax.numpy as jnp
from jax import lax

BLOCKS = 16
BLOCK_DOFS = 128
FACE_SLOTS = 4
LOAD_CASES = 128
PRIMALS = 8
SUB_ROWS = 4
SUB_COLS = 8
COARSE_ROWS = 256


def face_layout(key):
    base = jax.random.fold_in(key, 7001)
    first_key, second_key, third_key = jax.random.split(base, 3)
    rows_len = jax.random.randint(first_key, (SUB_ROWS - 1, SUB_COLS), 1, FACE_SLOTS + 1)
    rows_len = rows_len.at[0, 0].set(FACE_SLOTS)
    cols_len = jax.random.randint(second_key, (SUB_ROWS, SUB_COLS - 1), 1, FACE_SLOTS + 1)
    cols_len = cols_len.at[0, 0].set(FACE_SLOTS)
    zero_row = jnp.zeros((1, SUB_COLS), jnp.int32)
    zero_col = jnp.zeros((SUB_ROWS, 1), jnp.int32)
    north = jnp.concatenate([zero_row, rows_len], axis=0)
    south = jnp.concatenate([rows_len, zero_row], axis=0)
    west = jnp.concatenate([zero_col, cols_len], axis=1)
    east = jnp.concatenate([cols_len, zero_col], axis=1)
    lengths = jnp.stack([north, south, west, east], axis=-1).astype(jnp.int32)
    starts = jnp.cumsum(lengths, axis=-1) - lengths
    scores = jax.random.randint(third_key, (SUB_ROWS, SUB_COLS, BLOCKS), 0, 1 << 20) * BLOCKS + jnp.arange(BLOCKS)
    order = jnp.argsort(scores, axis=-1).astype(jnp.int32)
    slots = jnp.arange(FACE_SLOTS).astype(jnp.int32)
    position = jnp.minimum(starts[..., None] + slots, BLOCKS - 1)
    picked = jnp.take_along_axis(order, position.reshape(SUB_ROWS, SUB_COLS, 4 * FACE_SLOTS), axis=-1)
    picked = picked.reshape(SUB_ROWS, SUB_COLS, 4, FACE_SLOTS)
    return jnp.where(slots < lengths[..., None], picked, BLOCKS).astype(jnp.int32)


def pattern_layout(key):
    base = jax.random.fold_in(key, 7002)
    scores = jax.random.randint(base, (SUB_ROWS, SUB_COLS, BLOCKS), 0, 1 << 20) * BLOCKS + jnp.arange(BLOCKS)
    order = jnp.argsort(scores, axis=-1).astype(jnp.int32)
    position = jnp.argsort(order, axis=-1).astype(jnp.int32)
    next_block = jnp.take_along_axis(order, (position + 1) % BLOCKS, axis=-1)
    prev_block = jnp.take_along_axis(order, (position + BLOCKS - 1) % BLOCKS, axis=-1)
    own_block = jnp.broadcast_to(jnp.arange(BLOCKS).astype(jnp.int32), next_block.shape)
    return jnp.stack([own_block, next_block, prev_block], axis=-1).astype(jnp.int32)


def draw_face_lists(key, part):
    return face_layout(key)


def draw_multiplicity(key, part):
    faces = face_layout(key)
    named = (faces[..., None] == jnp.arange(BLOCKS)).astype(jnp.int32)
    return (1 + jnp.sum(named, axis=(2, 3))).astype(jnp.int32)


def draw_block_pattern(key, part):
    return pattern_layout(key)


def symmetric_blocks(key, salt, lower, upper, diag_lower, diag_upper):
    pattern = pattern_layout(key)
    base = jax.random.fold_in(key, salt)
    first_key, second_key = jax.random.split(base)
    shape = (SUB_ROWS, SUB_COLS, BLOCKS, 3, BLOCK_DOFS, BLOCK_DOFS)
    uniform_draw = jax.random.uniform(first_key, shape, jnp.float32)
    random_draw = lower + (upper - lower) * uniform_draw
    subdomain = (jnp.arange(SUB_ROWS * SUB_COLS).reshape(SUB_ROWS, SUB_COLS, 1) * BLOCKS).astype(jnp.int32)
    flat_next = random_draw[:, :, :, 2].reshape(SUB_ROWS * SUB_COLS * BLOCKS, BLOCK_DOFS, BLOCK_DOFS)
    flat_prev = random_draw[:, :, :, 1].reshape(SUB_ROWS * SUB_COLS * BLOCKS, BLOCK_DOFS, BLOCK_DOFS)
    from_next = jnp.take(flat_next, (subdomain + pattern[..., 1]).reshape(-1), axis=0)
    from_prev = jnp.take(flat_prev, (subdomain + pattern[..., 2]).reshape(-1), axis=0)
    from_next = from_next.reshape(SUB_ROWS, SUB_COLS, BLOCKS, BLOCK_DOFS, BLOCK_DOFS)
    from_prev = from_prev.reshape(SUB_ROWS, SUB_COLS, BLOCKS, BLOCK_DOFS, BLOCK_DOFS)
    block_next = (random_draw[:, :, :, 1] + jnp.swapaxes(from_next, -1, -2)) * 0.5
    block_prev = (random_draw[:, :, :, 2] + jnp.swapaxes(from_prev, -1, -2)) * 0.5
    diagonal_block = (random_draw[:, :, :, 0] + jnp.swapaxes(random_draw[:, :, :, 0], -1, -2)) * 0.5
    log_values = jax.random.uniform(second_key, (SUB_ROWS, SUB_COLS, BLOCKS, BLOCK_DOFS), jnp.float32, jnp.log(diag_lower), jnp.log(diag_upper))
    diag_values = jnp.exp(log_values)
    identity = jnp.eye(BLOCK_DOFS, dtype=jnp.float32)
    diagonal_block = diagonal_block * (1.0 - identity) + diag_values[..., None] * identity
    return jnp.stack([diagonal_block, block_next, block_prev], axis=3)


def draw_schur(key, part):
    blocks = symmetric_blocks(key, 7003, -2.0 / (3 * BLOCK_DOFS), 0.0, 0.05, 2.0)
    identity = jnp.eye(BLOCK_DOFS, dtype=jnp.float32)
    shift = jnp.zeros((3, 1, 1), jnp.float32).at[0].set(2.0)
    return blocks + shift * identity


def draw_neumann_inverse(key, part):
    return symmetric_blocks(key, 7004, 0.0, 0.5 / (3 * BLOCK_DOFS), 0.6, 2.0)


def draw_coarse_inverse(key, part):
    base = jax.random.fold_in(key, 7005)
    first_key, second_key = jax.random.split(base)
    bound_value = 0.2 / COARSE_ROWS
    random_draw = jax.random.uniform(first_key, (COARSE_ROWS, COARSE_ROWS), jnp.float32, -bound_value, bound_value)
    symmetric = (random_draw + random_draw.T) * 0.5
    diag_values = jnp.exp(jax.random.uniform(second_key, (COARSE_ROWS,), jnp.float32, jnp.log(0.25), 0.0))
    identity = jnp.eye(COARSE_ROWS, dtype=jnp.float32)
    return symmetric * (1.0 - identity) + diag_values[:, None] * identity


def matched_field(key, salt):
    faces = face_layout(key)
    base = jax.random.fold_in(key, salt)
    shape = (SUB_ROWS, SUB_COLS, BLOCKS, BLOCK_DOFS, LOAD_CASES)
    random_draw = jnp.clip(jax.random.normal(base, shape, jnp.float32), -6.0, 6.0)
    subdomain = (jnp.arange(SUB_ROWS * SUB_COLS).reshape(SUB_ROWS, SUB_COLS, 1) * BLOCKS).astype(jnp.int32)
    result = random_draw
    for axis_number, mine_face, their_face in ((0, 0, 1), (1, 2, 3)):
        neighbour = jnp.roll(random_draw, 1, axis=axis_number).reshape(SUB_ROWS * SUB_COLS * BLOCKS, BLOCK_DOFS, LOAD_CASES)
        their_list = jnp.minimum(jnp.roll(faces[:, :, their_face], 1, axis=axis_number), BLOCKS - 1)
        incoming = jnp.take(neighbour, (subdomain + their_list).reshape(-1), axis=0)
        incoming = incoming.reshape(SUB_ROWS, SUB_COLS, FACE_SLOTS, BLOCK_DOFS, LOAD_CASES)
        mine_list = faces[:, :, mine_face]
        for slot_number in range(FACE_SLOTS):
            chosen = mine_list[:, :, slot_number][..., None] == jnp.arange(BLOCKS)
            result = jnp.where(chosen[..., None, None], incoming[:, :, slot_number][:, :, None], result)
    return result


def draw_residual(key, part):
    return matched_field(key, 7010)


def draw_prev_direction(key, part):
    return matched_field(key, 7011)


def shard_levels(own_key, extent, pieces, least, largest):
    loudness = 1.0
    for dim, shards_of in pieces:
        steps = jax.random.uniform(jax.random.fold_in(jax.random.fold_in(own_key, 6), dim), (shards_of,), jnp.float32, least / len(pieces), largest / len(pieces))
        loudness = loudness * jnp.repeat(jnp.exp(steps), extent[dim] // shards_of).reshape((-1,) + (1,) * (len(extent) - 1 - dim))
    return loudness


def picks_of(stream_key, rows, number_of, top, lift):
    order = jax.random.permutation(jax.random.fold_in(stream_key, 1), number_of)
    favour = order
    for power in range(3):
        favour = favour * favour // number_of
    favour = favour * lift // number_of
    chance = jax.random.randint(jax.random.fold_in(stream_key, 2), (rows, number_of), 0, 4096) + favour
    fixed_rows = jax.random.permutation(jax.random.fold_in(stream_key, 3), rows)[jnp.arange(number_of) % rows]
    chance = jnp.where(jnp.arange(rows)[:, None] == fixed_rows[None, :], 1 << 14, chance)
    priority = chance * number_of + jnp.arange(number_of)
    return lax.top_k(priority.astype(jnp.int32), top)[1].astype(jnp.int32)


def bell_draw(rng, shape, deviation, reach, shards=(), kind=jnp.bfloat16):
    level = shard_levels(rng, shape, shards, -0.22, 0.18) if shards else 1.0
    drawn = jax.random.normal(rng, shape, jnp.float32) * deviation * level
    return jnp.minimum(jnp.maximum(drawn, -reach), reach).astype(kind)


def setup_inputs(seed: int = 0) -> dict:
    streams_of = jax.random.split(jax.random.key(seed), 13)
    solution = bell_draw(streams_of[0], (SUB_ROWS, SUB_COLS, BLOCKS, BLOCK_DOFS, LOAD_CASES), 1.0, 6.0, ((0, 4), (1, 8)), jnp.float32)
    residual = draw_residual(jax.random.fold_in(streams_of[12], 71), 0)
    prev_direction = draw_prev_direction(jax.random.fold_in(streams_of[12], 71), 0)
    prev_dot = jnp.clip(jnp.exp(jax.random.uniform(streams_of[3], (LOAD_CASES,), jnp.float32, math.log(32768.0), math.log(131072.0))), 32768.0, 131072.0)
    face_lists = draw_face_lists(jax.random.fold_in(streams_of[12], 71), 0)
    multiplicity = draw_multiplicity(jax.random.fold_in(streams_of[12], 71), 0)
    block_pattern = draw_block_pattern(jax.random.fold_in(streams_of[12], 71), 0)
    schur = draw_schur(jax.random.fold_in(streams_of[12], 71), 0)
    neumann_inverse = draw_neumann_inverse(jax.random.fold_in(streams_of[12], 71), 0)
    coarse_basis = bell_draw(streams_of[9], (SUB_ROWS, SUB_COLS, PRIMALS, BLOCKS * BLOCK_DOFS), (BLOCKS * BLOCK_DOFS // 4) ** -0.5, 0.25, ((0, 4), (1, 8)), jnp.float32)
    primal_map = picks_of(streams_of[10], SUB_ROWS * SUB_COLS, COARSE_ROWS, PRIMALS, 256).reshape((SUB_ROWS, SUB_COLS, PRIMALS))
    coarse_inverse = draw_coarse_inverse(jax.random.fold_in(streams_of[12], 71), 0)
    return {"solution": solution, "residual": residual, "prev_direction": prev_direction, "prev_dot": prev_dot, "face_lists": face_lists, "multiplicity": multiplicity, "block_pattern": block_pattern, "schur": schur, "neumann_inverse": neumann_inverse, "coarse_basis": coarse_basis, "primal_map": primal_map, "coarse_inverse": coarse_inverse}


HIGH = lax.Precision.HIGHEST


def apply_blocks(blocks, pattern, values_in):
    def one_row(packed):
        row_blocks, row_pattern, row_values = packed
        columns = row_pattern.shape[0]
        count = row_pattern.shape[1] * row_pattern.shape[2]
        index = row_pattern.reshape(columns, count)[:, :, None, None]
        gathered = jnp.take_along_axis(row_values, index, axis=1)
        gathered = gathered.reshape(row_blocks.shape[:3] + row_values.shape[2:])
        return jnp.einsum("sbkij,sbkjn->sbin", row_blocks, gathered, precision=HIGH)
    return lax.map(one_row, (blocks, pattern, values_in))


def assemble(values_in, face_lists):
    blocks = values_in.shape[2]
    indicator = (face_lists[..., None] == jnp.arange(blocks)).astype(jnp.float32)
    face_values = jnp.einsum("ijfkb,ijbcn->ijfkcn", indicator, values_in, precision=HIGH)
    zero_row = jnp.zeros_like(face_values[:1, :, 0])
    from_north = jnp.concatenate([zero_row, face_values[:-1, :, 1]], axis=0)
    from_south = jnp.concatenate([face_values[1:, :, 0], zero_row], axis=0)
    zero_col = jnp.zeros_like(face_values[:, :1, 2])
    from_west = jnp.concatenate([zero_col, face_values[:, :-1, 3]], axis=1)
    from_east = jnp.concatenate([face_values[:, 1:, 2], zero_col], axis=1)
    received = jnp.stack([from_north, from_south, from_west, from_east], axis=2)
    return values_in + jnp.einsum("ijfkb,ijfkcn->ijbcn", indicator, received, precision=HIGH)


def reference(solution, residual, prev_direction, prev_dot, face_lists, multiplicity, block_pattern, schur, neumann_inverse, coarse_basis, primal_map, coarse_inverse):
    weight = (1.0 / multiplicity.astype(jnp.float32))[..., None, None]
    scaled = residual * weight
    local_term = apply_blocks(neumann_inverse, block_pattern, scaled)
    sub_rows, sub_cols, blocks, dofs, cases = residual.shape
    flattened = scaled.reshape(sub_rows, sub_cols, blocks * dofs, cases)
    coarse_local = jnp.einsum("ijpd,ijdn->ijpn", coarse_basis, flattened, precision=HIGH)
    indicator = (primal_map[..., None] == jnp.arange(coarse_inverse.shape[0])).astype(jnp.float32)
    coarse_rhs = jnp.einsum("ijpc,ijpn->cn", indicator, coarse_local, precision=HIGH)
    coarse_sol = jnp.dot(coarse_inverse, coarse_rhs, precision=HIGH)
    own_coarse = jnp.einsum("ijpc,cn->ijpn", indicator, coarse_sol, precision=HIGH)
    coarse_back = jnp.einsum("ijpd,ijpn->ijdn", coarse_basis, own_coarse, precision=HIGH)
    coarse_back = coarse_back.reshape(residual.shape)
    precond = assemble((local_term + coarse_back) * weight, face_lists)
    precond_dot = jnp.sum(residual * precond * weight, axis=(0, 1, 2, 3))
    direction = precond + (precond_dot / prev_dot) * prev_direction
    image = assemble(apply_blocks(schur, block_pattern, direction), face_lists)
    curvature = jnp.sum(direction * image * weight, axis=(0, 1, 2, 3))
    step_size = precond_dot / curvature
    return solution + step_size * direction, residual - step_size * image, direction
```

```python
import jax
import jax.numpy as jnp
from jax import lax
from jax.experimental import pallas as pl
from jax.experimental.pallas import tpu as pltpu
from jax.sharding import PartitionSpec as P

F32 = jnp.float32
BF16 = jnp.bfloat16
SLOTS = 4
SMEM = pl.BlockSpec(memory_space=pltpu.SMEM)
VMEM = pl.BlockSpec(memory_space=pltpu.VMEM)
ANY = pl.BlockSpec(memory_space=pl.ANY)


def halves(x):
    high = x.astype(BF16)
    return high, (x - high.astype(F32)).astype(BF16)


def dot(a, b):
    return jnp.dot(a, b, preferred_element_type=F32)


def dot_first(a, b):
    return lax.dot_general(a, b, (((0,), (0,)), ((), ())), preferred_element_type=F32)


def fold(x):
    width = x.shape[1] // 2
    return x[:, :width] + x[:, width:]


def product(matrix, pair):
    high, low = halves(matrix)
    return fold(dot(high, pair)) + dot(low, pair[:, : pair.shape[1] // 2])


def exact_pair(x):
    return jnp.concatenate(halves(x), axis=1)


def block_row(row_blocks, pattern, b, pairs):
    matrix = jnp.concatenate([row_blocks[b, k] for k in range(3)], axis=1)
    field = jnp.concatenate([pairs[pattern[b, k]] for k in range(3)], axis=0)
    return product(matrix, field)


def partial_rows(x):
    rows, cols = x.shape
    return jnp.sum(x.reshape(rows // 8, 8, cols), axis=0)


def weight_of(multiplicity, b):
    return 1.0 / jnp.full((1, 128), multiplicity[b].astype(F32))


def mapped(primal_map, shape, dim):
    place = lax.broadcasted_iota(jnp.int32, shape, dim)
    found = jnp.zeros(shape, jnp.int32)
    for p in range(8):
        found = jnp.where(place == p, primal_map[p], found)
    return found


def slots_by_block(faces, slot):
    for b in range(17):
        slot[b] = 16
    for f in range(4):
        for k in range(SLOTS):
            slot[faces[f, k]] = f * SLOTS + k


def local_kernel(
    faces, multiplicity, pattern, primal_map, residual_any, neumann_any, basis,
    local, north, south, west, east, coarse,
    residual, neumann, pairs, residual_sems, neumann_sems,
):
    count = residual.shape[0]
    copies = []
    for c in range(4):
        part = pl.ds(c * count // 4, count // 4)
        copies.append(pltpu.make_async_copy(residual_any.at[part], residual.at[part], residual_sems.at[c]))
    for c in range(8):
        part = pl.ds(c * count // 8, count // 8)
        copies.append(pltpu.make_async_copy(neumann_any.at[part], neumann.at[part], neumann_sems.at[c]))
    for copy in copies:
        copy.start()
    for b in range(count):
        if b % (count // 4) == 0:
            copies[b // (count // 4)].wait()
        pairs[b] = exact_pair(residual[b] * weight_of(multiplicity, b))
    field = pairs[...].reshape(count * 128, 256)
    coarse[0:8, :] = product(basis[...], field)
    total = jnp.zeros((8, 128), F32)
    for b in range(count):
        if b % (count // 8) == 0:
            copies[4 + b // (count // 8)].wait()
        weight = weight_of(multiplicity, b)
        out = block_row(neumann, pattern, b, pairs) * weight
        local[b] = out
        total += partial_rows(residual[b] * out)
    row = lax.broadcasted_iota(jnp.int32, (8, 128), 0)
    total = jnp.sum(total, axis=0, keepdims=True)
    map_row = mapped(primal_map, (8, 128), 1).astype(F32)
    coarse[8:16, :] = jnp.where(row == 0, total, jnp.where(row == 1, map_row, 0.0))
    map_rows = mapped(primal_map, (8, 128), 0).astype(F32)
    for f, sent in enumerate((north, south, west, east)):
        for k in range(SLOTS):
            b = jnp.minimum(faces[f, k], count - 1)
            sent[k * 128 : (k + 1) * 128, :] = local[b]
            lanes = pl.ds(pl.multiple_of(b * 128, 128), 128)
            sent[512 + 8 * k : 520 + 8 * k, :] = basis[:, lanes] * weight_of(multiplicity, b)
        sent[544:552, :] = map_rows


def back(basis, own):
    bh, bl = (h.astype(F32) for h in halves(basis))
    oh, ol = (h.astype(F32) for h in halves(own))
    left = jnp.concatenate([bh, bl, bh, bl], axis=0).astype(BF16)
    right = jnp.concatenate([oh, oh, ol, ol], axis=0).astype(BF16)
    return dot_first(left, right)


def direction_kernel(
    faces, multiplicity, pattern, primal_map, me,
    local, north, south, west, east, gathered, inverse_rows, basis, previous, prev_dot, schur,
    direction, image, to_north, to_south, to_west, to_east, curvature, precond_dot,
    added, pairs, inverse, slot,
):
    count = local.shape[0]
    owners = gathered.shape[0] // 16
    order = inverse_rows.shape[1]
    chunks = order // 32
    slots_by_block(faces, slot)
    for j in range(chunks):
        target = pl.multiple_of((me[0] ^ j) * 32, 32)
        inverse[pl.ds(target, 32), :] = inverse_rows[j * 32 : (j + 1) * 32, :]

    maps = gathered[pl.ds(9, owners, stride=16), :].astype(jnp.int32)
    lane = lax.broadcasted_iota(jnp.int32, (owners, order), 1)
    chosen = [(maps[:, p : p + 1] == lane).astype(F32) for p in range(8)]
    chosen = jnp.concatenate(chosen, axis=0).astype(BF16)
    rows = jnp.concatenate([gathered[pl.ds(p, owners, stride=16), :] for p in range(8)], axis=0)
    rhs = fold(dot_first(chosen, exact_pair(rows)))
    coarse = product(inverse[...], exact_pair(rhs))
    dots = jnp.sum(gathered[pl.ds(8, owners, stride=16), :], axis=0, keepdims=True)
    dots = dots + jnp.sum(rhs * coarse, axis=0, keepdims=True)
    precond_dot[...] = dots
    beta = dots / prev_dot[...]

    received = (north, south, west, east)
    maps = [mapped(primal_map, (8, 128), 0)] + [r[544:552, :].astype(jnp.int32) for r in received]
    maps = jnp.concatenate(maps, axis=0)
    lane = lax.broadcasted_iota(jnp.int32, (40, order), 1)
    wanted = (maps[:, 0:1] == lane).astype(F32).astype(BF16)
    wanted = fold(dot(wanted, exact_pair(coarse)))

    for f, r in enumerate(received):
        face_basis = jnp.concatenate([r[512 + 8 * k : 520 + 8 * k, :] for k in range(SLOTS)], axis=1)
        face_back = back(face_basis, wanted[8 + 8 * f : 16 + 8 * f])
        for k in range(SLOTS):
            part = slice(k * 128, (k + 1) * 128)
            added[f * SLOTS + k] = r[part, :] + face_back[part]
    added[16] = jnp.zeros((128, 128), F32)
    own_back = back(basis[...], wanted[0:8])
    for b in range(count):
        mine = local[b] + own_back[b * 128 : (b + 1) * 128] * weight_of(multiplicity, b)
        value = mine + added[slot[b]] + beta * previous[b]
        direction[b] = value
        pairs[b] = exact_pair(value)
    total = jnp.zeros((8, 128), F32)
    for b in range(count):
        out = block_row(schur, pattern, b, pairs)
        image[b] = out
        total += partial_rows(direction[b] * out)
    curvature[...] = total
    for f, sent in enumerate((to_north, to_south, to_west, to_east)):
        for k in range(SLOTS):
            sent[k * 128 : (k + 1) * 128, :] = image[jnp.minimum(faces[f, k], count - 1)]


def update_kernel(
    faces, current, residual, direction, image, north, south, west, east, curvature, precond_dot,
    new_solution, new_residual,
    added, slot,
):
    slots_by_block(faces, slot)
    step = precond_dot[...] / jnp.sum(curvature[...], axis=0, keepdims=True)
    for f, r in enumerate((north, south, west, east)):
        for k in range(SLOTS):
            added[f * SLOTS + k] = r[k * 128 : (k + 1) * 128, :]
    added[16] = jnp.zeros((128, 128), F32)
    for b in range(current.shape[0]):
        new_solution[b] = current[b] + step * direction[b]
        new_residual[b] = residual[b] - step * (image[b] + added[slot[b]])


def swap(x, axis, bit):
    return lax.ppermute(x, axis, [(i, i ^ bit) for i in range(lax.axis_size(axis))])


def bits_of(axis):
    bit = 1
    while bit < lax.axis_size(axis):
        yield bit
        bit *= 2


def everyone(x, axis):
    for bit in bits_of(axis):
        x = jnp.concatenate([x, swap(x, axis, bit)], axis=0)
    return x


def total_of(x, axis):
    for bit in bits_of(axis):
        x = x + swap(x, axis, bit)
    return x


def faces_from_neighbours(north, south, west, east):
    def shifted(x, axis, up):
        pairs = [(i, i + 1) for i in range(lax.axis_size(axis) - 1)]
        return lax.ppermute(x, axis, pairs if up else [(j, i) for i, j in pairs])

    return (
        shifted(south, "row", True),
        shifted(north, "row", False),
        shifted(east, "col", True),
        shifted(west, "col", False),
    )


def shape(*dims):
    return jax.ShapeDtypeStruct(dims, F32)


def kernel_params(mib):
    return pltpu.CompilerParams(vmem_limit_bytes=mib << 20)


def per_device(
    solution,
    residual,
    prev_direction,
    prev_dot,
    face_lists,
    multiplicity,
    block_pattern,
    schur,
    neumann_inverse,
    coarse_basis,
    primal_map,
    coarse_inverse,
):
    current, residual, previous = solution[0, 0], residual[0, 0], prev_direction[0, 0]
    faces, multiplicity, pattern = face_lists[0, 0], multiplicity[0, 0], block_pattern[0, 0]
    schur, neumann = schur[0, 0], neumann_inverse[0, 0]
    basis, primal_map = coarse_basis[0, 0], primal_map[0, 0]
    count, dofs, cases = residual.shape
    field = shape(count, dofs, cases)

    inverse_rows = everyone(coarse_inverse, "col")
    order = inverse_rows.shape[0]
    me = lax.axis_index("col").astype(jnp.int32).reshape(1)

    local, *faces_out, coarse = pl.pallas_call(
        local_kernel,
        out_shape=(field,) + (shape(SLOTS * dofs + 40, cases),) * 4 + (shape(16, cases),),
        in_specs=[SMEM] * 4 + [ANY, ANY, VMEM],
        out_specs=(VMEM,) * 6,
        scratch_shapes=[
            pltpu.VMEM(residual.shape, F32),
            pltpu.VMEM(neumann.shape, F32),
            pltpu.VMEM((count, dofs, 2 * cases), BF16),
            pltpu.SemaphoreType.DMA((4,)),
            pltpu.SemaphoreType.DMA((8,)),
        ],
        compiler_params=kernel_params(24),
        name="local_solve",
    )(faces, multiplicity, pattern, primal_map, residual, neumann, basis)

    gathered = everyone(everyone(coarse, "col"), "row")
    faces_in = faces_from_neighbours(*faces_out)

    direction, image, *faces_out, curvature, precond_dot = pl.pallas_call(
        direction_kernel,
        out_shape=(field, field) + (shape(SLOTS * dofs, cases),) * 4 + (shape(8, cases), shape(1, cases)),
        in_specs=[SMEM] * 5 + [VMEM] * 11,
        out_specs=(VMEM,) * 8,
        scratch_shapes=[
            pltpu.VMEM((17, dofs, cases), F32),
            pltpu.VMEM((count, dofs, 2 * cases), BF16),
            pltpu.VMEM((order, order), F32),
            pltpu.SMEM((17,), jnp.int32),
        ],
        compiler_params=kernel_params(40),
        name="direction_image",
    )(
        faces, multiplicity, pattern, primal_map, me,
        local, *faces_in, gathered, inverse_rows, basis, previous, prev_dot.reshape(1, cases), schur,
    )

    curvature = total_of(total_of(curvature, "col"), "row")
    faces_in = faces_from_neighbours(*faces_out)

    new_solution, new_residual = pl.pallas_call(
        update_kernel,
        out_shape=(field, field),
        in_specs=[SMEM] + [VMEM] * 10,
        out_specs=(VMEM,) * 2,
        scratch_shapes=[pltpu.VMEM((17, dofs, cases), F32), pltpu.SMEM((17,), jnp.int32)],
        compiler_params=kernel_params(24),
        name="update",
    )(faces, current, residual, direction, image, *faces_in, curvature, precond_dot)
    return (new_solution[None, None], new_residual[None, None], direction[None, None])


def solution(mesh):
    split = lambda dims: P("row", "col", *(None,) * dims)
    placed = (
        split(3), split(3), split(3), P(), split(2), split(1), split(2), split(4), split(4), split(2), split(1),
        P("col", None),
    )
    return jax.shard_map(
        per_device,
        mesh=mesh,
        in_specs=placed,
        out_specs=(split(3), split(3), split(3)),
        check_vma=False,
    )
```

```python
import jax
import jax.numpy as jnp
from jax import lax
from jax.experimental import pallas as pl
from jax.experimental.pallas import tpu as pltpu
from jax.sharding import PartitionSpec as P

F32 = jnp.float32
BF16 = jnp.bfloat16
SLOTS = 4
SMEM = pl.BlockSpec(memory_space=pltpu.SMEM)
VMEM = pl.BlockSpec(memory_space=pltpu.VMEM)
HBM = pl.BlockSpec(memory_space=pltpu.HBM)


def halves(x):
    high = x.astype(BF16)
    return high, (x - high.astype(F32)).astype(BF16)


def dot(a, b):
    return jnp.dot(a, b, preferred_element_type=F32)


def dot_first(a, b):
    return lax.dot_general(a, b, (((0,), (0,)), ((), ())), preferred_element_type=F32)


def fold(x):
    width = x.shape[1] // 2
    return x[:, :width] + x[:, width:]


def product(matrix, pair):
    high, low = halves(matrix)
    return fold(dot(high, pair)) + dot(low, pair[:, : pair.shape[1] // 2])


def exact_pair(x):
    return jnp.concatenate(halves(x), axis=1)


def block_row(row_blocks, pattern, b, pairs):
    matrix = jnp.concatenate([row_blocks[b, k] for k in range(3)], axis=1)
    stacked = jnp.concatenate(halves(matrix), axis=0)
    field = jnp.concatenate([pairs[pattern[k, 0, b]] for k in range(3)], axis=0)
    both = fold(dot(stacked, field))
    return both[:128] + both[128:]


def partial_rows(x):
    rows, cols = x.shape
    return jnp.sum(x.reshape(rows // 8, 8, cols), axis=0)


def weight_of(multiplicity, b):
    return 1.0 / jnp.full((1, 128), multiplicity[b].astype(F32))


def mapped(primal_map, shape, dim):
    place = lax.broadcasted_iota(jnp.int32, shape, dim)
    found = jnp.zeros(shape, jnp.int32)
    for p in range(8):
        found = jnp.where(place == p, primal_map[p], found)
    return found


def partner_faces():
    row, col = lax.axis_index("row") % 2, lax.axis_index("col") % 2
    return 1 - row, row, 3 - col, 2 + col


def slots_by_block(faces, slot):
    for b in range(17):
        slot[b] = 16
    for s, f in enumerate(partner_faces()):
        for k in range(SLOTS):
            slot[faces[f, k]] = s * SLOTS + k


def local_kernel(
    faces_hbm, multiplicity_hbm, pattern_hbm, primal_map_hbm, residual_hbm, neumann_hbm, basis_hbm,
    local, send_0, send_1, send_2, send_3, coarse,
    faces, multiplicity, pattern, primal_map, residual, neumann, basis, pairs,
    index_sems, residual_sems, neumann_sems, basis_sem,
):
    count = residual.shape[0]
    index_copies = [
        pltpu.make_async_copy(source, target, index_sems.at[i])
        for i, (source, target) in enumerate(
            ((multiplicity_hbm, multiplicity), (pattern_hbm, pattern), (primal_map_hbm, primal_map), (faces_hbm, faces))
        )
    ]
    basis_copy = pltpu.make_async_copy(basis_hbm, basis, basis_sem)
    copies = []
    for c in range(4):
        part = pl.ds(c * count // 4, count // 4)
        copies.append(pltpu.make_async_copy(residual_hbm.at[part], residual.at[part], residual_sems.at[c]))
    for c in range(8):
        part = pl.ds(c * count // 8, count // 8)
        copies.append(pltpu.make_async_copy(neumann_hbm.at[part], neumann.at[part], neumann_sems.at[c]))
    for copy in (*index_copies, *copies[:4], basis_copy, *copies[4:]):
        copy.start()
    for copy in index_copies:
        copy.wait()
    for b in range(count):
        if b % (count // 4) == 0:
            copies[b // (count // 4)].wait()
        pairs[b] = exact_pair(residual[b] * weight_of(multiplicity, b))
    total = jnp.zeros((8, 128), F32)
    for b in range(count):
        if b % (count // 8) == 0:
            copies[4 + b // (count // 8)].wait()
        weight = weight_of(multiplicity, b)
        out = block_row(neumann, pattern, b, pairs) * weight
        local[b] = out
        total += partial_rows(residual[b] * out)
    basis_copy.wait()
    map_rows = mapped(primal_map, (8, 128), 0).astype(F32)
    for f, sent in zip(partner_faces(), (send_0, send_1, send_2, send_3)):
        for k in range(SLOTS):
            b = jnp.minimum(faces[f, k], count - 1)
            sent[k * 128 : (k + 1) * 128, :] = local[b]
            lanes = pl.ds(pl.multiple_of(b * 128, 128), 128)
            sent[512 + 8 * k : 520 + 8 * k, :] = basis[:, lanes] * weight_of(multiplicity, b)
        sent[544:552, :] = map_rows
    field = pairs[...].reshape(count * 128, 256)
    row = lax.broadcasted_iota(jnp.int32, (8, 128), 0)
    total = jnp.sum(total, axis=0, keepdims=True)
    map_row = mapped(primal_map, (8, 128), 1).astype(F32)
    rows = jnp.concatenate(
        [product(basis[...], field), jnp.where(row == 0, total, jnp.where(row == 1, map_row, 0.0))], axis=0
    )
    for i in range(coarse.shape[0] // 16):
        coarse[16 * i : 16 * i + 16, :] = rows


def back(basis, own):
    bh, bl = (h.astype(F32) for h in halves(basis))
    oh, ol = (h.astype(F32) for h in halves(own))
    left = jnp.concatenate([bh, bl, bh, bl], axis=0).astype(BF16)
    right = jnp.concatenate([oh, oh, ol, ol], axis=0).astype(BF16)
    return dot_first(left, right)


def direction_kernel(
    faces, multiplicity, pattern, primal_map,
    local, got_0, got_1, got_2, got_3, gathered, inverse, basis, previous, prev_dot, schur,
    direction, image, send_0, send_1, send_2, send_3, curvature, precond_dot,
    added, pairs, slot,
):
    count = local.shape[0]
    owners = gathered.shape[0] // 16
    order = inverse.shape[1]
    slots_by_block(faces, slot)

    maps = gathered[pl.ds(9, owners, stride=16), :].astype(jnp.int32)
    lane = lax.broadcasted_iota(jnp.int32, (owners, order), 1)
    chosen = [(maps[:, p : p + 1] == lane).astype(F32) for p in range(8)]
    chosen = jnp.concatenate(chosen, axis=0).astype(BF16)
    rows = jnp.concatenate([gathered[pl.ds(p, owners, stride=16), :] for p in range(8)], axis=0)
    rhs = fold(dot_first(chosen, exact_pair(rows)))
    coarse = product(inverse[...], exact_pair(rhs))
    dots = jnp.sum(gathered[pl.ds(8, owners, stride=16), :], axis=0, keepdims=True)
    dots = dots + jnp.sum(rhs * coarse, axis=0, keepdims=True)
    precond_dot[...] = dots
    beta = dots / prev_dot[...]

    received = (got_0, got_1, got_2, got_3)
    maps = [mapped(primal_map, (8, 128), 0)] + [r[544:552, :].astype(jnp.int32) for r in received]
    maps = jnp.concatenate(maps, axis=0)
    lane = lax.broadcasted_iota(jnp.int32, (40, order), 1)
    wanted = (maps[:, 0:1] == lane).astype(F32).astype(BF16)
    wanted = fold(dot(wanted, exact_pair(coarse)))

    for f, r in enumerate(received):
        face_basis = jnp.concatenate([r[512 + 8 * k : 520 + 8 * k, :] for k in range(SLOTS)], axis=1)
        face_back = back(face_basis, wanted[8 + 8 * f : 16 + 8 * f])
        for k in range(SLOTS):
            part = slice(k * 128, (k + 1) * 128)
            added[f * SLOTS + k] = r[part, :] + face_back[part]
    added[16] = jnp.zeros((128, 128), F32)
    own_back = back(basis[...], wanted[0:8])
    for b in range(count):
        mine = local[b] + own_back[b * 128 : (b + 1) * 128] * weight_of(multiplicity, b)
        value = mine + added[slot[b]] + beta * previous[b]
        direction[b] = value
        pairs[b] = exact_pair(value)
    total = jnp.zeros((8, 128), F32)
    for b in range(count):
        out = block_row(schur, pattern, b, pairs)
        image[b] = out
        total += partial_rows(direction[b] * out)
    for i in range(curvature.shape[0] // 8):
        curvature[8 * i : 8 * i + 8, :] = total
    for f, sent in zip(partner_faces(), (send_0, send_1, send_2, send_3)):
        for k in range(SLOTS):
            sent[k * 128 : (k + 1) * 128, :] = image[jnp.minimum(faces[f, k], count - 1)]


def update_kernel(
    faces, current, residual, direction, image, got_0, got_1, got_2, got_3, curvature, precond_dot,
    new_solution, new_residual,
    added, slot,
):
    slots_by_block(faces, slot)
    step = precond_dot[...] / jnp.sum(curvature[...], axis=0, keepdims=True)
    for f, r in enumerate((got_0, got_1, got_2, got_3)):
        for k in range(SLOTS):
            added[f * SLOTS + k] = r[k * 128 : (k + 1) * 128, :]
    added[16] = jnp.zeros((128, 128), F32)
    for b in range(current.shape[0]):
        new_solution[b] = current[b] + step * direction[b]
        new_residual[b] = residual[b] - step * (image[b] + added[slot[b]])


def swap_pairs(x, axis, first):
    pairs = [(i, i + 1) for i in range(first, lax.axis_size(axis) - 1, 2)]
    return lax.ppermute(x, axis, pairs + [(j, i) for i, j in pairs])


def swapped(sends):
    steps = (("row", 0), ("row", 1), ("col", 0), ("col", 1))
    return [swap_pairs(x, *step) for x, step in zip(sends, steps)]


def from_all(x, axes):
    return lax.all_to_all(x, axes, split_axis=0, concat_axis=0, tiled=True)


def shape(*dims):
    return jax.ShapeDtypeStruct(dims, F32)


def held(*dims):
    return pltpu.VMEM(dims, F32)


def kernel_params(mib):
    return pltpu.CompilerParams(vmem_limit_bytes=mib << 20)


def per_device(
    solution,
    residual,
    prev_direction,
    prev_dot,
    face_lists,
    multiplicity,
    block_pattern,
    schur,
    neumann_inverse,
    coarse_basis,
    primal_map,
    coarse_inverse,
):
    current, residual, previous = solution[0, 0], residual[0, 0], prev_direction[0, 0]
    faces, multiplicity = face_lists[0, 0], multiplicity[0, 0]
    pattern = block_pattern[0, 0].T.reshape(3, 1, -1)
    schur, neumann = schur[0, 0], neumann_inverse[0, 0]
    basis, primal_map = coarse_basis[0, 0], primal_map[0, 0]
    count, dofs, cases = residual.shape

    everywhere = lax.axis_size("row") * lax.axis_size("col")

    inverse = from_all(jnp.tile(coarse_inverse, (lax.axis_size("col"), 1)), "col")
    local, *sends, coarse = pl.pallas_call(
        local_kernel,
        out_shape=(held(count, dofs, cases),)
        + (held(SLOTS * dofs + 40, cases),) * 4
        + (held(16 * everywhere, cases),),
        in_specs=[HBM] * 7,
        out_specs=(VMEM,) * 6,
        scratch_shapes=[pltpu.SMEM(x.shape, jnp.int32) for x in (faces, multiplicity, pattern, primal_map)]
        + [
            pltpu.VMEM(residual.shape, F32),
            pltpu.VMEM(neumann.shape, F32),
            pltpu.VMEM(basis.shape, F32),
            pltpu.VMEM((count, dofs, 2 * cases), BF16),
            pltpu.SemaphoreType.DMA((4,)),
            pltpu.SemaphoreType.DMA((4,)),
            pltpu.SemaphoreType.DMA((8,)),
            pltpu.SemaphoreType.DMA,
        ],
        compiler_params=kernel_params(16),
        name="local_solve",
    )(faces, multiplicity, pattern, primal_map, residual, neumann, basis)

    gathered = from_all(coarse, ("row", "col"))
    received = swapped(sends)

    direction, image, *sends, curvature, precond_dot = pl.pallas_call(
        direction_kernel,
        out_shape=(shape(count, dofs, cases), held(count, dofs, cases))
        + (held(SLOTS * dofs, cases),) * 4
        + (held(8 * everywhere, cases), shape(1, cases)),
        in_specs=[SMEM] * 4 + [VMEM] * 11,
        out_specs=(VMEM,) * 8,
        scratch_shapes=[
            pltpu.VMEM((17, dofs, cases), F32),
            pltpu.VMEM((count, dofs, 2 * cases), BF16),
            pltpu.SMEM((17,), jnp.int32),
        ],
        compiler_params=kernel_params(20),
        name="direction_image",
    )(
        faces, multiplicity, pattern, primal_map,
        local, *received, gathered, inverse, basis, previous, prev_dot.reshape(1, cases), schur,
    )

    curvature = from_all(curvature, ("row", "col"))
    received = swapped(sends)

    new_solution, new_residual = pl.pallas_call(
        update_kernel,
        out_shape=(shape(count, dofs, cases),) * 2,
        in_specs=[SMEM] + [VMEM] * 10,
        out_specs=(VMEM,) * 2,
        scratch_shapes=[pltpu.VMEM((17, dofs, cases), F32), pltpu.SMEM((17,), jnp.int32)],
        compiler_params=kernel_params(16),
        name="update",
    )(faces, current, residual, direction, image, *received, curvature, precond_dot)
    return (new_solution[None, None], new_residual[None, None], direction[None, None])


def solution(mesh):
    split = lambda dims: P("row", "col", *(None,) * dims)
    placed = (
        split(3), split(3), split(3), P(), split(2), split(1), split(2), split(4), split(4), split(2), split(1),
        P("col", None),
    )
    return jax.shard_map(
        per_device,
        mesh=mesh,
        in_specs=placed,
        out_specs=(split(3), split(3), split(3)),
        check_vma=False,
    )
```

```python
import jax
import jax.numpy as jnp
from jax import lax
from jax.experimental import pallas as pl
from jax.experimental.pallas import tpu as pltpu
from jax.sharding import PartitionSpec as P

F32 = jnp.float32
BF16 = jnp.bfloat16
SLOTS = 4
ROWS = 10
SMEM = pl.BlockSpec(memory_space=pltpu.SMEM)
VMEM = pl.BlockSpec(memory_space=pltpu.VMEM)
HBM = pl.BlockSpec(memory_space=pltpu.HBM)


def halves(x):
    high = x.astype(BF16)
    return high, (x - high.astype(F32)).astype(BF16)


def dot(a, b):
    return jnp.dot(a, b, preferred_element_type=F32)


def dot_first(a, b):
    return lax.dot_general(a, b, (((0,), (0,)), ((), ())), preferred_element_type=F32)


def fold(x):
    width = x.shape[1] // 2
    return x[:, :width] + x[:, width:]


def product(matrix, pair):
    high, low = halves(matrix)
    return fold(dot(high, pair)) + dot(low, pair[:, : pair.shape[1] // 2])


def exact_pair(x):
    return jnp.concatenate(halves(x), axis=1)


def block_row(row_blocks, pattern, b, pairs):
    matrix = jnp.concatenate([row_blocks[b, k] for k in range(3)], axis=1)
    stacked = jnp.concatenate(halves(matrix), axis=0)
    field = jnp.concatenate([pairs[pattern[k, 0, b]] for k in range(3)], axis=0)
    both = fold(dot(stacked, field))
    return both[:128] + both[128:]


def partial_rows(x):
    rows, cols = x.shape
    return jnp.sum(x.reshape(rows // 8, 8, cols), axis=0)


def weight_of(multiplicity, b):
    return 1.0 / jnp.full((1, 128), multiplicity[b].astype(F32))


def mapped(primal_map, shape, dim):
    place = lax.broadcasted_iota(jnp.int32, shape, dim)
    found = jnp.zeros(shape, jnp.int32)
    for p in range(8):
        found = jnp.where(place == p, primal_map[p], found)
    return found


def partner_faces():
    row, col = lax.axis_index("row") % 2, lax.axis_index("col") % 2
    return 1 - row, row, 3 - col, 2 + col


def slots_by_block(faces, slot):
    for b in range(17):
        slot[b] = 16
    for s, f in enumerate(partner_faces()):
        for k in range(SLOTS):
            slot[faces[f, k]] = s * SLOTS + k


def local_kernel(
    faces_hbm, multiplicity_hbm, pattern_hbm, primal_map_hbm, residual_hbm, neumann_hbm, basis_hbm,
    local, send_0, send_1, send_2, send_3, coarse,
    faces, multiplicity, pattern, primal_map, residual, neumann, basis, pairs,
    index_sems, residual_sems, neumann_sems, basis_sem,
):
    count = residual.shape[0]
    index_copies = [
        pltpu.make_async_copy(source, target, index_sems.at[i])
        for i, (source, target) in enumerate(
            ((multiplicity_hbm, multiplicity), (pattern_hbm, pattern), (primal_map_hbm, primal_map), (faces_hbm, faces))
        )
    ]
    basis_copy = pltpu.make_async_copy(basis_hbm, basis, basis_sem)
    copies = []
    for c in range(4):
        part = pl.ds(c * count // 4, count // 4)
        copies.append(pltpu.make_async_copy(residual_hbm.at[part], residual.at[part], residual_sems.at[c]))
    for c in range(8):
        part = pl.ds(c * count // 8, count // 8)
        copies.append(pltpu.make_async_copy(neumann_hbm.at[part], neumann.at[part], neumann_sems.at[c]))
    for copy in (*index_copies, *copies[:4], basis_copy, *copies[4:]):
        copy.start()
    for copy in index_copies:
        copy.wait()
    for b in range(count):
        if b % (count // 4) == 0:
            copies[b // (count // 4)].wait()
        pairs[b] = exact_pair(residual[b] * weight_of(multiplicity, b))
    total = jnp.zeros((8, 128), F32)
    for b in range(count):
        if b % (count // 8) == 0:
            copies[4 + b // (count // 8)].wait()
        weight = weight_of(multiplicity, b)
        out = block_row(neumann, pattern, b, pairs) * weight
        local[b] = out
        total += partial_rows(residual[b] * out)
    basis_copy.wait()
    map_rows = mapped(primal_map, (8, 128), 0).astype(F32)
    for f, sent in zip(partner_faces(), (send_0, send_1, send_2, send_3)):
        for k in range(SLOTS):
            b = jnp.minimum(faces[f, k], count - 1)
            sent[k * 128 : (k + 1) * 128, :] = local[b]
            lanes = pl.ds(pl.multiple_of(b * 128, 128), 128)
            sent[512 + 8 * k : 520 + 8 * k, :] = basis[:, lanes] * weight_of(multiplicity, b)
        sent[544:552, :] = map_rows
    field = pairs[...].reshape(count * 128, 256)
    row = lax.broadcasted_iota(jnp.int32, (8, 128), 0)
    total = jnp.sum(total, axis=0, keepdims=True)
    map_row = mapped(primal_map, (8, 128), 1).astype(F32)
    rows = jnp.concatenate(
        [product(basis[...], field), jnp.where(row == 0, total, jnp.where(row == 1, map_row, 0.0))], axis=0
    )
    for i in range(coarse.shape[0] // ROWS):
        coarse[ROWS * i : ROWS * i + ROWS, :] = rows[:ROWS]


def back(basis, own):
    bh, bl = (h.astype(F32) for h in halves(basis))
    oh, ol = (h.astype(F32) for h in halves(own))
    left = jnp.concatenate([bh, bl, bh, bl], axis=0).astype(BF16)
    right = jnp.concatenate([oh, oh, ol, ol], axis=0).astype(BF16)
    return dot_first(left, right)


def coarse_kernel(
    multiplicity, primal_map, local, gathered, basis, prev_dot, previous_hbm, schur_hbm, *rest
):
    *pieces, started, stacked, wanted, precond_dot, inverse, previous, schur, previous_sem, schur_sems = rest
    count = local.shape[0]
    previous_copy = pltpu.make_async_copy(previous_hbm, previous, previous_sem)
    previous_copy.start()
    schur_copies = []
    for c in range(4):
        part = pl.ds(c * count // 4, count // 4)
        schur_copies.append(pltpu.make_async_copy(schur_hbm.at[part], schur.at[part], schur_sems.at[c]))
        schur_copies[c].start()

    owners = gathered.shape[0] // ROWS
    order = inverse.shape[1]
    owned = pieces[0].shape[0]
    me = lax.axis_index("col")
    j = 0
    for piece in pieces:
        for i in range(piece.shape[0] // owned):
            target = pl.multiple_of((me ^ j) * owned, owned)
            inverse[pl.ds(target, owned), :] = piece[i * owned : (i + 1) * owned, :]
            j += 1

    maps = gathered[pl.ds(9, owners, stride=ROWS), :].astype(jnp.int32)
    lane = lax.broadcasted_iota(jnp.int32, (owners, order), 1)
    chosen = [(maps[:, p : p + 1] == lane).astype(F32) for p in range(8)]
    chosen = jnp.concatenate(chosen, axis=0).astype(BF16)
    rows = jnp.concatenate([gathered[pl.ds(p, owners, stride=ROWS), :] for p in range(8)], axis=0)
    rhs = fold(dot_first(chosen, exact_pair(rows)))
    coarse = product(inverse[...], exact_pair(rhs))
    dots = jnp.sum(gathered[pl.ds(8, owners, stride=ROWS), :], axis=0, keepdims=True)
    dots = dots + jnp.sum(rhs * coarse, axis=0, keepdims=True)
    precond_dot[...] = dots
    beta = dots / prev_dot[...]
    wanted[...] = coarse

    lane = lax.broadcasted_iota(jnp.int32, (8, order), 1)
    own = (mapped(primal_map, (8, 128), 0)[:, 0:1] == lane).astype(F32).astype(BF16)
    own_back = back(basis[...], fold(dot(own, exact_pair(coarse))))
    previous_copy.wait()
    for b in range(count):
        mine = local[b] + own_back[b * 128 : (b + 1) * 128] * weight_of(multiplicity, b)
        started[b] = mine + beta * previous[b]
    for b in range(count):
        if b % (count // 4) == 0:
            schur_copies[b // (count // 4)].wait()
        matrix = jnp.concatenate([schur[b, k] for k in range(3)], axis=1)
        stacked[b] = jnp.concatenate(halves(matrix), axis=0)


def direction_kernel(
    faces, pattern, started, coarse, got_0, got_1, got_2, got_3, stacked,
    direction_hbm, direction, image, send_0, send_1, send_2, send_3, curvature,
    added, pairs, slot, direction_sem,
):
    count = started.shape[0]
    order = coarse.shape[0]
    slots_by_block(faces, slot)
    received = (got_0, got_1, got_2, got_3)
    maps = jnp.concatenate([r[544:552, :] for r in received], axis=0).astype(jnp.int32)
    lane = lax.broadcasted_iota(jnp.int32, (32, order), 1)
    wanted = (maps[:, 0:1] == lane).astype(F32).astype(BF16)
    wanted = fold(dot(wanted, exact_pair(coarse[...])))
    for s, r in enumerate(received):
        face_basis = jnp.concatenate([r[512 + 8 * k : 520 + 8 * k, :] for k in range(SLOTS)], axis=1)
        face_back = back(face_basis, wanted[8 * s : 8 * s + 8])
        for k in range(SLOTS):
            part = slice(k * 128, (k + 1) * 128)
            added[s * SLOTS + k] = r[part, :] + face_back[part]
    added[16] = jnp.zeros((128, 128), F32)
    for b in range(count):
        value = started[b] + added[slot[b]]
        direction[b] = value
        pairs[b] = exact_pair(value)
    direction_copy = pltpu.make_async_copy(direction, direction_hbm, direction_sem)
    direction_copy.start()
    total = jnp.zeros((8, 128), F32)
    for b in range(count):
        field = jnp.concatenate([pairs[pattern[k, 0, b]] for k in range(3)], axis=0)
        out = fold(dot(stacked[b], field))
        out = out[:128] + out[128:]
        image[b] = out
        total += partial_rows(direction[b] * out)
    for f, sent in zip(partner_faces(), (send_0, send_1, send_2, send_3)):
        for k in range(SLOTS):
            sent[k * 128 : (k + 1) * 128, :] = image[jnp.minimum(faces[f, k], count - 1)]
    curvature[...] = jnp.broadcast_to(jnp.sum(total, axis=0, keepdims=True), curvature.shape)
    direction_copy.wait()


def update_kernel(
    faces, current, residual, direction, image, got_0, got_1, got_2, got_3, curvature, precond_dot,
    new_solution_hbm, new_residual_hbm,
    new_solution, new_residual, added, slot, solution_sems, residual_sems,
):
    count = current.shape[0]
    slots_by_block(faces, slot)
    step = precond_dot[...] / jnp.sum(curvature[...], axis=0, keepdims=True)
    copies = []

    def leave(c, value, value_hbm, sems):
        part = pl.ds(c * count // 4, count // 4)
        copies.append(pltpu.make_async_copy(value.at[part], value_hbm.at[part], sems.at[c]))
        copies[-1].start()

    for b in range(count):
        new_solution[b] = current[b] + step * direction[b]
        if (b + 1) % (count // 4) == 0:
            leave(b // (count // 4), new_solution, new_solution_hbm, solution_sems)
    for s, r in enumerate((got_0, got_1, got_2, got_3)):
        for k in range(SLOTS):
            added[s * SLOTS + k] = r[k * 128 : (k + 1) * 128, :]
    added[16] = jnp.zeros((128, 128), F32)
    for b in range(count):
        new_residual[b] = residual[b] - step * (image[b] + added[slot[b]])
        if (b + 1) % (count // 4) == 0:
            leave(b // (count // 4), new_residual, new_residual_hbm, residual_sems)
    for copy in copies:
        copy.wait()


def swap_pairs(x, axis, first):
    pairs = [(i, i + 1) for i in range(first, lax.axis_size(axis) - 1, 2)]
    return lax.ppermute(x, axis, pairs + [(j, i) for i, j in pairs])


def swapped(sends):
    steps = (("row", 0), ("row", 1), ("col", 0), ("col", 1))
    got = {i: swap_pairs(sends[i], *steps[i]) for i in (3, 2, 1, 0)}
    return [got[i] for i in range(4)]


def pieces_of(x, axis):
    pieces = [x]
    bit = 1
    while bit < lax.axis_size(axis):
        whole = jnp.concatenate(pieces, axis=0) if bit > 1 else x
        pieces.append(lax.ppermute(whole, axis, [(i, i ^ bit) for i in range(lax.axis_size(axis))]))
        bit *= 2
    return pieces


def from_all(x):
    everywhere = lax.axis_size("row") * lax.axis_size("col")
    sent = x.reshape(everywhere, 1, -1)
    return lax.all_to_all(sent, ("row", "col"), split_axis=0, concat_axis=0, tiled=True).reshape(x.shape)


def shape(*dims):
    return jax.ShapeDtypeStruct(dims, F32)


def held(*dims):
    return pltpu.VMEM(dims, F32)


def in_hbm(x):
    return pltpu.with_memory_space_constraint(x, pltpu.HBM)


def kernel_params(mib):
    return pltpu.CompilerParams(vmem_limit_bytes=mib << 20)


def per_device(
    solution,
    residual,
    prev_direction,
    prev_dot,
    face_lists,
    multiplicity,
    block_pattern,
    schur,
    neumann_inverse,
    coarse_basis,
    primal_map,
    coarse_inverse,
):
    current, residual, previous = solution[0, 0], residual[0, 0], prev_direction[0, 0]
    faces, multiplicity = face_lists[0, 0], multiplicity[0, 0]
    pattern = block_pattern[0, 0].T.reshape(3, 1, -1)
    schur, neumann = schur[0, 0], neumann_inverse[0, 0]
    basis, primal_map = coarse_basis[0, 0], primal_map[0, 0]
    count, dofs, cases = residual.shape

    everywhere = lax.axis_size("row") * lax.axis_size("col")

    pieces = pieces_of(coarse_inverse, "col")
    order = coarse_inverse.shape[1]
    indices = (faces, multiplicity, pattern, primal_map)
    local, *sends, coarse = pl.pallas_call(
        local_kernel,
        out_shape=(held(count, dofs, cases),)
        + (held(SLOTS * dofs + 40, cases),) * 4
        + (held(ROWS * everywhere, cases),),
        in_specs=[HBM] * 7,
        out_specs=(VMEM,) * 6,
        scratch_shapes=[pltpu.SMEM(x.shape, jnp.int32) for x in indices]
        + [
            pltpu.VMEM(residual.shape, F32),
            pltpu.VMEM(neumann.shape, F32),
            pltpu.VMEM(basis.shape, F32),
            pltpu.VMEM((count, dofs, 2 * cases), BF16),
            pltpu.SemaphoreType.DMA((4,)),
            pltpu.SemaphoreType.DMA((4,)),
            pltpu.SemaphoreType.DMA((8,)),
            pltpu.SemaphoreType.DMA,
        ],
        compiler_params=kernel_params(16),
        name="local_solve",
    )(*(in_hbm(x) for x in (*indices, residual, neumann, basis)))

    received = swapped(sends)
    gathered = from_all(coarse)

    started, stacked, coarse, precond_dot = pl.pallas_call(
        coarse_kernel,
        out_shape=(
            held(count, dofs, cases),
            pltpu.VMEM((count, 2 * dofs, 3 * dofs), BF16),
            held(order, cases),
            held(1, cases),
        ),
        in_specs=[SMEM] * 2 + [VMEM] * 4 + [HBM] * 2 + [VMEM] * len(pieces),
        out_specs=(VMEM,) * 4,
        scratch_shapes=[
            pltpu.VMEM((order, order), F32),
            pltpu.VMEM(previous.shape, F32),
            pltpu.VMEM(schur.shape, F32),
            pltpu.SemaphoreType.DMA,
            pltpu.SemaphoreType.DMA((4,)),
        ],
        compiler_params=kernel_params(32),
        name="coarse_solve",
    )(
        multiplicity, primal_map, local, gathered, basis, prev_dot.reshape(1, cases),
        in_hbm(previous), in_hbm(schur), *pieces,
    )

    direction, direction_held, image, *sends, curvature = pl.pallas_call(
        direction_kernel,
        out_shape=(shape(count, dofs, cases), held(count, dofs, cases), held(count, dofs, cases))
        + (held(SLOTS * dofs, cases),) * 4
        + (held(everywhere, cases),),
        in_specs=[SMEM] * 2 + [VMEM] * 7,
        out_specs=(HBM,) + (VMEM,) * 7,
        scratch_shapes=[
            pltpu.VMEM((17, dofs, cases), F32),
            pltpu.VMEM((count, dofs, 2 * cases), BF16),
            pltpu.SMEM((17,), jnp.int32),
            pltpu.SemaphoreType.DMA,
        ],
        compiler_params=kernel_params(16),
        name="direction_image",
    )(faces, pattern, started, coarse, *received, stacked)

    received = swapped(sends)
    curvature = from_all(curvature)

    new_solution, new_residual = pl.pallas_call(
        update_kernel,
        out_shape=(shape(count, dofs, cases),) * 2,
        in_specs=[SMEM] + [VMEM] * 10,
        out_specs=(HBM,) * 2,
        scratch_shapes=[
            pltpu.VMEM(residual.shape, F32),
            pltpu.VMEM(residual.shape, F32),
            pltpu.VMEM((17, dofs, cases), F32),
            pltpu.SMEM((17,), jnp.int32),
            pltpu.SemaphoreType.DMA((4,)),
            pltpu.SemaphoreType.DMA((4,)),
        ],
        compiler_params=kernel_params(16),
        name="update",
    )(faces, current, residual, direction_held, image, *received, curvature, precond_dot)
    return (new_solution[None, None], new_residual[None, None], direction[None, None])


def solution(mesh):
    split = lambda dims: P("row", "col", *(None,) * dims)
    placed = (
        split(3), split(3), split(3), P(), split(2), split(1), split(2), split(4), split(4), split(2), split(1),
        P("col", None),
    )
    return jax.shard_map(
        per_device,
        mesh=mesh,
        in_specs=placed,
        out_specs=(split(3), split(3), split(3)),
        check_vma=False,
    )
```

```python
import jax
import jax.numpy as jnp
from jax import lax
from jax.experimental import pallas as pl
from jax.experimental.pallas import tpu as pltpu
from jax.sharding import PartitionSpec as P

F32 = jnp.float32
BF16 = jnp.bfloat16
SLOTS = 4
ROWS = 10
SMEM = pl.BlockSpec(memory_space=pltpu.SMEM)
VMEM = pl.BlockSpec(memory_space=pltpu.VMEM)
HBM = pl.BlockSpec(memory_space=pltpu.HBM)


def halves(x):
    high = x.astype(BF16)
    return high, (x - high.astype(F32)).astype(BF16)


def dot(a, b):
    return jnp.dot(a, b, preferred_element_type=F32)


def dot_first(a, b):
    return lax.dot_general(a, b, (((0,), (0,)), ((), ())), preferred_element_type=F32)


def fold(x):
    width = x.shape[1] // 2
    return x[:, :width] + x[:, width:]


def product(matrix, pair):
    high, low = halves(matrix)
    return fold(dot(high, pair)) + dot(low, pair[:, : pair.shape[1] // 2])


def exact_pair(x):
    return jnp.concatenate(halves(x), axis=1)


def halved_rows(row_blocks):
    matrix = jnp.concatenate([row_blocks[k] for k in range(3)], axis=1)
    return jnp.concatenate(halves(matrix), axis=0)


def row_product(stacked, pattern, b, pairs):
    field = jnp.concatenate([pairs[pattern[k, 0, b]] for k in range(3)], axis=0)
    both = fold(dot(stacked, field))
    return both[:128] + both[128:]


def partial_rows(x):
    rows, cols = x.shape
    return jnp.sum(x.reshape(rows // 8, 8, cols), axis=0)


def weight_of(multiplicity, b):
    return 1.0 / jnp.full((1, 128), multiplicity[b].astype(F32))


def mapped(primal_map, shape, dim):
    place = lax.broadcasted_iota(jnp.int32, shape, dim)
    found = jnp.zeros(shape, jnp.int32)
    for p in range(8):
        found = jnp.where(place == p, primal_map[p], found)
    return found


def partner_faces():
    row, col = lax.axis_index("row") % 2, lax.axis_index("col") % 2
    return 1 - row, row, 3 - col, 2 + col


def slots_by_block(faces, slot):
    for b in range(17):
        slot[b] = 16
    for s, f in enumerate(partner_faces()):
        for k in range(SLOTS):
            slot[faces[f, k]] = s * SLOTS + k


def face_block(faces, f, k, count):
    return jnp.minimum(faces[f, k], count - 1)


def send_basis(sent, faces, f, basis, multiplicity, primal_map, count):
    for k in range(SLOTS):
        b = face_block(faces, f, k, count)
        lanes = pl.ds(pl.multiple_of(b * 128, 128), 128)
        sent[512 + 8 * k : 520 + 8 * k, :] = basis[:, lanes] * weight_of(multiplicity, b)
    sent[544:552, :] = mapped(primal_map, (8, 128), 0).astype(F32)


def first_face_kernel(
    faces_hbm, multiplicity_hbm, pattern_hbm, primal_map_hbm, residual_hbm, neumann_hbm, basis_hbm, inverse_hbm,
    send, residual, pairs, basis, inverse,
    faces, multiplicity, pattern, primal_map, neumann, index_sems, residual_sems, neumann_sems, basis_sems,
):
    count = residual.shape[0]
    index_copies = [
        pltpu.make_async_copy(source, target, index_sems.at[i])
        for i, (source, target) in enumerate(
            ((faces_hbm, faces), (multiplicity_hbm, multiplicity), (pattern_hbm, pattern), (primal_map_hbm, primal_map))
        )
    ]
    copies = []
    for c in range(4):
        part = pl.ds(c * count // 4, count // 4)
        copies.append(pltpu.make_async_copy(residual_hbm.at[part], residual.at[part], residual_sems.at[c]))
    basis_copy = pltpu.make_async_copy(basis_hbm, basis, basis_sems.at[0])
    inverse_copy = pltpu.make_async_copy(inverse_hbm, inverse, basis_sems.at[1])
    for copy in (*index_copies, *copies):
        copy.start()
    for copy in index_copies:
        copy.wait()
    f = partner_faces()[2]
    neumann_copies = []
    for k in range(SLOTS):
        b = face_block(faces, f, k, count)
        neumann_copies.append(pltpu.make_async_copy(neumann_hbm.at[b], neumann.at[k], neumann_sems.at[k]))
        neumann_copies[k].start()
    basis_copy.start()
    inverse_copy.start()
    for b in range(count):
        if b % (count // 4) == 0:
            copies[b // (count // 4)].wait()
        pairs[b] = exact_pair(residual[b] * weight_of(multiplicity, b))
    for k in range(SLOTS):
        neumann_copies[k].wait()
        b = face_block(faces, f, k, count)
        out = row_product(halved_rows(neumann.at[k]), pattern, b, pairs)
        send[k * 128 : (k + 1) * 128, :] = out * weight_of(multiplicity, b)
    basis_copy.wait()
    send_basis(send, faces, f, basis, multiplicity, primal_map, count)
    inverse_copy.wait()


def local_kernel(
    faces, multiplicity, pattern, primal_map, residual, pairs, basis, neumann_hbm,
    local, send_0, send_1, send_3, coarse,
    neumann, neumann_sems,
):
    count = residual.shape[0]
    copies = []
    for c in range(8):
        part = pl.ds(c * count // 8, count // 8)
        copies.append(pltpu.make_async_copy(neumann_hbm.at[part], neumann.at[part], neumann_sems.at[c]))
        copies[c].start()
    field = pairs[...].reshape(count * 128, 256)
    coarse_local = product(basis[...], field)
    total = jnp.zeros((8, 128), F32)
    for b in range(count):
        if b % (count // 8) == 0:
            copies[b // (count // 8)].wait()
        out = row_product(halved_rows(neumann.at[b]), pattern, b, pairs) * weight_of(multiplicity, b)
        local[b] = out
        total += partial_rows(residual[b] * out)
    row = lax.broadcasted_iota(jnp.int32, (8, 128), 0)
    total = jnp.sum(total, axis=0, keepdims=True)
    map_row = mapped(primal_map, (8, 128), 1).astype(F32)
    rows = jnp.concatenate(
        [coarse_local, jnp.where(row == 0, total, jnp.where(row == 1, map_row, 0.0))], axis=0
    )
    for i in range(coarse.shape[0] // ROWS):
        coarse[ROWS * i : ROWS * i + ROWS, :] = rows[:ROWS]
    partners = partner_faces()
    for f, sent in zip((partners[0], partners[1], partners[3]), (send_0, send_1, send_3)):
        for k in range(SLOTS):
            sent[k * 128 : (k + 1) * 128, :] = local[face_block(faces, f, k, count)]
        send_basis(sent, faces, f, basis, multiplicity, primal_map, count)


def back(basis, own):
    bh, bl = (h.astype(F32) for h in halves(basis))
    oh, ol = (h.astype(F32) for h in halves(own))
    left = jnp.concatenate([bh, bl, bh, bl], axis=0).astype(BF16)
    right = jnp.concatenate([oh, oh, ol, ol], axis=0).astype(BF16)
    return dot_first(left, right)


def coarse_kernel(
    multiplicity, primal_map, local, gathered, basis, prev_dot, previous_hbm, schur_hbm, *rest
):
    *pieces, started, stacked, wanted, precond_dot, inverse, previous, schur, previous_sem, schur_sems = rest
    count = local.shape[0]
    previous_copy = pltpu.make_async_copy(previous_hbm, previous, previous_sem)
    previous_copy.start()
    schur_copies = []
    for c in range(4):
        part = pl.ds(c * count // 4, count // 4)
        schur_copies.append(pltpu.make_async_copy(schur_hbm.at[part], schur.at[part], schur_sems.at[c]))
        schur_copies[c].start()

    owners = gathered.shape[0] // ROWS
    order = inverse.shape[1]
    owned = pieces[0].shape[0]
    me = lax.axis_index("col")
    j = 0
    for piece in pieces:
        for i in range(piece.shape[0] // owned):
            apart = sum(bit for k, bit in enumerate(exchange_bits(order // owned)) if j >> k & 1)
            target = pl.multiple_of((me ^ apart) * owned, owned)
            inverse[pl.ds(target, owned), :] = piece[i * owned : (i + 1) * owned, :]
            j += 1

    maps = gathered[pl.ds(9, owners, stride=ROWS), :].astype(jnp.int32)
    lane = lax.broadcasted_iota(jnp.int32, (owners, order), 1)
    chosen = [(maps[:, p : p + 1] == lane).astype(F32) for p in range(8)]
    chosen = jnp.concatenate(chosen, axis=0).astype(BF16)
    rows = jnp.concatenate([gathered[pl.ds(p, owners, stride=ROWS), :] for p in range(8)], axis=0)
    rhs = fold(dot_first(chosen, exact_pair(rows)))
    coarse = product(inverse[...], exact_pair(rhs))
    dots = jnp.sum(gathered[pl.ds(8, owners, stride=ROWS), :], axis=0, keepdims=True)
    dots = dots + jnp.sum(rhs * coarse, axis=0, keepdims=True)
    precond_dot[...] = dots
    beta = dots / prev_dot[...]
    wanted[...] = coarse

    lane = lax.broadcasted_iota(jnp.int32, (8, order), 1)
    own = (mapped(primal_map, (8, 128), 0)[:, 0:1] == lane).astype(F32).astype(BF16)
    own_back = back(basis[...], fold(dot(own, exact_pair(coarse))))
    previous_copy.wait()
    for b in range(count):
        mine = local[b] + own_back[b * 128 : (b + 1) * 128] * weight_of(multiplicity, b)
        started[b] = mine + beta * previous[b]
    for b in range(count):
        if b % (count // 4) == 0:
            schur_copies[b // (count // 4)].wait()
        stacked[b] = halved_rows(schur.at[b])


def direction_kernel(
    faces, pattern, started, coarse, got_0, got_1, got_2, got_3, stacked,
    direction, pairs, send,
    added, slot,
):
    count = started.shape[0]
    order = coarse.shape[0]
    slots_by_block(faces, slot)
    received = (got_0, got_1, got_2, got_3)
    maps = jnp.concatenate([r[544:552, :] for r in received], axis=0).astype(jnp.int32)
    lane = lax.broadcasted_iota(jnp.int32, (32, order), 1)
    wanted = (maps[:, 0:1] == lane).astype(F32).astype(BF16)
    wanted = fold(dot(wanted, exact_pair(coarse[...])))
    for s, r in enumerate(received):
        face_basis = jnp.concatenate([r[512 + 8 * k : 520 + 8 * k, :] for k in range(SLOTS)], axis=1)
        face_back = back(face_basis, wanted[8 * s : 8 * s + 8])
        for k in range(SLOTS):
            part = slice(k * 128, (k + 1) * 128)
            added[s * SLOTS + k] = r[part, :] + face_back[part]
    added[16] = jnp.zeros((128, 128), F32)
    for b in range(count):
        value = started[b] + added[slot[b]]
        direction[b] = value
        pairs[b] = exact_pair(value)
    f = partner_faces()[2]
    for k in range(SLOTS):
        b = face_block(faces, f, k, count)
        send[k * 128 : (k + 1) * 128, :] = row_product(stacked[b], pattern, b, pairs)


def image_kernel(
    faces, pattern, direction, pairs, stacked,
    direction_hbm, image, send_0, send_1, send_3, curvature,
    direction_sem,
):
    count = direction.shape[0]
    direction_copy = pltpu.make_async_copy(direction, direction_hbm, direction_sem)
    direction_copy.start()
    total = jnp.zeros((8, 128), F32)
    for b in range(count):
        out = row_product(stacked[b], pattern, b, pairs)
        image[b] = out
        total += partial_rows(direction[b] * out)
    curvature[...] = jnp.broadcast_to(jnp.sum(total, axis=0, keepdims=True), curvature.shape)
    partners = partner_faces()
    for f, sent in zip((partners[0], partners[1], partners[3]), (send_0, send_1, send_3)):
        for k in range(SLOTS):
            sent[k * 128 : (k + 1) * 128, :] = image[face_block(faces, f, k, count)]
    direction_copy.wait()


def update_kernel(
    faces, current, residual, direction, image, got_0, got_1, got_2, got_3, curvature, precond_dot,
    new_solution_hbm, new_residual_hbm,
    new_solution, new_residual, added, slot, solution_sems, residual_sems,
):
    count = current.shape[0]
    slots_by_block(faces, slot)
    step = precond_dot[...] / jnp.sum(curvature[...], axis=0, keepdims=True)
    copies = []

    def leave(c, value, value_hbm, sems):
        part = pl.ds(c * count // 4, count // 4)
        copies.append(pltpu.make_async_copy(value.at[part], value_hbm.at[part], sems.at[c]))
        copies[-1].start()

    for b in range(count):
        new_solution[b] = current[b] + step * direction[b]
        if (b + 1) % (count // 4) == 0:
            leave(b // (count // 4), new_solution, new_solution_hbm, solution_sems)
    for s, r in enumerate((got_0, got_1, got_2, got_3)):
        for k in range(SLOTS):
            added[s * SLOTS + k] = r[k * 128 : (k + 1) * 128, :]
    added[16] = jnp.zeros((128, 128), F32)
    for b in range(count):
        new_residual[b] = residual[b] - step * (image[b] + added[slot[b]])
        if (b + 1) % (count // 4) == 0:
            leave(b // (count // 4), new_residual, new_residual_hbm, residual_sems)
    for copy in copies:
        copy.wait()


def swap_pairs(x, axis, first):
    pairs = [(i, i + 1) for i in range(first, lax.axis_size(axis) - 1, 2)]
    return lax.ppermute(x, axis, pairs + [(j, i) for i, j in pairs])


def exchange_bits(count):
    bits = [1 << k for k in range(count.bit_length() - 1)]
    return bits[-1:] + bits[:-1]


def pieces_of(x, axis):
    pieces = [x]
    for bit in exchange_bits(lax.axis_size(axis)):
        whole = jnp.concatenate(pieces, axis=0) if len(pieces) > 1 else x
        pieces.append(lax.ppermute(whole, axis, [(i, i ^ bit) for i in range(lax.axis_size(axis))]))
    return pieces


def from_all(x):
    everywhere = lax.axis_size("row") * lax.axis_size("col")
    sent = x.reshape(everywhere, 1, -1)
    return lax.all_to_all(sent, ("row", "col"), split_axis=0, concat_axis=0, tiled=True).reshape(x.shape)


def shape(*dims):
    return jax.ShapeDtypeStruct(dims, F32)


def held(*dims):
    return pltpu.VMEM(dims, F32)


def in_hbm(x):
    return pltpu.with_memory_space_constraint(x, pltpu.HBM)


def kernel_params(mib):
    return pltpu.CompilerParams(vmem_limit_bytes=mib << 20)


def per_device(
    solution,
    residual,
    prev_direction,
    prev_dot,
    face_lists,
    multiplicity,
    block_pattern,
    schur,
    neumann_inverse,
    coarse_basis,
    primal_map,
    coarse_inverse,
):
    current, residual, previous = solution[0, 0], residual[0, 0], prev_direction[0, 0]
    faces, multiplicity = face_lists[0, 0], multiplicity[0, 0]
    pattern = jnp.transpose(block_pattern, (0, 3, 1, 2))[0]
    schur, neumann = schur[0, 0], neumann_inverse[0, 0]
    basis, primal_map = coarse_basis[0, 0], primal_map[0, 0]
    count, dofs, cases = residual.shape

    everywhere = lax.axis_size("row") * lax.axis_size("col")

    order = coarse_inverse.shape[1]
    indices = (faces, multiplicity, pattern, primal_map)
    face = held(SLOTS * dofs + 40, cases)
    pairs_held = pltpu.VMEM((count, dofs, 2 * cases), BF16)

    send_2, residual_held, pairs, basis, own_inverse = pl.pallas_call(
        first_face_kernel,
        out_shape=(face, held(*residual.shape), pairs_held, held(*basis.shape), held(*coarse_inverse.shape)),
        in_specs=[HBM] * 8,
        out_specs=(VMEM,) * 5,
        scratch_shapes=[pltpu.SMEM(x.shape, jnp.int32) for x in indices]
        + [
            pltpu.VMEM((SLOTS,) + neumann.shape[1:], F32),
            pltpu.SemaphoreType.DMA((4,)),
            pltpu.SemaphoreType.DMA((4,)),
            pltpu.SemaphoreType.DMA((SLOTS,)),
            pltpu.SemaphoreType.DMA((2,)),
        ],
        compiler_params=kernel_params(12),
        name="first_face",
    )(*(in_hbm(x) for x in (*indices, residual, neumann, basis, coarse_inverse)))
    got_2 = swap_pairs(send_2, "col", 0)
    pieces = pieces_of(own_inverse, "col")

    local, send_0, send_1, send_3, coarse = pl.pallas_call(
        local_kernel,
        out_shape=(held(count, dofs, cases), face, face, face, held(ROWS * everywhere, cases)),
        in_specs=[SMEM] * 4 + [VMEM] * 3 + [HBM],
        out_specs=(VMEM,) * 5,
        scratch_shapes=[pltpu.VMEM(neumann.shape, F32), pltpu.SemaphoreType.DMA((8,))],
        compiler_params=kernel_params(16),
        name="local_solve",
    )(*indices, residual_held, pairs, basis, in_hbm(neumann))

    gathered = from_all(coarse)
    got_3 = swap_pairs(send_3, "col", 1)
    got_0 = swap_pairs(send_0, "row", 0)
    got_1 = swap_pairs(send_1, "row", 1)

    started, stacked, coarse, precond_dot = pl.pallas_call(
        coarse_kernel,
        out_shape=(
            held(count, dofs, cases),
            pltpu.VMEM((count, 2 * dofs, 3 * dofs), BF16),
            held(order, cases),
            held(1, cases),
        ),
        in_specs=[SMEM] * 2 + [VMEM] * 4 + [HBM] * 2 + [VMEM] * len(pieces),
        out_specs=(VMEM,) * 4,
        scratch_shapes=[
            pltpu.VMEM((order, order), F32),
            pltpu.VMEM(previous.shape, F32),
            pltpu.VMEM(schur.shape, F32),
            pltpu.SemaphoreType.DMA,
            pltpu.SemaphoreType.DMA((4,)),
        ],
        compiler_params=kernel_params(32),
        name="coarse_solve",
    )(
        multiplicity, primal_map, local, gathered, basis, prev_dot.reshape(1, cases),
        in_hbm(previous), in_hbm(schur), *pieces,
    )

    face = held(SLOTS * dofs, cases)
    direction_held, pairs, send_2 = pl.pallas_call(
        direction_kernel,
        out_shape=(held(count, dofs, cases), pairs_held, face),
        in_specs=[SMEM] * 2 + [VMEM] * 7,
        out_specs=(VMEM,) * 3,
        scratch_shapes=[pltpu.VMEM((17, dofs, cases), F32), pltpu.SMEM((17,), jnp.int32)],
        compiler_params=kernel_params(12),
        name="direction",
    )(faces, pattern, started, coarse, got_0, got_1, got_2, got_3, stacked)
    got_2 = swap_pairs(send_2, "col", 0)

    direction, image, send_0, send_1, send_3, curvature = pl.pallas_call(
        image_kernel,
        out_shape=(shape(count, dofs, cases), held(count, dofs, cases), face, face, face, held(everywhere, cases)),
        in_specs=[SMEM] * 2 + [VMEM] * 3,
        out_specs=(HBM,) + (VMEM,) * 5,
        scratch_shapes=[pltpu.SemaphoreType.DMA],
        compiler_params=kernel_params(12),
        name="image",
    )(faces, pattern, direction_held, pairs, stacked)
    curvature = from_all(curvature)
    got_3 = swap_pairs(send_3, "col", 1)
    got_0 = swap_pairs(send_0, "row", 0)
    got_1 = swap_pairs(send_1, "row", 1)

    new_solution, new_residual = pl.pallas_call(
        update_kernel,
        out_shape=(shape(count, dofs, cases),) * 2,
        in_specs=[SMEM] + [VMEM] * 10,
        out_specs=(HBM,) * 2,
        scratch_shapes=[
            pltpu.VMEM(residual.shape, F32),
            pltpu.VMEM(residual.shape, F32),
            pltpu.VMEM((17, dofs, cases), F32),
            pltpu.SMEM((17,), jnp.int32),
            pltpu.SemaphoreType.DMA((4,)),
            pltpu.SemaphoreType.DMA((4,)),
        ],
        compiler_params=kernel_params(16),
        name="update",
    )(
        faces, current, residual_held, direction_held, image, got_0, got_1, got_2, got_3, curvature, precond_dot
    )
    return (new_solution[None, None], new_residual[None, None], direction[None, None])


def solution(mesh):
    split = lambda dims: P("row", "col", *(None,) * dims)
    placed = (
        split(3), split(3), split(3), P(), split(2), split(1), split(2), split(4), split(4), split(2), split(1),
        P("col", None),
    )
    return jax.shard_map(
        per_device,
        mesh=mesh,
        in_specs=placed,
        out_specs=(split(3), split(3), split(3)),
        check_vma=False,
    )
```

```python
import jax
import jax.numpy as jnp
from jax import lax
from jax.experimental import pallas as pl
from jax.experimental.pallas import tpu as pltpu
from jax.sharding import PartitionSpec as P

F32 = jnp.float32
BF16 = jnp.bfloat16
SLOTS = 4
ROWS = 10
SMEM = pl.BlockSpec(memory_space=pltpu.SMEM)
VMEM = pl.BlockSpec(memory_space=pltpu.VMEM)
HBM = pl.BlockSpec(memory_space=pltpu.HBM)


def halves(x):
    high = x.astype(BF16)
    return high, (x - high.astype(F32)).astype(BF16)


def dot(a, b):
    return jnp.dot(a, b, preferred_element_type=F32)


def dot_first(a, b):
    return lax.dot_general(a, b, (((0,), (0,)), ((), ())), preferred_element_type=F32)


def fold(x):
    width = x.shape[1] // 2
    return x[:, :width] + x[:, width:]


def product(matrix, pair):
    high, low = halves(matrix)
    return fold(dot(high, pair)) + dot(low, pair[:, : pair.shape[1] // 2])


def exact_pair(x):
    return jnp.concatenate(halves(x), axis=1)


def halved_rows(row_blocks):
    matrix = jnp.concatenate([row_blocks[k] for k in range(3)], axis=1)
    return jnp.concatenate(halves(matrix), axis=0)


def row_product(stacked, pattern, b, pairs):
    field = jnp.concatenate([pairs[pattern[k, 0, b]] for k in range(3)], axis=0)
    both = fold(dot(stacked, field))
    return both[:128] + both[128:]


def partial_rows(x):
    rows, cols = x.shape
    return jnp.sum(x.reshape(rows // 8, 8, cols), axis=0)


def weight_of(multiplicity, b):
    return 1.0 / jnp.full((1, 128), multiplicity[b].astype(F32))


def mapped(primal_map, shape, dim):
    place = lax.broadcasted_iota(jnp.int32, shape, dim)
    found = jnp.zeros(shape, jnp.int32)
    for p in range(8):
        found = jnp.where(place == p, primal_map[p], found)
    return found


def partner_faces():
    row, col = lax.axis_index("row") % 2, lax.axis_index("col") % 2
    return 1 - row, row, 3 - col, 2 + col


def slots_by_block(faces, slot):
    for b in range(17):
        slot[b] = 16
    for s, f in enumerate(partner_faces()):
        for k in range(SLOTS):
            slot[faces[f, k]] = s * SLOTS + k


def local_kernel(
    faces_hbm, multiplicity_hbm, pattern_hbm, primal_map_hbm, residual_hbm, neumann_hbm, basis_hbm, inverse_hbm,
    local, send_0, send_1, send_2, send_3, coarse,
    faces, multiplicity, pattern, primal_map, residual, neumann, basis, inverse, pairs,
    index_sems, residual_sems, neumann_sems, basis_sems,
):
    count = residual.shape[0]
    index_copies = [
        pltpu.make_async_copy(source, target, index_sems.at[i])
        for i, (source, target) in enumerate(
            ((multiplicity_hbm, multiplicity), (pattern_hbm, pattern), (primal_map_hbm, primal_map), (faces_hbm, faces))
        )
    ]
    basis_copy = pltpu.make_async_copy(basis_hbm, basis, basis_sems.at[0])
    inverse_copy = pltpu.make_async_copy(inverse_hbm, inverse, basis_sems.at[1])
    copies = []
    for c in range(4):
        part = pl.ds(c * count // 4, count // 4)
        copies.append(pltpu.make_async_copy(residual_hbm.at[part], residual.at[part], residual_sems.at[c]))
    for c in range(8):
        part = pl.ds(c * count // 8, count // 8)
        copies.append(pltpu.make_async_copy(neumann_hbm.at[part], neumann.at[part], neumann_sems.at[c]))
    for copy in (*index_copies, *copies[:4], *copies[4:], basis_copy, inverse_copy):
        copy.start()
    for copy in index_copies:
        copy.wait()
    for b in range(count):
        if b % (count // 4) == 0:
            copies[b // (count // 4)].wait()
        pairs[b] = exact_pair(residual[b] * weight_of(multiplicity, b))
    total = jnp.zeros((8, 128), F32)
    for b in range(count):
        if b % (count // 8) == 0:
            copies[4 + b // (count // 8)].wait()
        weight = weight_of(multiplicity, b)
        out = row_product(halved_rows(neumann.at[b]), pattern, b, pairs) * weight
        local[b] = out
        total += partial_rows(residual[b] * out)
    basis_copy.wait()
    map_rows = mapped(primal_map, (8, 128), 0).astype(F32)
    for f, sent in zip(partner_faces(), (send_0, send_1, send_2, send_3)):
        for k in range(SLOTS):
            b = jnp.minimum(faces[f, k], count - 1)
            sent[k * 128 : (k + 1) * 128, :] = local[b]
            lanes = pl.ds(pl.multiple_of(b * 128, 128), 128)
            sent[512 + 8 * k : 520 + 8 * k, :] = basis[:, lanes] * weight_of(multiplicity, b)
        sent[544:552, :] = map_rows
    field = pairs[...].reshape(count * 128, 256)
    row = lax.broadcasted_iota(jnp.int32, (8, 128), 0)
    total = jnp.sum(total, axis=0, keepdims=True)
    map_row = mapped(primal_map, (8, 128), 1).astype(F32)
    rows = jnp.concatenate(
        [product(basis[...], field), jnp.where(row == 0, total, jnp.where(row == 1, map_row, 0.0))], axis=0
    )
    inverse_copy.wait()
    shared = inverse.shape[0] // lax.axis_size("row")
    share = inverse[0:shared, :]
    for r in range(1, lax.axis_size("row")):
        share = jnp.where(lax.axis_index("row") == r, inverse[r * shared : (r + 1) * shared, :], share)
    lanes = range(0, inverse.shape[1], 128)
    rows = jnp.concatenate([rows[:ROWS]] + [share[:, i : i + 128] for i in lanes], axis=0)
    told = rows.shape[0]
    for i in range(coarse.shape[0] // told):
        coarse[told * i : told * i + told, :] = rows


def back(basis, own):
    bh, bl = (h.astype(F32) for h in halves(basis))
    oh, ol = (h.astype(F32) for h in halves(own))
    left = jnp.concatenate([bh, bl, bh, bl], axis=0).astype(BF16)
    right = jnp.concatenate([oh, oh, ol, ol], axis=0).astype(BF16)
    return dot_first(left, right)


def coarse_kernel(
    multiplicity, primal_map, local, gathered, basis, prev_dot, previous_hbm, schur_hbm,
    started, stacked, wanted, precond_dot, inverse, previous, schur, previous_sem, schur_sems,
):
    count = local.shape[0]
    previous_copy = pltpu.make_async_copy(previous_hbm, previous, previous_sem)
    previous_copy.start()
    schur_copies = []
    for c in range(4):
        part = pl.ds(c * count // 4, count // 4)
        schur_copies.append(pltpu.make_async_copy(schur_hbm.at[part], schur.at[part], schur_sems.at[c]))
        schur_copies[c].start()

    order = inverse.shape[1]
    rows_of_mesh = lax.axis_size("row")
    owners = rows_of_mesh * lax.axis_size("col")
    shared = order // owners
    told = ROWS + shared * (order // 128)
    for i in range(owners):
        r, c = i // (owners // rows_of_mesh), i % (owners // rows_of_mesh)
        target = (c * rows_of_mesh + r) * shared
        for j in range(order // 128):
            source = told * i + ROWS + shared * j
            inverse[target : target + shared, 128 * j : 128 * j + 128] = gathered[source : source + shared, :]

    maps = gathered[pl.ds(9, owners, stride=told), :].astype(jnp.int32)
    lane = lax.broadcasted_iota(jnp.int32, (owners, order), 1)
    chosen = [(maps[:, p : p + 1] == lane).astype(F32) for p in range(8)]
    chosen = jnp.concatenate(chosen, axis=0).astype(BF16)
    rows = jnp.concatenate([gathered[pl.ds(p, owners, stride=told), :] for p in range(8)], axis=0)
    rhs = fold(dot_first(chosen, exact_pair(rows)))
    coarse = product(inverse[...], exact_pair(rhs))
    dots = jnp.sum(gathered[pl.ds(8, owners, stride=told), :], axis=0, keepdims=True)
    dots = dots + jnp.sum(rhs * coarse, axis=0, keepdims=True)
    precond_dot[...] = dots
    beta = dots / prev_dot[...]
    wanted[...] = coarse

    lane = lax.broadcasted_iota(jnp.int32, (8, order), 1)
    own = (mapped(primal_map, (8, 128), 0)[:, 0:1] == lane).astype(F32).astype(BF16)
    own_back = back(basis[...], fold(dot(own, exact_pair(coarse))))
    previous_copy.wait()
    for b in range(count):
        mine = local[b] + own_back[b * 128 : (b + 1) * 128] * weight_of(multiplicity, b)
        started[b] = mine + beta * previous[b]
    for b in range(count):
        if b % (count // 4) == 0:
            schur_copies[b // (count // 4)].wait()
        stacked[b] = halved_rows(schur.at[b])


def direction_kernel(
    faces, pattern, started, coarse, got_0, got_1, got_2, got_3, stacked,
    direction_hbm, direction, image, send_0, send_1, send_2, send_3, curvature,
    added, pairs, slot, direction_sem,
):
    count = started.shape[0]
    order = coarse.shape[0]
    slots_by_block(faces, slot)
    received = (got_0, got_1, got_2, got_3)
    maps = jnp.concatenate([r[544:552, :] for r in received], axis=0).astype(jnp.int32)
    lane = lax.broadcasted_iota(jnp.int32, (32, order), 1)
    wanted = (maps[:, 0:1] == lane).astype(F32).astype(BF16)
    wanted = fold(dot(wanted, exact_pair(coarse[...])))
    for s, r in enumerate(received):
        face_basis = jnp.concatenate([r[512 + 8 * k : 520 + 8 * k, :] for k in range(SLOTS)], axis=1)
        face_back = back(face_basis, wanted[8 * s : 8 * s + 8])
        for k in range(SLOTS):
            part = slice(k * 128, (k + 1) * 128)
            added[s * SLOTS + k] = r[part, :] + face_back[part]
    added[16] = jnp.zeros((128, 128), F32)
    for b in range(count):
        value = started[b] + added[slot[b]]
        direction[b] = value
        pairs[b] = exact_pair(value)
    direction_copy = pltpu.make_async_copy(direction, direction_hbm, direction_sem)
    direction_copy.start()
    total = jnp.zeros((8, 128), F32)
    for b in range(count):
        out = row_product(stacked[b], pattern, b, pairs)
        image[b] = out
        total += partial_rows(direction[b] * out)
    for f, sent in zip(partner_faces(), (send_0, send_1, send_2, send_3)):
        for k in range(SLOTS):
            sent[k * 128 : (k + 1) * 128, :] = image[jnp.minimum(faces[f, k], count - 1)]
    curvature[...] = jnp.broadcast_to(jnp.sum(total, axis=0, keepdims=True), curvature.shape)
    direction_copy.wait()


def update_kernel(
    faces, current, residual, direction, image, got_0, got_1, got_2, got_3, curvature, precond_dot,
    new_solution_hbm, new_residual_hbm,
    new_solution, new_residual, added, slot, solution_sems, residual_sems,
):
    count = current.shape[0]
    slots_by_block(faces, slot)
    step = precond_dot[...] / jnp.sum(curvature[...], axis=0, keepdims=True)
    copies = []

    def leave(c, value, value_hbm, sems):
        part = pl.ds(c * count // 4, count // 4)
        copies.append(pltpu.make_async_copy(value.at[part], value_hbm.at[part], sems.at[c]))
        copies[-1].start()

    for b in range(count):
        new_solution[b] = current[b] + step * direction[b]
        if (b + 1) % (count // 4) == 0:
            leave(b // (count // 4), new_solution, new_solution_hbm, solution_sems)
    for s, r in enumerate((got_0, got_1, got_2, got_3)):
        for k in range(SLOTS):
            added[s * SLOTS + k] = r[k * 128 : (k + 1) * 128, :]
    added[16] = jnp.zeros((128, 128), F32)
    for b in range(count):
        new_residual[b] = residual[b] - step * (image[b] + added[slot[b]])
        if (b + 1) % (count // 4) == 0:
            leave(b // (count // 4), new_residual, new_residual_hbm, residual_sems)
    for copy in copies:
        copy.wait()


def swap_pairs(x, axis, first):
    pairs = [(i, i + 1) for i in range(first, lax.axis_size(axis) - 1, 2)]
    return lax.ppermute(x, axis, pairs + [(j, i) for i, j in pairs])


def swapped(sends):
    steps = (("row", 0), ("row", 1), ("col", 0), ("col", 1))
    got = {i: swap_pairs(sends[i], *steps[i]) for i in (3, 2, 1, 0)}
    return [got[i] for i in range(4)]


def from_all(x):
    everywhere = lax.axis_size("row") * lax.axis_size("col")
    sent = x.reshape(everywhere, 1, -1)
    return lax.all_to_all(sent, ("row", "col"), split_axis=0, concat_axis=0, tiled=True).reshape(x.shape)


def shape(*dims):
    return jax.ShapeDtypeStruct(dims, F32)


def held(*dims):
    return pltpu.VMEM(dims, F32)


def in_hbm(x):
    return pltpu.with_memory_space_constraint(x, pltpu.HBM)


def kernel_params(mib):
    return pltpu.CompilerParams(vmem_limit_bytes=mib << 20)


def per_device(
    solution,
    residual,
    prev_direction,
    prev_dot,
    face_lists,
    multiplicity,
    block_pattern,
    schur,
    neumann_inverse,
    coarse_basis,
    primal_map,
    coarse_inverse,
):
    current, residual, previous = solution[0, 0], residual[0, 0], prev_direction[0, 0]
    faces, multiplicity = face_lists[0, 0], multiplicity[0, 0]
    pattern = jnp.transpose(block_pattern, (0, 3, 1, 2))[0]
    schur, neumann = schur[0, 0], neumann_inverse[0, 0]
    basis, primal_map = coarse_basis[0, 0], primal_map[0, 0]
    count, dofs, cases = residual.shape

    everywhere = lax.axis_size("row") * lax.axis_size("col")

    order = coarse_inverse.shape[1]
    told = ROWS + coarse_inverse.shape[0] // lax.axis_size("row") * (order // 128)
    indices = (faces, multiplicity, pattern, primal_map)
    local, *sends, coarse = pl.pallas_call(
        local_kernel,
        out_shape=(held(count, dofs, cases),)
        + (held(SLOTS * dofs + 40, cases),) * 4
        + (held(told * everywhere, cases),),
        in_specs=[HBM] * 8,
        out_specs=(VMEM,) * 6,
        scratch_shapes=[pltpu.SMEM(x.shape, jnp.int32) for x in indices]
        + [
            pltpu.VMEM(residual.shape, F32),
            pltpu.VMEM(neumann.shape, F32),
            pltpu.VMEM(basis.shape, F32),
            pltpu.VMEM(coarse_inverse.shape, F32),
            pltpu.VMEM((count, dofs, 2 * cases), BF16),
            pltpu.SemaphoreType.DMA((4,)),
            pltpu.SemaphoreType.DMA((4,)),
            pltpu.SemaphoreType.DMA((8,)),
            pltpu.SemaphoreType.DMA((2,)),
        ],
        compiler_params=kernel_params(16),
        name="local_solve",
    )(*(in_hbm(x) for x in (*indices, residual, neumann, basis, coarse_inverse)))

    received = swapped(sends)
    gathered = from_all(coarse)

    started, stacked, coarse, precond_dot = pl.pallas_call(
        coarse_kernel,
        out_shape=(
            held(count, dofs, cases),
            pltpu.VMEM((count, 2 * dofs, 3 * dofs), BF16),
            held(order, cases),
            held(1, cases),
        ),
        in_specs=[SMEM] * 2 + [VMEM] * 4 + [HBM] * 2,
        out_specs=(VMEM,) * 4,
        scratch_shapes=[
            pltpu.VMEM((order, order), F32),
            pltpu.VMEM(previous.shape, F32),
            pltpu.VMEM(schur.shape, F32),
            pltpu.SemaphoreType.DMA,
            pltpu.SemaphoreType.DMA((4,)),
        ],
        compiler_params=kernel_params(32),
        name="coarse_solve",
    )(
        multiplicity, primal_map, local, gathered, basis, prev_dot.reshape(1, cases),
        in_hbm(previous), in_hbm(schur),
    )

    direction, direction_held, image, *sends, curvature = pl.pallas_call(
        direction_kernel,
        out_shape=(shape(count, dofs, cases), held(count, dofs, cases), held(count, dofs, cases))
        + (held(SLOTS * dofs, cases),) * 4
        + (held(everywhere, cases),),
        in_specs=[SMEM] * 2 + [VMEM] * 7,
        out_specs=(HBM,) + (VMEM,) * 7,
        scratch_shapes=[
            pltpu.VMEM((17, dofs, cases), F32),
            pltpu.VMEM((count, dofs, 2 * cases), BF16),
            pltpu.SMEM((17,), jnp.int32),
            pltpu.SemaphoreType.DMA,
        ],
        compiler_params=kernel_params(16),
        name="direction_image",
    )(faces, pattern, started, coarse, *received, stacked)

    received = swapped(sends)
    curvature = from_all(curvature)

    new_solution, new_residual = pl.pallas_call(
        update_kernel,
        out_shape=(shape(count, dofs, cases),) * 2,
        in_specs=[SMEM] + [VMEM] * 10,
        out_specs=(HBM,) * 2,
        scratch_shapes=[
            pltpu.VMEM(residual.shape, F32),
            pltpu.VMEM(residual.shape, F32),
            pltpu.VMEM((17, dofs, cases), F32),
            pltpu.SMEM((17,), jnp.int32),
            pltpu.SemaphoreType.DMA((4,)),
            pltpu.SemaphoreType.DMA((4,)),
        ],
        compiler_params=kernel_params(16),
        name="update",
    )(faces, current, residual, direction_held, image, *received, curvature, precond_dot)
    return (new_solution[None, None], new_residual[None, None], direction[None, None])


def solution(mesh):
    split = lambda dims: P("row", "col", *(None,) * dims)
    placed = (
        split(3), split(3), split(3), P(), split(2), split(1), split(2), split(4), split(4), split(2), split(1),
        P("col", None),
    )
    return jax.shard_map(
        per_device,
        mesh=mesh,
        in_specs=placed,
        out_specs=(split(3), split(3), split(3)),
        check_vma=False,
    )
```

```python
import jax
import jax.numpy as jnp
from jax import lax
from jax.experimental import pallas as pl
from jax.experimental.pallas import tpu as pltpu
from jax.sharding import PartitionSpec as P

F32 = jnp.float32
BF16 = jnp.bfloat16
SLOTS = 4
HEAD = 16
SMEM = pl.BlockSpec(memory_space=pltpu.SMEM)
VMEM = pl.BlockSpec(memory_space=pltpu.VMEM)
HBM = pl.BlockSpec(memory_space=pltpu.HBM)
ANY = pl.BlockSpec(memory_space=pl.ANY)


def halves(x):
    high = x.astype(BF16)
    return high, (x - high.astype(F32)).astype(BF16)


def dot(a, b):
    return jnp.dot(a, b, preferred_element_type=F32)


def dot_first(a, b):
    return lax.dot_general(a, b, (((0,), (0,)), ((), ())), preferred_element_type=F32)


def fold(x):
    width = x.shape[1] // 2
    return x[:, :width] + x[:, width:]


def product(matrix, pair):
    high, low = halves(matrix)
    return fold(dot(high, pair)) + dot(low, pair[:, : pair.shape[1] // 2])


def exact_pair(x):
    return jnp.concatenate(halves(x), axis=1)


def halved_rows(row_blocks):
    matrix = jnp.concatenate([row_blocks[k] for k in range(3)], axis=1)
    return jnp.concatenate(halves(matrix), axis=0)


def row_product(stacked, pattern, b, pairs):
    field = jnp.concatenate([pairs[pattern[k, 0, b]] for k in range(3)], axis=0)
    both = fold(dot(stacked, field))
    return both[:128] + both[128:]


def partial_rows(x):
    rows, cols = x.shape
    return jnp.sum(x.reshape(rows // 8, 8, cols), axis=0)


def weight_of(multiplicity, b):
    return 1.0 / jnp.full((1, 128), multiplicity[b].astype(F32))


def mapped(primal_map, shape, dim):
    place = lax.broadcasted_iota(jnp.int32, shape, dim)
    found = jnp.zeros(shape, jnp.int32)
    for p in range(8):
        found = jnp.where(place == p, primal_map[p], found)
    return found


def partner_faces():
    row, col = lax.axis_index("row") % 2, lax.axis_index("col") % 2
    return 1 - row, row, 3 - col, 2 + col


def slots_by_block(faces, slot):
    for b in range(17):
        slot[b] = 16
    for s, f in enumerate(partner_faces()):
        for k in range(SLOTS):
            slot[faces[f, k]] = s * SLOTS + k


def local_kernel(
    faces_hbm, multiplicity_hbm, pattern_hbm, primal_map_hbm, residual_hbm, neumann_hbm, basis_hbm, inverse_hbm,
    local, send_2, told, send_3, send_0, send_1,
    faces, multiplicity, pattern, primal_map, residual, neumann, basis, inverse, pairs,
    index_sems, residual_sems, neumann_sems, basis_sems,
):
    count = residual.shape[0]
    index_copies = [
        pltpu.make_async_copy(source, target, index_sems.at[i])
        for i, (source, target) in enumerate(
            ((multiplicity_hbm, multiplicity), (pattern_hbm, pattern), (primal_map_hbm, primal_map), (faces_hbm, faces))
        )
    ]
    basis_copy = pltpu.make_async_copy(basis_hbm, basis, basis_sems.at[0])
    inverse_copy = pltpu.make_async_copy(inverse_hbm, inverse, basis_sems.at[1])
    copies = []
    for c in range(4):
        part = pl.ds(c * count // 4, count // 4)
        copies.append(pltpu.make_async_copy(residual_hbm.at[part], residual.at[part], residual_sems.at[c]))
    for c in range(8):
        part = pl.ds(c * count // 8, count // 8)
        copies.append(pltpu.make_async_copy(neumann_hbm.at[part], neumann.at[part], neumann_sems.at[c]))
    for copy in (*index_copies, *copies[:4], *copies[4:], basis_copy, inverse_copy):
        copy.start()
    for copy in index_copies:
        copy.wait()
    for b in range(count):
        if b % (count // 4) == 0:
            copies[b // (count // 4)].wait()
        pairs[b] = exact_pair(residual[b] * weight_of(multiplicity, b))
    total = jnp.zeros((8, 128), F32)
    for b in range(count):
        if b % (count // 8) == 0:
            copies[4 + b // (count // 8)].wait()
        weight = weight_of(multiplicity, b)
        out = row_product(halved_rows(neumann.at[b]), pattern, b, pairs) * weight
        local[b] = out
        total += partial_rows(residual[b] * out)
    basis_copy.wait()
    map_rows = mapped(primal_map, (8, 128), 0).astype(F32)
    for f, sent in zip(partner_faces(), (send_0, send_1, send_2, send_3)):
        for k in range(SLOTS):
            b = jnp.minimum(faces[f, k], count - 1)
            sent[k * 128 : (k + 1) * 128, :] = local[b]
            lanes = pl.ds(pl.multiple_of(b * 128, 128), 128)
            sent[512 + 8 * k : 520 + 8 * k, :] = basis[:, lanes] * weight_of(multiplicity, b)
        sent[544:552, :] = map_rows
    field = pairs[...].reshape(count * 128, 256)
    row = lax.broadcasted_iota(jnp.int32, (8, 128), 0)
    total = jnp.sum(total, axis=0, keepdims=True)
    map_row = mapped(primal_map, (8, 128), 1).astype(F32)
    told[0:8, :] = product(basis[...], field)
    told[8:HEAD, :] = jnp.where(row == 0, total, jnp.where(row == 1, map_row, 0.0))
    inverse_copy.wait()
    sharers = inverse.shape[0] // 8
    mine = lax.axis_index("row") % sharers
    share = inverse[pl.ds(pl.multiple_of(mine * 8, 8), 8), :]
    for i in range(inverse.shape[1] // 128):
        told[HEAD + 8 * i : HEAD + 8 * i + 8, :] = share[:, i * 128 : (i + 1) * 128]


def back(basis, own):
    bh, bl = (h.astype(F32) for h in halves(basis))
    oh, ol = (h.astype(F32) for h in halves(own))
    left = jnp.concatenate([bh, bl, bh, bl], axis=0).astype(BF16)
    right = jnp.concatenate([oh, oh, ol, ol], axis=0).astype(BF16)
    return dot_first(left, right)


def coarse_kernel(
    multiplicity, primal_map, local, nearer, farther, basis, prev_dot, previous_hbm, schur_hbm,
    started, stacked, wanted, precond_dot, inverse, previous, schur, previous_sem, schur_sems,
):
    count = local.shape[0]
    previous_copy = pltpu.make_async_copy(previous_hbm, previous, previous_sem)
    previous_copy.start()
    schur_copies = []
    for c in range(4):
        part = pl.ds(c * count // 4, count // 4)
        schur_copies.append(pltpu.make_async_copy(schur_hbm.at[part], schur.at[part], schur_sems.at[c]))
        schur_copies[c].start()

    order = inverse.shape[1]
    rounds = gather_rounds()
    each = HEAD + 8 * (order // 128)
    half = nearer.shape[0] // each
    sharers = order // lax.axis_size("col") // 8
    for j in range(2 * half):
        place = {name: lax.axis_index(name) for name in ("row", "col")}
        for k, (axis, bit) in enumerate(rounds):
            if j >> k & 1:
                place[axis] = place[axis] ^ bit
        target = pl.multiple_of((place["col"] * sharers + place["row"] % sharers) * 8, 8)
        told, start = (nearer, j * each) if j < half else (farther, (j - half) * each)
        for i in range(order // 128):
            source = start + HEAD + 8 * i
            inverse[pl.ds(target, 8), 128 * i : 128 * i + 128] = told[source : source + 8, :]

    def row_of_all(p):
        return jnp.concatenate([x[pl.ds(p, half, stride=each), :] for x in (nearer, farther)], axis=0)

    maps = row_of_all(9).astype(jnp.int32)
    lane = lax.broadcasted_iota(jnp.int32, (2 * half, order), 1)
    chosen = [(maps[:, p : p + 1] == lane).astype(F32) for p in range(8)]
    chosen = jnp.concatenate(chosen, axis=0).astype(BF16)
    rows = jnp.concatenate([row_of_all(p) for p in range(8)], axis=0)
    rhs = fold(dot_first(chosen, exact_pair(rows)))
    coarse = product(inverse[...], exact_pair(rhs))
    dots = jnp.sum(row_of_all(8), axis=0, keepdims=True)
    dots = dots + jnp.sum(rhs * coarse, axis=0, keepdims=True)
    precond_dot[...] = dots
    beta = dots / prev_dot[...]
    wanted[...] = coarse

    lane = lax.broadcasted_iota(jnp.int32, (8, order), 1)
    own = (mapped(primal_map, (8, 128), 0)[:, 0:1] == lane).astype(F32).astype(BF16)
    own_back = back(basis[...], fold(dot(own, exact_pair(coarse))))
    previous_copy.wait()
    for b in range(count):
        mine = local[b] + own_back[b * 128 : (b + 1) * 128] * weight_of(multiplicity, b)
        started[b] = mine + beta * previous[b]
    for b in range(count):
        if b % (count // 4) == 0:
            schur_copies[b // (count // 4)].wait()
        stacked[b] = halved_rows(schur.at[b])


def direction_kernel(
    faces, pattern, started, coarse, got_2, got_3, got_0, got_1, stacked,
    direction_hbm, direction, image, send_2, send_3, send_0, send_1, curvature,
    added, pairs, slot, direction_sem,
):
    count = started.shape[0]
    order = coarse.shape[0]
    slots_by_block(faces, slot)
    received = (got_0, got_1, got_2, got_3)
    maps = jnp.concatenate([r[544:552, :] for r in received], axis=0).astype(jnp.int32)
    lane = lax.broadcasted_iota(jnp.int32, (32, order), 1)
    wanted = (maps[:, 0:1] == lane).astype(F32).astype(BF16)
    wanted = fold(dot(wanted, exact_pair(coarse[...])))
    for s, r in enumerate(received):
        face_basis = jnp.concatenate([r[512 + 8 * k : 520 + 8 * k, :] for k in range(SLOTS)], axis=1)
        face_back = back(face_basis, wanted[8 * s : 8 * s + 8])
        for k in range(SLOTS):
            part = slice(k * 128, (k + 1) * 128)
            added[s * SLOTS + k] = r[part, :] + face_back[part]
    added[16] = jnp.zeros((128, 128), F32)
    for b in range(count):
        value = started[b] + added[slot[b]]
        direction[b] = value
        pairs[b] = exact_pair(value)
    direction_copy = pltpu.make_async_copy(direction, direction_hbm, direction_sem)
    direction_copy.start()
    total = jnp.zeros((8, 128), F32)
    for b in range(count):
        out = row_product(stacked[b], pattern, b, pairs)
        image[b] = out
        total += partial_rows(direction[b] * out)
    for f, sent in zip(partner_faces(), (send_0, send_1, send_2, send_3)):
        for k in range(SLOTS):
            sent[k * 128 : (k + 1) * 128, :] = image[jnp.minimum(faces[f, k], count - 1)]
    curvature[...] = jnp.broadcast_to(jnp.sum(total, axis=0, keepdims=True), curvature.shape)
    direction_copy.wait()


def update_kernel(
    faces, current, residual, direction, image, got_2, got_3, got_0, got_1, curvature, precond_dot,
    new_solution_hbm, new_residual_hbm,
    new_solution, new_residual, added, slot, solution_sems, residual_sems,
):
    count = current.shape[0]
    slots_by_block(faces, slot)
    step = precond_dot[...] / jnp.sum(curvature[...], axis=0, keepdims=True)
    copies = []

    def leave(c, value, value_hbm, sems):
        part = pl.ds(c * count // 4, count // 4)
        copies.append(pltpu.make_async_copy(value.at[part], value_hbm.at[part], sems.at[c]))
        copies[-1].start()

    for b in range(count):
        new_solution[b] = current[b] + step * direction[b]
        if (b + 1) % (count // 4) == 0:
            leave(b // (count // 4), new_solution, new_solution_hbm, solution_sems)
    for s, r in enumerate((got_0, got_1, got_2, got_3)):
        for k in range(SLOTS):
            added[s * SLOTS + k] = r[k * 128 : (k + 1) * 128, :]
    added[16] = jnp.zeros((128, 128), F32)
    for b in range(count):
        new_residual[b] = residual[b] - step * (image[b] + added[slot[b]])
        if (b + 1) % (count // 4) == 0:
            leave(b // (count // 4), new_residual, new_residual_hbm, residual_sems)
    for copy in copies:
        copy.wait()


def swap_pairs(x, axis, first):
    pairs = [(i, i + 1) for i in range(first, lax.axis_size(axis) - 1, 2)]
    return lax.ppermute(x, axis, pairs + [(j, i) for i, j in pairs])


def gather_rounds():
    rounds = []
    for axis in ("col", "row"):
        bits = [1 << k for k in reversed(range(lax.axis_size(axis).bit_length() - 1))]
        rounds += [(axis, bit) for bit in (bits[-1:] + bits[:-1] if axis == "col" else bits)]
    return rounds


def exchange(x, axis, bit):
    return lax.ppermute(x, axis, [(i, i ^ bit) for i in range(lax.axis_size(axis))])


def join_kernel(mine, theirs, first_face, *rest):
    both = rest[len(rest) // 2]
    both[0 : mine.shape[0], :] = mine[...]
    both[mine.shape[0] :, :] = theirs[...]


def joined(mine, theirs, first_face, faces):
    face = held(*faces[0].shape)
    out = pl.pallas_call(
        join_kernel,
        out_shape=(held(2 * mine.shape[0], mine.shape[1]),) + (face,) * len(faces),
        in_specs=[VMEM, VMEM] + [ANY] * (1 + len(faces)),
        out_specs=(VMEM,) + (ANY,) * len(faces),
        input_output_aliases={3 + i: 1 + i for i in range(len(faces))},
        compiler_params=kernel_params(8),
        name="join",
    )(mine, theirs, first_face, *faces)
    return out[0], out[1:]


def from_all(x):
    everywhere = lax.axis_size("row") * lax.axis_size("col")
    sent = x.reshape(everywhere, 1, -1)
    return lax.all_to_all(sent, ("row", "col"), split_axis=0, concat_axis=0, tiled=True).reshape(x.shape)


def shape(*dims):
    return jax.ShapeDtypeStruct(dims, F32)


def held(*dims):
    return pltpu.VMEM(dims, F32)


def in_hbm(x):
    return pltpu.with_memory_space_constraint(x, pltpu.HBM)


def kernel_params(mib):
    return pltpu.CompilerParams(vmem_limit_bytes=mib << 20)


def per_device(
    solution,
    residual,
    prev_direction,
    prev_dot,
    face_lists,
    multiplicity,
    block_pattern,
    schur,
    neumann_inverse,
    coarse_basis,
    primal_map,
    coarse_inverse,
):
    current, residual, previous = solution[0, 0], residual[0, 0], prev_direction[0, 0]
    faces, multiplicity = face_lists[0, 0], multiplicity[0, 0]
    pattern = jnp.transpose(block_pattern, (0, 3, 1, 2))[0]
    schur, neumann = schur[0, 0], neumann_inverse[0, 0]
    basis, primal_map = coarse_basis[0, 0], primal_map[0, 0]
    count, dofs, cases = residual.shape

    everywhere = lax.axis_size("row") * lax.axis_size("col")

    order = coarse_inverse.shape[1]
    face = held(SLOTS * dofs + 40, cases)
    indices = (faces, multiplicity, pattern, primal_map)
    local, send_2, told, send_3, send_0, send_1 = pl.pallas_call(
        local_kernel,
        out_shape=(held(count, dofs, cases), face, held(HEAD + 8 * (order // cases), cases), face, face, face),
        in_specs=[HBM] * 8,
        out_specs=(VMEM,) * 6,
        scratch_shapes=[pltpu.SMEM(x.shape, jnp.int32) for x in indices]
        + [
            pltpu.VMEM(residual.shape, F32),
            pltpu.VMEM(neumann.shape, F32),
            pltpu.VMEM(basis.shape, F32),
            pltpu.VMEM(coarse_inverse.shape, F32),
            pltpu.VMEM((count, dofs, 2 * cases), BF16),
            pltpu.SemaphoreType.DMA((4,)),
            pltpu.SemaphoreType.DMA((4,)),
            pltpu.SemaphoreType.DMA((8,)),
            pltpu.SemaphoreType.DMA((2,)),
        ],
        compiler_params=kernel_params(16),
        name="local_solve",
    )(*(in_hbm(x) for x in (*indices, residual, neumann, basis, coarse_inverse)))

    got_2 = swap_pairs(send_2, "col", 0)
    rounds = gather_rounds()
    near = lax.axis_size("col").bit_length() - 1
    for step, (axis, bit) in enumerate(rounds[:-1]):
        theirs = exchange(told, axis, bit)
        if step == near - 1:
            told, (send_3, send_0, send_1) = joined(told, theirs, got_2, (send_3, send_0, send_1))
        else:
            told = jnp.concatenate([told, theirs], axis=0)
    farther = exchange(told, *rounds[-1])
    got_3 = swap_pairs(send_3, "col", 1)
    got_0 = swap_pairs(send_0, "row", 0)
    got_1 = swap_pairs(send_1, "row", 1)

    started, stacked, coarse, precond_dot = pl.pallas_call(
        coarse_kernel,
        out_shape=(
            held(count, dofs, cases),
            pltpu.VMEM((count, 2 * dofs, 3 * dofs), BF16),
            held(order, cases),
            held(1, cases),
        ),
        in_specs=[SMEM] * 2 + [VMEM] * 5 + [HBM] * 2,
        out_specs=(VMEM,) * 4,
        scratch_shapes=[
            pltpu.VMEM((order, order), F32),
            pltpu.VMEM(previous.shape, F32),
            pltpu.VMEM(schur.shape, F32),
            pltpu.SemaphoreType.DMA,
            pltpu.SemaphoreType.DMA((4,)),
        ],
        compiler_params=kernel_params(32),
        name="coarse_solve",
    )(
        multiplicity, primal_map, local, told, farther, basis, prev_dot.reshape(1, cases),
        in_hbm(previous), in_hbm(schur),
    )

    direction, direction_held, image, send_2, send_3, send_0, send_1, curvature = pl.pallas_call(
        direction_kernel,
        out_shape=(shape(count, dofs, cases), held(count, dofs, cases), held(count, dofs, cases))
        + (held(SLOTS * dofs, cases),) * 4
        + (held(everywhere, cases),),
        in_specs=[SMEM] * 2 + [VMEM] * 7,
        out_specs=(HBM,) + (VMEM,) * 7,
        scratch_shapes=[
            pltpu.VMEM((17, dofs, cases), F32),
            pltpu.VMEM((count, dofs, 2 * cases), BF16),
            pltpu.SMEM((17,), jnp.int32),
            pltpu.SemaphoreType.DMA,
        ],
        compiler_params=kernel_params(16),
        name="direction_image",
    )(faces, pattern, started, coarse, got_2, got_3, got_0, got_1, stacked)

    got_2 = swap_pairs(send_2, "col", 0)
    got_3 = swap_pairs(send_3, "col", 1)
    got_0 = swap_pairs(send_0, "row", 0)
    got_1 = swap_pairs(send_1, "row", 1)
    curvature = from_all(curvature)

    new_solution, new_residual = pl.pallas_call(
        update_kernel,
        out_shape=(shape(count, dofs, cases),) * 2,
        in_specs=[SMEM] + [VMEM] * 10,
        out_specs=(HBM,) * 2,
        scratch_shapes=[
            pltpu.VMEM(residual.shape, F32),
            pltpu.VMEM(residual.shape, F32),
            pltpu.VMEM((17, dofs, cases), F32),
            pltpu.SMEM((17,), jnp.int32),
            pltpu.SemaphoreType.DMA((4,)),
            pltpu.SemaphoreType.DMA((4,)),
        ],
        compiler_params=kernel_params(16),
        name="update",
    )(
        faces, current, residual, direction_held, image, got_2, got_3, got_0, got_1, curvature, precond_dot
    )
    return (new_solution[None, None], new_residual[None, None], direction[None, None])


def solution(mesh):
    split = lambda dims: P("row", "col", *(None,) * dims)
    placed = (
        split(3), split(3), split(3), P(), split(2), split(1), split(2), split(4), split(4), split(2), split(1),
        P("col", None),
    )
    return jax.shard_map(
        per_device,
        mesh=mesh,
        in_specs=placed,
        out_specs=(split(3), split(3), split(3)),
        check_vma=False,
    )
```

```python
import jax
import jax.numpy as jnp
from jax import lax
from jax.experimental import pallas as pl
from jax.experimental.pallas import tpu as pltpu
from jax.sharding import PartitionSpec as P

F32 = jnp.float32
BF16 = jnp.bfloat16
SLOTS = 4
HEAD = 10
SMEM = pl.BlockSpec(memory_space=pltpu.SMEM)
VMEM = pl.BlockSpec(memory_space=pltpu.VMEM)
HBM = pl.BlockSpec(memory_space=pltpu.HBM)
ANY = pl.BlockSpec(memory_space=pl.ANY)


def halves(x):
    high = x.astype(BF16)
    return high, (x - high.astype(F32)).astype(BF16)


def dot(a, b):
    return jnp.dot(a, b, preferred_element_type=F32)


def dot_first(a, b):
    return lax.dot_general(a, b, (((0,), (0,)), ((), ())), preferred_element_type=F32)


def fold(x):
    width = x.shape[1] // 2
    return x[:, :width] + x[:, width:]


def product(matrix, pair):
    high, low = halves(matrix)
    return fold(dot(high, pair)) + dot(low, pair[:, : pair.shape[1] // 2])


def exact_pair(x):
    return jnp.concatenate(halves(x), axis=1)


def halved_rows(row_blocks):
    matrix = jnp.concatenate([row_blocks[k] for k in range(3)], axis=1)
    return jnp.concatenate(halves(matrix), axis=0)


def row_product(stacked, pattern, b, pairs):
    field = jnp.concatenate([pairs[pattern[k, 0, b]] for k in range(3)], axis=0)
    both = fold(dot(stacked, field))
    return both[:128] + both[128:]


def partial_rows(x):
    rows, cols = x.shape
    return jnp.sum(x.reshape(rows // 8, 8, cols), axis=0)


def weight_of(multiplicity, b):
    return 1.0 / jnp.full((1, 128), multiplicity[b].astype(F32))


def mapped(primal_map, shape, dim):
    place = lax.broadcasted_iota(jnp.int32, shape, dim)
    found = jnp.zeros(shape, jnp.int32)
    for p in range(8):
        found = jnp.where(place == p, primal_map[p], found)
    return found


def row_index():
    return 2 * lax.axis_index("y") + lax.axis_index("core")


def partner_faces():
    row, col = lax.axis_index("core"), lax.axis_index("col") % 2
    return 1 - row, row, 3 - col, 2 + col


def slots_by_block(faces, slot):
    for b in range(17):
        slot[b] = 16
    for s, f in enumerate(partner_faces()):
        for k in range(SLOTS):
            slot[faces[f, k]] = s * SLOTS + k


def local_kernel(
    faces_hbm, multiplicity_hbm, pattern_hbm, primal_map_hbm, residual_hbm, neumann_hbm, basis_hbm, inverse_hbm,
    local, send_2, told, send_3, send_0, send_1,
    faces, multiplicity, pattern, primal_map, residual, neumann, basis, inverse, pairs,
    index_sems, residual_sems, neumann_sems, basis_sems,
):
    count = residual.shape[0]
    index_copies = [
        pltpu.make_async_copy(source, target, index_sems.at[i])
        for i, (source, target) in enumerate(
            ((multiplicity_hbm, multiplicity), (pattern_hbm, pattern), (primal_map_hbm, primal_map), (faces_hbm, faces))
        )
    ]
    basis_copy = pltpu.make_async_copy(basis_hbm, basis, basis_sems.at[0])
    inverse_copy = pltpu.make_async_copy(inverse_hbm, inverse, basis_sems.at[1])
    copies = []
    for c in range(4):
        part = pl.ds(c * count // 4, count // 4)
        copies.append(pltpu.make_async_copy(residual_hbm.at[part], residual.at[part], residual_sems.at[c]))
    for c in range(8):
        part = pl.ds(c * count // 8, count // 8)
        copies.append(pltpu.make_async_copy(neumann_hbm.at[part], neumann.at[part], neumann_sems.at[c]))
    for copy in (*index_copies, *copies[:4], *copies[4:], basis_copy, inverse_copy):
        copy.start()
    for copy in index_copies:
        copy.wait()
    for b in range(count):
        if b % (count // 4) == 0:
            copies[b // (count // 4)].wait()
        pairs[b] = exact_pair(residual[b] * weight_of(multiplicity, b))
    total = jnp.zeros((8, 128), F32)
    for b in range(count):
        if b % (count // 8) == 0:
            copies[4 + b // (count // 8)].wait()
        weight = weight_of(multiplicity, b)
        out = row_product(halved_rows(neumann.at[b]), pattern, b, pairs) * weight
        local[b] = out
        total += partial_rows(residual[b] * out)
    basis_copy.wait()
    map_rows = mapped(primal_map, (8, 128), 0).astype(F32)
    for f, sent in zip(partner_faces(), (send_0, send_1, send_2, send_3)):
        for k in range(SLOTS):
            b = jnp.minimum(faces[f, k], count - 1)
            sent[k * 128 : (k + 1) * 128, :] = local[b]
            lanes = pl.ds(pl.multiple_of(b * 128, 128), 128)
            sent[512 + 8 * k : 520 + 8 * k, :] = basis[:, lanes] * weight_of(multiplicity, b)
        sent[544:552, :] = map_rows
    field = pairs[...].reshape(count * 128, 256)
    row = lax.broadcasted_iota(jnp.int32, (8, 128), 0)
    total = jnp.sum(total, axis=0, keepdims=True)
    map_row = mapped(primal_map, (8, 128), 1).astype(F32)
    inverse_copy.wait()
    sharers = inverse.shape[0] // 8
    mine = row_index() % sharers
    share = inverse[pl.ds(pl.multiple_of(mine * 8, 8), 8), :]
    rows = [product(basis[...], field), jnp.where(row == 0, total, map_row)[:2]]
    rows = jnp.concatenate(rows + [share[:, i : i + 128] for i in range(0, inverse.shape[1], 128)], axis=0)
    each = rows.shape[0]
    for i in range(told.shape[0] // each):
        told[each * i : each * i + each, :] = rows


def back(basis, own):
    bh, bl = (h.astype(F32) for h in halves(basis))
    oh, ol = (h.astype(F32) for h in halves(own))
    left = jnp.concatenate([bh, bl, bh, bl], axis=0).astype(BF16)
    right = jnp.concatenate([oh, oh, ol, ol], axis=0).astype(BF16)
    return dot_first(left, right)


def halving_kernel(schur_hbm, stacked, schur, sems):
    count = schur.shape[0]
    copies = []
    for c in range(4):
        part = pl.ds(c * count // 4, count // 4)
        copies.append(pltpu.make_async_copy(schur_hbm.at[part], schur.at[part], sems.at[c]))
        copies[c].start()
    for b in range(count):
        if b % (count // 4) == 0:
            copies[b // (count // 4)].wait()
        stacked[b] = halved_rows(schur.at[b])


def coarse_kernel(
    multiplicity, primal_map, local, same_core, other_core, basis, prev_dot, previous_hbm,
    started, wanted, precond_dot, inverse, previous, previous_sem,
):
    count = local.shape[0]
    previous_copy = pltpu.make_async_copy(previous_hbm, previous, previous_sem)
    previous_copy.start()

    order = inverse.shape[1]
    each = HEAD + 8 * (order // 128)
    half = same_core.shape[0] // each
    cols = lax.axis_size("col")
    sharers = order // cols // 8
    for told, core in ((same_core, lax.axis_index("core")), (other_core, 1 - lax.axis_index("core"))):
        for i in range(half):
            target = pl.multiple_of((i % cols * sharers + (2 * (i // cols) + core) % sharers) * 8, 8)
            for j in range(order // 128):
                source = i * each + HEAD + 8 * j
                inverse[pl.ds(target, 8), 128 * j : 128 * j + 128] = told[source : source + 8, :]

    def row_of_all(p):
        return jnp.concatenate([x[pl.ds(p, half, stride=each), :] for x in (same_core, other_core)], axis=0)

    maps = row_of_all(9).astype(jnp.int32)
    lane = lax.broadcasted_iota(jnp.int32, (2 * half, order), 1)
    chosen = [(maps[:, p : p + 1] == lane).astype(F32) for p in range(8)]
    chosen = jnp.concatenate(chosen, axis=0).astype(BF16)
    rows = jnp.concatenate([row_of_all(p) for p in range(8)], axis=0)
    rhs = fold(dot_first(chosen, exact_pair(rows)))
    coarse = product(inverse[...], exact_pair(rhs))
    dots = jnp.sum(row_of_all(8), axis=0, keepdims=True)
    dots = dots + jnp.sum(rhs * coarse, axis=0, keepdims=True)
    precond_dot[...] = dots
    beta = dots / prev_dot[...]
    wanted[...] = coarse

    lane = lax.broadcasted_iota(jnp.int32, (8, order), 1)
    own = (mapped(primal_map, (8, 128), 0)[:, 0:1] == lane).astype(F32).astype(BF16)
    own_back = back(basis[...], fold(dot(own, exact_pair(coarse))))
    previous_copy.wait()
    for b in range(count):
        mine = local[b] + own_back[b * 128 : (b + 1) * 128] * weight_of(multiplicity, b)
        started[b] = mine + beta * previous[b]
def direction_kernel(
    faces, pattern, started, coarse, got_2, got_3, got_0, got_1, stacked,
    direction_hbm, direction, image, send_2, send_3, send_0, send_1, curvature,
    added, pairs, slot, direction_sem,
):
    count = started.shape[0]
    order = coarse.shape[0]
    slots_by_block(faces, slot)
    received = (got_0, got_1, got_2, got_3)
    maps = jnp.concatenate([r[544:552, :] for r in received], axis=0).astype(jnp.int32)
    lane = lax.broadcasted_iota(jnp.int32, (32, order), 1)
    wanted = (maps[:, 0:1] == lane).astype(F32).astype(BF16)
    wanted = fold(dot(wanted, exact_pair(coarse[...])))
    for s, r in enumerate(received):
        face_basis = jnp.concatenate([r[512 + 8 * k : 520 + 8 * k, :] for k in range(SLOTS)], axis=1)
        face_back = back(face_basis, wanted[8 * s : 8 * s + 8])
        for k in range(SLOTS):
            part = slice(k * 128, (k + 1) * 128)
            added[s * SLOTS + k] = r[part, :] + face_back[part]
    added[16] = jnp.zeros((128, 128), F32)
    for b in range(count):
        value = started[b] + added[slot[b]]
        direction[b] = value
        pairs[b] = exact_pair(value)
    direction_copy = pltpu.make_async_copy(direction, direction_hbm, direction_sem)
    direction_copy.start()
    total = jnp.zeros((8, 128), F32)
    for b in range(count):
        out = row_product(stacked[b], pattern, b, pairs)
        image[b] = out
        total += partial_rows(direction[b] * out)
    for f, sent in zip(partner_faces(), (send_0, send_1, send_2, send_3)):
        for k in range(SLOTS):
            sent[k * 128 : (k + 1) * 128, :] = image[jnp.minimum(faces[f, k], count - 1)]
    curvature[...] = jnp.broadcast_to(jnp.sum(total, axis=0, keepdims=True), curvature.shape)
    direction_copy.wait()


def update_kernel(
    faces, current, residual, direction, image, got_2, got_3, got_0, got_1, curvature, precond_dot,
    new_solution_hbm, new_residual_hbm,
    new_solution, new_residual, added, slot, solution_sems, residual_sems,
):
    count = current.shape[0]
    slots_by_block(faces, slot)
    step = precond_dot[...] / jnp.sum(curvature[...], axis=0, keepdims=True)
    copies = []

    def leave(c, value, value_hbm, sems):
        part = pl.ds(c * count // 4, count // 4)
        copies.append(pltpu.make_async_copy(value.at[part], value_hbm.at[part], sems.at[c]))
        copies[-1].start()

    for b in range(count):
        new_solution[b] = current[b] + step * direction[b]
        if (b + 1) % (count // 4) == 0:
            leave(b // (count // 4), new_solution, new_solution_hbm, solution_sems)
    for s, r in enumerate((got_0, got_1, got_2, got_3)):
        for k in range(SLOTS):
            added[s * SLOTS + k] = r[k * 128 : (k + 1) * 128, :]
    added[16] = jnp.zeros((128, 128), F32)
    for b in range(count):
        new_residual[b] = residual[b] - step * (image[b] + added[slot[b]])
        if (b + 1) % (count // 4) == 0:
            leave(b // (count // 4), new_residual, new_residual_hbm, residual_sems)
    for copy in copies:
        copy.wait()


def swap_pairs(x, axis, first):
    pairs = [(i, i + 1) for i in range(first, lax.axis_size(axis) - 1, 2)]
    return lax.ppermute(x, axis, pairs + [(j, i) for i, j in pairs])


def from_all(x, axes):
    sent = x.reshape(lax.axis_size(axes), 1, -1)
    return lax.all_to_all(sent, axes, split_axis=0, concat_axis=0, tiled=True).reshape(x.shape)


def shape(*dims):
    return jax.ShapeDtypeStruct(dims, F32)


def held(*dims):
    return pltpu.VMEM(dims, F32)


def in_hbm(x):
    return pltpu.with_memory_space_constraint(x, pltpu.HBM)


def kernel_params(mib):
    return pltpu.CompilerParams(vmem_limit_bytes=mib << 20)


def per_device(
    solution,
    residual,
    prev_direction,
    prev_dot,
    face_lists,
    multiplicity,
    block_pattern,
    schur,
    neumann_inverse,
    coarse_basis,
    primal_map,
    coarse_inverse,
):
    current, residual, previous = solution[0, 0], residual[0, 0], prev_direction[0, 0]
    faces, multiplicity = face_lists[0, 0], multiplicity[0, 0]
    pattern = jnp.transpose(block_pattern, (0, 3, 1, 2))[0]
    schur, neumann = schur[0, 0], neumann_inverse[0, 0]
    basis, primal_map = coarse_basis[0, 0], primal_map[0, 0]
    count, dofs, cases = residual.shape

    everywhere = lax.axis_size(("y", "core", "col"))
    order = coarse_inverse.shape[1]
    told_rows = (HEAD + 8 * (order // cases)) * (everywhere // 2)

    face = held(SLOTS * dofs + 40, cases)
    indices = (faces, multiplicity, pattern, primal_map)
    local, send_2, told, send_3, send_0, send_1 = pl.pallas_call(
        local_kernel,
        out_shape=(held(count, dofs, cases), face, held(told_rows, cases), face, face, face),
        in_specs=[HBM] * 8,
        out_specs=(VMEM,) * 6,
        scratch_shapes=[pltpu.SMEM(x.shape, jnp.int32) for x in indices]
        + [
            pltpu.VMEM(residual.shape, F32),
            pltpu.VMEM(neumann.shape, F32),
            pltpu.VMEM(basis.shape, F32),
            pltpu.VMEM(coarse_inverse.shape, F32),
            pltpu.VMEM((count, dofs, 2 * cases), BF16),
            pltpu.SemaphoreType.DMA((4,)),
            pltpu.SemaphoreType.DMA((4,)),
            pltpu.SemaphoreType.DMA((8,)),
            pltpu.SemaphoreType.DMA((2,)),
        ],
        compiler_params=kernel_params(16),
        name="local_solve",
    )(*(in_hbm(x) for x in (*indices, residual, neumann, basis, coarse_inverse)))

    same_core = from_all(told, ("y", "col"))
    other_core = lax.ppermute(same_core, "core", [(0, 1), (1, 0)])
    got_2 = swap_pairs(send_2, "col", 0)
    got_3 = swap_pairs(send_3, "col", 1)
    got_0 = swap_pairs(send_0, ("y", "core"), 0)
    got_1 = swap_pairs(send_1, ("y", "core"), 1)

    stacked = pl.pallas_call(
        halving_kernel,
        out_shape=pltpu.VMEM((count, 2 * dofs, 3 * dofs), BF16),
        in_specs=[HBM],
        out_specs=VMEM,
        scratch_shapes=[pltpu.VMEM(schur.shape, F32), pltpu.SemaphoreType.DMA((4,))],
        compiler_params=kernel_params(12),
        name="halving",
    )(in_hbm(schur))

    started, coarse, precond_dot = pl.pallas_call(
        coarse_kernel,
        out_shape=(held(count, dofs, cases), held(order, cases), held(1, cases)),
        in_specs=[SMEM] * 2 + [VMEM] * 5 + [HBM],
        out_specs=(VMEM,) * 3,
        scratch_shapes=[
            pltpu.VMEM((order, order), F32),
            pltpu.VMEM(previous.shape, F32),
            pltpu.SemaphoreType.DMA,
        ],
        compiler_params=kernel_params(24),
        name="coarse_solve",
    )(
        multiplicity, primal_map, local, same_core, other_core, basis, prev_dot.reshape(1, cases),
        in_hbm(previous),
    )

    direction, direction_held, image, send_2, send_3, send_0, send_1, curvature = pl.pallas_call(
        direction_kernel,
        out_shape=(shape(count, dofs, cases), held(count, dofs, cases), held(count, dofs, cases))
        + (held(SLOTS * dofs, cases),) * 4
        + (held(everywhere, cases),),
        in_specs=[SMEM] * 2 + [VMEM] * 7,
        out_specs=(HBM,) + (VMEM,) * 7,
        scratch_shapes=[
            pltpu.VMEM((17, dofs, cases), F32),
            pltpu.VMEM((count, dofs, 2 * cases), BF16),
            pltpu.SMEM((17,), jnp.int32),
            pltpu.SemaphoreType.DMA,
        ],
        compiler_params=kernel_params(16),
        name="direction_image",
    )(faces, pattern, started, coarse, got_2, got_3, got_0, got_1, stacked)

    got_2 = swap_pairs(send_2, "col", 0)
    got_3 = swap_pairs(send_3, "col", 1)
    got_0 = swap_pairs(send_0, ("y", "core"), 0)
    got_1 = swap_pairs(send_1, ("y", "core"), 1)
    curvature = from_all(curvature, ("y", "core", "col"))

    new_solution, new_residual = pl.pallas_call(
        update_kernel,
        out_shape=(shape(count, dofs, cases),) * 2,
        in_specs=[SMEM] + [VMEM] * 10,
        out_specs=(HBM,) * 2,
        scratch_shapes=[
            pltpu.VMEM(residual.shape, F32),
            pltpu.VMEM(residual.shape, F32),
            pltpu.VMEM((17, dofs, cases), F32),
            pltpu.SMEM((17,), jnp.int32),
            pltpu.SemaphoreType.DMA((4,)),
            pltpu.SemaphoreType.DMA((4,)),
        ],
        compiler_params=kernel_params(16),
        name="update",
    )(
        faces, current, residual, direction_held, image, got_2, got_3, got_0, got_1, curvature, precond_dot
    )
    return (new_solution[None, None], new_residual[None, None], direction[None, None])


def solution(mesh):
    rows, cols = mesh.devices.shape
    mesh = jax.sharding.Mesh(mesh.devices.reshape(rows // 2, 2, cols), ("y", "core", "col"))
    split = lambda dims: P(("y", "core"), "col", *(None,) * dims)
    placed = (
        split(3), split(3), split(3), P(), split(2), split(1), split(2), split(4), split(4), split(2), split(1),
        P("col", None),
    )
    return jax.shard_map(
        per_device,
        mesh=mesh,
        in_specs=placed,
        out_specs=(split(3), split(3), split(3)),
        check_vma=False,
    )
```

```python
import jax
import jax.numpy as jnp
from jax import lax
from jax.experimental import pallas as pl
from jax.experimental.pallas import tpu as pltpu
from jax.sharding import PartitionSpec as P

F32 = jnp.float32
BF16 = jnp.bfloat16
SLOTS = 4
HEAD = 10
SMEM = pl.BlockSpec(memory_space=pltpu.SMEM)
VMEM = pl.BlockSpec(memory_space=pltpu.VMEM)
HBM = pl.BlockSpec(memory_space=pltpu.HBM)
ANY = pl.BlockSpec(memory_space=pl.ANY)


def halves(x):
    high = x.astype(BF16)
    return high, (x - high.astype(F32)).astype(BF16)


def dot(a, b):
    return jnp.dot(a, b, preferred_element_type=F32)


def dot_first(a, b):
    return lax.dot_general(a, b, (((0,), (0,)), ((), ())), preferred_element_type=F32)


def fold(x):
    width = x.shape[1] // 2
    return x[:, :width] + x[:, width:]


def product(matrix, pair):
    high, low = halves(matrix)
    return fold(dot(high, pair)) + dot(low, pair[:, : pair.shape[1] // 2])


def exact_pair(x):
    return jnp.concatenate(halves(x), axis=1)


def halved_rows(row_blocks):
    matrix = jnp.concatenate([row_blocks[k] for k in range(3)], axis=1)
    return jnp.concatenate(halves(matrix), axis=0)


def row_product(stacked, pattern, b, pairs):
    field = jnp.concatenate([pairs[pattern[k, 0, b]] for k in range(3)], axis=0)
    both = fold(dot(stacked, field))
    return both[:128] + both[128:]


def partial_rows(x):
    rows, cols = x.shape
    return jnp.sum(x.reshape(rows // 8, 8, cols), axis=0)


def weight_of(multiplicity, b):
    return 1.0 / jnp.full((1, 128), multiplicity[b].astype(F32))


def mapped(primal_map, shape, dim):
    place = lax.broadcasted_iota(jnp.int32, shape, dim)
    found = jnp.zeros(shape, jnp.int32)
    for p in range(8):
        found = jnp.where(place == p, primal_map[p], found)
    return found


def row_index():
    return 2 * lax.axis_index("y") + lax.axis_index("core")


def partner_faces():
    row, col = lax.axis_index("core"), lax.axis_index("col") % 2
    return 1 - row, row, 3 - col, 2 + col


def slots_by_block(faces, slot):
    for b in range(17):
        slot[b] = 16
    for s, f in enumerate(partner_faces()):
        for k in range(SLOTS):
            slot[faces[f, k]] = s * SLOTS + k


def local_kernel(
    faces_hbm, multiplicity_hbm, pattern_hbm, primal_map_hbm, residual_hbm, neumann_hbm, basis_hbm, inverse_hbm,
    local, send_2, told, send_3, send_0, send_1,
    faces, multiplicity, pattern, primal_map, residual, neumann, basis, inverse, pairs,
    index_sems, residual_sems, neumann_sems, basis_sems,
):
    count = residual.shape[0]
    index_copies = [
        pltpu.make_async_copy(source, target, index_sems.at[i])
        for i, (source, target) in enumerate(
            ((multiplicity_hbm, multiplicity), (pattern_hbm, pattern), (primal_map_hbm, primal_map), (faces_hbm, faces))
        )
    ]
    basis_copy = pltpu.make_async_copy(basis_hbm, basis, basis_sems.at[0])
    inverse_copy = pltpu.make_async_copy(inverse_hbm, inverse, basis_sems.at[1])
    copies = []
    for c in range(4):
        part = pl.ds(c * count // 4, count // 4)
        copies.append(pltpu.make_async_copy(residual_hbm.at[part], residual.at[part], residual_sems.at[c]))
    for c in range(8):
        part = pl.ds(c * count // 8, count // 8)
        copies.append(pltpu.make_async_copy(neumann_hbm.at[part], neumann.at[part], neumann_sems.at[c]))
    for copy in (*index_copies, *copies[:4], *copies[4:], basis_copy, inverse_copy):
        copy.start()
    for copy in index_copies:
        copy.wait()
    for b in range(count):
        if b % (count // 4) == 0:
            copies[b // (count // 4)].wait()
        pairs[b] = exact_pair(residual[b] * weight_of(multiplicity, b))
    total = jnp.zeros((8, 128), F32)
    for b in range(count):
        if b % (count // 8) == 0:
            copies[4 + b // (count // 8)].wait()
        weight = weight_of(multiplicity, b)
        out = row_product(halved_rows(neumann.at[b]), pattern, b, pairs) * weight
        local[b] = out
        total += partial_rows(residual[b] * out)
    basis_copy.wait()
    map_rows = mapped(primal_map, (8, 128), 0).astype(F32)
    for f, sent in zip(partner_faces(), (send_0, send_1, send_2, send_3)):
        for k in range(SLOTS):
            b = jnp.minimum(faces[f, k], count - 1)
            sent[k * 128 : (k + 1) * 128, :] = local[b]
            lanes = pl.ds(pl.multiple_of(b * 128, 128), 128)
            sent[512 + 8 * k : 520 + 8 * k, :] = basis[:, lanes] * weight_of(multiplicity, b)
        sent[544:552, :] = map_rows
    field = pairs[...].reshape(count * 128, 256)
    row = lax.broadcasted_iota(jnp.int32, (8, 128), 0)
    total = jnp.sum(total, axis=0, keepdims=True)
    map_row = mapped(primal_map, (8, 128), 1).astype(F32)
    inverse_copy.wait()
    sharers = inverse.shape[0] // 8
    mine = row_index() % sharers
    share = inverse[pl.ds(pl.multiple_of(mine * 8, 8), 8), :]
    rows = [product(basis[...], field), jnp.where(row == 0, total, map_row)[:2]]
    rows = jnp.concatenate(rows + [share[:, i : i + 128] for i in range(0, inverse.shape[1], 128)], axis=0)
    each = rows.shape[0]
    for i in range(told.shape[0] // each):
        told[each * i : each * i + each, :] = rows


def back(basis, own):
    bh, bl = (h.astype(F32) for h in halves(basis))
    oh, ol = (h.astype(F32) for h in halves(own))
    left = jnp.concatenate([bh, bl, bh, bl], axis=0).astype(BF16)
    right = jnp.concatenate([oh, oh, ol, ol], axis=0).astype(BF16)
    return dot_first(left, right)


def halving_kernel(schur_hbm, stacked, schur, sems):
    count = schur.shape[0]
    copies = []
    for c in range(4):
        part = pl.ds(c * count // 4, count // 4)
        copies.append(pltpu.make_async_copy(schur_hbm.at[part], schur.at[part], sems.at[c]))
        copies[c].start()
    for b in range(count):
        if b % (count // 4) == 0:
            copies[b // (count // 4)].wait()
        stacked[b] = halved_rows(schur.at[b])


def coarse_kernel(
    multiplicity, primal_map, local, same_core, other_core, basis, prev_dot, previous_hbm,
    started, wanted, precond_dot, inverse, previous, previous_sem,
):
    count = local.shape[0]
    previous_copy = pltpu.make_async_copy(previous_hbm, previous, previous_sem)
    previous_copy.start()

    order = inverse.shape[1]
    each = HEAD + 8 * (order // 128)
    half = same_core.shape[0] // each
    cols = lax.axis_size("col")
    sharers = order // cols // 8
    for told, core in ((same_core, lax.axis_index("core")), (other_core, 1 - lax.axis_index("core"))):
        for i in range(half):
            target = pl.multiple_of((i % cols * sharers + (2 * (i // cols) + core) % sharers) * 8, 8)
            for j in range(order // 128):
                source = i * each + HEAD + 8 * j
                inverse[pl.ds(target, 8), 128 * j : 128 * j + 128] = told[source : source + 8, :]

    def row_of_all(p):
        return jnp.concatenate([x[pl.ds(p, half, stride=each), :] for x in (same_core, other_core)], axis=0)

    maps = row_of_all(9).astype(jnp.int32)
    lane = lax.broadcasted_iota(jnp.int32, (2 * half, order), 1)
    chosen = [(maps[:, p : p + 1] == lane).astype(F32) for p in range(8)]
    chosen = jnp.concatenate(chosen, axis=0).astype(BF16)
    rows = jnp.concatenate([row_of_all(p) for p in range(8)], axis=0)
    rhs = fold(dot_first(chosen, exact_pair(rows)))
    coarse = product(inverse[...], exact_pair(rhs))
    dots = jnp.sum(row_of_all(8), axis=0, keepdims=True)
    dots = dots + jnp.sum(rhs * coarse, axis=0, keepdims=True)
    precond_dot[...] = dots
    beta = dots / prev_dot[...]
    wanted[...] = coarse

    lane = lax.broadcasted_iota(jnp.int32, (8, order), 1)
    own = (mapped(primal_map, (8, 128), 0)[:, 0:1] == lane).astype(F32).astype(BF16)
    own_back = back(basis[...], fold(dot(own, exact_pair(coarse))))
    previous_copy.wait()
    for b in range(count):
        mine = local[b] + own_back[b * 128 : (b + 1) * 128] * weight_of(multiplicity, b)
        started[b] = mine + beta * previous[b]
def direction_kernel(
    faces, pattern, started, coarse, got_2, got_3, got_0, got_1, stacked,
    direction_hbm, direction, image, send_2, send_3, send_0, send_1, curvature,
    added, pairs, slot, direction_sem,
):
    count = started.shape[0]
    order = coarse.shape[0]
    slots_by_block(faces, slot)
    received = (got_0, got_1, got_2, got_3)
    maps = jnp.concatenate([r[544:552, :] for r in received], axis=0).astype(jnp.int32)
    lane = lax.broadcasted_iota(jnp.int32, (32, order), 1)
    wanted = (maps[:, 0:1] == lane).astype(F32).astype(BF16)
    wanted = fold(dot(wanted, exact_pair(coarse[...])))
    for s, r in enumerate(received):
        face_basis = jnp.concatenate([r[512 + 8 * k : 520 + 8 * k, :] for k in range(SLOTS)], axis=1)
        face_back = back(face_basis, wanted[8 * s : 8 * s + 8])
        for k in range(SLOTS):
            part = slice(k * 128, (k + 1) * 128)
            added[s * SLOTS + k] = r[part, :] + face_back[part]
    added[16] = jnp.zeros((128, 128), F32)
    for b in range(count):
        value = started[b] + added[slot[b]]
        direction[b] = value
        pairs[b] = exact_pair(value)
    direction_copy = pltpu.make_async_copy(direction, direction_hbm, direction_sem)
    direction_copy.start()
    total = jnp.zeros((8, 128), F32)
    for b in range(count):
        out = row_product(stacked[b], pattern, b, pairs)
        image[b] = out
        total += partial_rows(direction[b] * out)
    for f, sent in zip(partner_faces(), (send_0, send_1, send_2, send_3)):
        for k in range(SLOTS):
            sent[k * 128 : (k + 1) * 128, :] = image[jnp.minimum(faces[f, k], count - 1)]
    curvature[...] = jnp.broadcast_to(jnp.sum(total, axis=0, keepdims=True), curvature.shape)
    direction_copy.wait()


def update_kernel(
    faces, current, residual, direction, image, got_2, got_3, got_0, got_1, curvature, precond_dot,
    new_solution_hbm, new_residual_hbm,
    new_solution, new_residual, added, slot, solution_sems, residual_sems,
):
    count = current.shape[0]
    slots_by_block(faces, slot)
    step = precond_dot[...] / jnp.sum(curvature[...], axis=0, keepdims=True)
    copies = []

    def leave(c, value, value_hbm, sems):
        part = pl.ds(c * count // 4, count // 4)
        copies.append(pltpu.make_async_copy(value.at[part], value_hbm.at[part], sems.at[c]))
        copies[-1].start()

    for b in range(count):
        new_solution[b] = current[b] + step * direction[b]
        if (b + 1) % (count // 4) == 0:
            leave(b // (count // 4), new_solution, new_solution_hbm, solution_sems)
    for s, r in enumerate((got_0, got_1, got_2, got_3)):
        for k in range(SLOTS):
            added[s * SLOTS + k] = r[k * 128 : (k + 1) * 128, :]
    added[16] = jnp.zeros((128, 128), F32)
    for b in range(count):
        new_residual[b] = residual[b] - step * (image[b] + added[slot[b]])
        if (b + 1) % (count // 4) == 0:
            leave(b // (count // 4), new_residual, new_residual_hbm, residual_sems)
    for copy in copies:
        copy.wait()


def swap_pairs(x, axis, first):
    pairs = [(i, i + 1) for i in range(first, lax.axis_size(axis) - 1, 2)]
    return lax.ppermute(x, axis, pairs + [(j, i) for i, j in pairs])


def pass_kernel(first, *rest):
    pass


def passed(first, *arrays):
    return pl.pallas_call(
        pass_kernel,
        out_shape=[held(*x.shape) for x in arrays],
        in_specs=[ANY] * (1 + len(arrays)),
        out_specs=[ANY] * len(arrays),
        input_output_aliases={1 + i: i for i in range(len(arrays))},
        compiler_params=kernel_params(4),
        name="passed",
    )(first, *arrays)


def from_all(x, axes):
    sent = x.reshape(lax.axis_size(axes), 1, -1)
    return lax.all_to_all(sent, axes, split_axis=0, concat_axis=0, tiled=True).reshape(x.shape)


def shape(*dims):
    return jax.ShapeDtypeStruct(dims, F32)


def held(*dims):
    return pltpu.VMEM(dims, F32)


def in_hbm(x):
    return pltpu.with_memory_space_constraint(x, pltpu.HBM)


def kernel_params(mib):
    return pltpu.CompilerParams(vmem_limit_bytes=mib << 20)


def per_device(
    solution,
    residual,
    prev_direction,
    prev_dot,
    face_lists,
    multiplicity,
    block_pattern,
    schur,
    neumann_inverse,
    coarse_basis,
    primal_map,
    coarse_inverse,
):
    current, residual, previous = solution[0, 0], residual[0, 0], prev_direction[0, 0]
    faces, multiplicity = face_lists[0, 0], multiplicity[0, 0]
    pattern = jnp.transpose(block_pattern, (0, 3, 1, 2))[0]
    schur, neumann = schur[0, 0], neumann_inverse[0, 0]
    basis, primal_map = coarse_basis[0, 0], primal_map[0, 0]
    count, dofs, cases = residual.shape

    everywhere = lax.axis_size(("y", "core", "col"))
    order = coarse_inverse.shape[1]
    told_rows = (HEAD + 8 * (order // cases)) * (everywhere // 2)

    face = held(SLOTS * dofs + 40, cases)
    indices = (faces, multiplicity, pattern, primal_map)
    local, send_2, told, send_3, send_0, send_1 = pl.pallas_call(
        local_kernel,
        out_shape=(held(count, dofs, cases), face, held(told_rows, cases), face, face, face),
        in_specs=[HBM] * 8,
        out_specs=(VMEM,) * 6,
        scratch_shapes=[pltpu.SMEM(x.shape, jnp.int32) for x in indices]
        + [
            pltpu.VMEM(residual.shape, F32),
            pltpu.VMEM(neumann.shape, F32),
            pltpu.VMEM(basis.shape, F32),
            pltpu.VMEM(coarse_inverse.shape, F32),
            pltpu.VMEM((count, dofs, 2 * cases), BF16),
            pltpu.SemaphoreType.DMA((4,)),
            pltpu.SemaphoreType.DMA((4,)),
            pltpu.SemaphoreType.DMA((8,)),
            pltpu.SemaphoreType.DMA((2,)),
        ],
        compiler_params=kernel_params(16),
        name="local_solve",
    )(*(in_hbm(x) for x in (*indices, residual, neumann, basis, coarse_inverse)))

    got_2 = swap_pairs(send_2, "col", 0)
    same_core = lax.cond(
        lax.axis_index("col") < lax.axis_size("col"), lambda x: from_all(x, ("y", "col")), lambda x: x, told
    )
    same_core, send_3, send_0, send_1 = passed(got_2, same_core, send_3, send_0, send_1)
    other_core = lax.ppermute(same_core, "core", [(0, 1), (1, 0)])
    got_3 = swap_pairs(send_3, "col", 1)
    got_0 = swap_pairs(send_0, ("y", "core"), 0)
    got_1 = swap_pairs(send_1, ("y", "core"), 1)

    stacked = pl.pallas_call(
        halving_kernel,
        out_shape=pltpu.VMEM((count, 2 * dofs, 3 * dofs), BF16),
        in_specs=[HBM],
        out_specs=VMEM,
        scratch_shapes=[pltpu.VMEM(schur.shape, F32), pltpu.SemaphoreType.DMA((4,))],
        compiler_params=kernel_params(12),
        name="halving",
    )(in_hbm(schur))

    started, coarse, precond_dot = pl.pallas_call(
        coarse_kernel,
        out_shape=(held(count, dofs, cases), held(order, cases), held(1, cases)),
        in_specs=[SMEM] * 2 + [VMEM] * 5 + [HBM],
        out_specs=(VMEM,) * 3,
        scratch_shapes=[
            pltpu.VMEM((order, order), F32),
            pltpu.VMEM(previous.shape, F32),
            pltpu.SemaphoreType.DMA,
        ],
        compiler_params=kernel_params(24),
        name="coarse_solve",
    )(
        multiplicity, primal_map, local, same_core, other_core, basis, prev_dot.reshape(1, cases),
        in_hbm(previous),
    )

    direction, direction_held, image, send_2, send_3, send_0, send_1, curvature = pl.pallas_call(
        direction_kernel,
        out_shape=(shape(count, dofs, cases), held(count, dofs, cases), held(count, dofs, cases))
        + (held(SLOTS * dofs, cases),) * 4
        + (held(everywhere, cases),),
        in_specs=[SMEM] * 2 + [VMEM] * 7,
        out_specs=(HBM,) + (VMEM,) * 7,
        scratch_shapes=[
            pltpu.VMEM((17, dofs, cases), F32),
            pltpu.VMEM((count, dofs, 2 * cases), BF16),
            pltpu.SMEM((17,), jnp.int32),
            pltpu.SemaphoreType.DMA,
        ],
        compiler_params=kernel_params(16),
        name="direction_image",
    )(faces, pattern, started, coarse, got_2, got_3, got_0, got_1, stacked)

    got_2 = swap_pairs(send_2, "col", 0)
    got_3 = swap_pairs(send_3, "col", 1)
    got_0 = swap_pairs(send_0, ("y", "core"), 0)
    got_1 = swap_pairs(send_1, ("y", "core"), 1)
    curvature = from_all(curvature, ("y", "core", "col"))

    new_solution, new_residual = pl.pallas_call(
        update_kernel,
        out_shape=(shape(count, dofs, cases),) * 2,
        in_specs=[SMEM] + [VMEM] * 10,
        out_specs=(HBM,) * 2,
        scratch_shapes=[
            pltpu.VMEM(residual.shape, F32),
            pltpu.VMEM(residual.shape, F32),
            pltpu.VMEM((17, dofs, cases), F32),
            pltpu.SMEM((17,), jnp.int32),
            pltpu.SemaphoreType.DMA((4,)),
            pltpu.SemaphoreType.DMA((4,)),
        ],
        compiler_params=kernel_params(16),
        name="update",
    )(
        faces, current, residual, direction_held, image, got_2, got_3, got_0, got_1, curvature, precond_dot
    )
    return (new_solution[None, None], new_residual[None, None], direction[None, None])


def solution(mesh):
    rows, cols = mesh.devices.shape
    mesh = jax.sharding.Mesh(mesh.devices.reshape(rows // 2, 2, cols), ("y", "core", "col"))
    split = lambda dims: P(("y", "core"), "col", *(None,) * dims)
    placed = (
        split(3), split(3), split(3), P(), split(2), split(1), split(2), split(4), split(4), split(2), split(1),
        P("col", None),
    )
    return jax.shard_map(
        per_device,
        mesh=mesh,
        in_specs=placed,
        out_specs=(split(3), split(3), split(3)),
        check_vma=False,
    )
```

```python
import jax
import jax.numpy as jnp
from jax import lax
from jax.experimental import pallas as pl
from jax.experimental.pallas import tpu as pltpu
from jax.sharding import PartitionSpec as P

F32 = jnp.float32
BF16 = jnp.bfloat16
SLOTS = 4
HEAD = 10
SMEM = pl.BlockSpec(memory_space=pltpu.SMEM)
VMEM = pl.BlockSpec(memory_space=pltpu.VMEM)
HBM = pl.BlockSpec(memory_space=pltpu.HBM)
ANY = pl.BlockSpec(memory_space=pl.ANY)


def halves(x):
    high = x.astype(BF16)
    return high, (x - high.astype(F32)).astype(BF16)


def dot(a, b):
    return jnp.dot(a, b, preferred_element_type=F32)


def dot_first(a, b):
    return lax.dot_general(a, b, (((0,), (0,)), ((), ())), preferred_element_type=F32)


def fold(x):
    width = x.shape[1] // 2
    return x[:, :width] + x[:, width:]


def product(matrix, pair):
    high, low = halves(matrix)
    return fold(dot(high, pair)) + dot(low, pair[:, : pair.shape[1] // 2])


def exact_pair(x):
    return jnp.concatenate(halves(x), axis=1)


def halved_rows(row_blocks):
    matrix = jnp.concatenate([row_blocks[k] for k in range(3)], axis=1)
    return jnp.concatenate(halves(matrix), axis=0)


def row_product(stacked, pattern, b, pairs):
    field = jnp.concatenate([pairs[pattern[k, 0, b]] for k in range(3)], axis=0)
    both = fold(dot(stacked, field))
    return both[:128] + both[128:]


def partial_rows(x):
    rows, cols = x.shape
    return jnp.sum(x.reshape(rows // 8, 8, cols), axis=0)


def weight_of(multiplicity, b):
    return 1.0 / jnp.full((1, 128), multiplicity[b].astype(F32))


def mapped(primal_map, shape, dim):
    place = lax.broadcasted_iota(jnp.int32, shape, dim)
    found = jnp.zeros(shape, jnp.int32)
    for p in range(8):
        found = jnp.where(place == p, primal_map[p], found)
    return found


def row_index():
    return 2 * lax.axis_index("y") + lax.axis_index("core")


def partner_faces():
    row, col = lax.axis_index("core"), lax.axis_index("col") % 2
    return 1 - row, row, 3 - col, 2 + col


def slots_by_block(faces, slot, swaps):
    none = len(swaps) * SLOTS
    for b in range(17):
        slot[b] = none
    partners = partner_faces()
    for i, s in enumerate(swaps):
        for k in range(SLOTS):
            slot[faces[partners[s], k]] = i * SLOTS + k


def local_kernel(
    faces_hbm, multiplicity_hbm, pattern_hbm, primal_map_hbm, residual_hbm, neumann_hbm, basis_hbm, inverse_hbm,
    local, send_2, told, send_3, send_0, send_1,
    faces, multiplicity, pattern, primal_map, residual, neumann, basis, inverse, pairs,
    index_sems, residual_sems, neumann_sems, basis_sems,
):
    count = residual.shape[0]
    index_copies = [
        pltpu.make_async_copy(source, target, index_sems.at[i])
        for i, (source, target) in enumerate(
            ((multiplicity_hbm, multiplicity), (pattern_hbm, pattern), (primal_map_hbm, primal_map), (faces_hbm, faces))
        )
    ]
    basis_copy = pltpu.make_async_copy(basis_hbm, basis, basis_sems.at[0])
    inverse_copy = pltpu.make_async_copy(inverse_hbm, inverse, basis_sems.at[1])
    copies = []
    for c in range(2):
        part = pl.ds(c * count // 2, count // 2)
        copies.append(pltpu.make_async_copy(residual_hbm.at[part], residual.at[part], residual_sems.at[c]))
    for c in range(4):
        part = pl.ds(c * count // 4, count // 4)
        copies.append(pltpu.make_async_copy(neumann_hbm.at[part], neumann.at[part], neumann_sems.at[c]))
    for copy in (*index_copies, *copies, basis_copy, inverse_copy):
        copy.start()
    for copy in index_copies:
        copy.wait()
    for b in range(count):
        if b % (count // 2) == 0:
            copies[b // (count // 2)].wait()
        pairs[b] = exact_pair(residual[b] * weight_of(multiplicity, b))
    total = jnp.zeros((8, 128), F32)
    for b in range(count):
        if b % (count // 4) == 0:
            copies[2 + b // (count // 4)].wait()
        weight = weight_of(multiplicity, b)
        out = row_product(halved_rows(neumann.at[b]), pattern, b, pairs) * weight
        local[b] = out
        total += partial_rows(residual[b] * out)
    basis_copy.wait()
    map_rows = mapped(primal_map, (8, 128), 0).astype(F32)
    for f, sent in zip(partner_faces(), (send_0, send_1, send_2, send_3)):
        for k in range(SLOTS):
            b = jnp.minimum(faces[f, k], count - 1)
            sent[k * 128 : (k + 1) * 128, :] = local[b]
            lanes = pl.ds(pl.multiple_of(b * 128, 128), 128)
            sent[512 + 8 * k : 520 + 8 * k, :] = basis[:, lanes] * weight_of(multiplicity, b)
        sent[544:552, :] = map_rows
    field = pairs[...].reshape(count * 128, 256)
    row = lax.broadcasted_iota(jnp.int32, (8, 128), 0)
    total = jnp.sum(total, axis=0, keepdims=True)
    map_row = mapped(primal_map, (8, 128), 1).astype(F32)
    inverse_copy.wait()
    sharers = inverse.shape[0] // 8
    mine = row_index() % sharers
    share = inverse[pl.ds(pl.multiple_of(mine * 8, 8), 8), :]
    rows = [product(basis[...], field), jnp.where(row == 0, total, map_row)[:2]]
    rows = jnp.concatenate(rows + [share[:, i : i + 128] for i in range(0, inverse.shape[1], 128)], axis=0)
    each = rows.shape[0]
    for i in range(told.shape[0] // each):
        told[each * i : each * i + each, :] = rows


def back(basis, own):
    bh, bl = (h.astype(F32) for h in halves(basis))
    oh, ol = (h.astype(F32) for h in halves(own))
    left = jnp.concatenate([bh, bl, bh, bl], axis=0).astype(BF16)
    right = jnp.concatenate([oh, oh, ol, ol], axis=0).astype(BF16)
    return dot_first(left, right)


def halving_kernel(schur_hbm, stacked, schur, sems):
    count = schur.shape[0]
    copies = []
    for c in range(4):
        part = pl.ds(c * count // 4, count // 4)
        copies.append(pltpu.make_async_copy(schur_hbm.at[part], schur.at[part], sems.at[c]))
        copies[c].start()
    for b in range(count):
        if b % (count // 4) == 0:
            copies[b // (count // 4)].wait()
        stacked[b] = halved_rows(schur.at[b])


def add_faces(received, coarse, added):
    maps = jnp.concatenate([r[544:552, :] for r in received], axis=0).astype(jnp.int32)
    lane = lax.broadcasted_iota(jnp.int32, (8 * len(received), coarse.shape[0]), 1)
    wanted = (maps[:, 0:1] == lane).astype(F32).astype(BF16)
    wanted = fold(dot(wanted, exact_pair(coarse)))
    for i, r in enumerate(received):
        face_basis = jnp.concatenate([r[512 + 8 * k : 520 + 8 * k, :] for k in range(SLOTS)], axis=1)
        face_back = back(face_basis, wanted[8 * i : 8 * i + 8])
        for k in range(SLOTS):
            part = slice(k * 128, (k + 1) * 128)
            added[i * SLOTS + k] = r[part, :] + face_back[part]
    added[len(received) * SLOTS] = jnp.zeros((128, 128), F32)


def coarse_kernel(
    faces, multiplicity, primal_map, local, same_core, other_core, got_2, got_0, got_1, basis, prev_dot, previous_hbm,
    started, wanted, precond_dot, inverse, added, slot, previous, previous_sem,
):
    count = local.shape[0]
    previous_copy = pltpu.make_async_copy(previous_hbm, previous, previous_sem)
    previous_copy.start()

    order = inverse.shape[1]
    each = HEAD + 8 * (order // 128)
    half = same_core.shape[0] // each
    cols = lax.axis_size("col")
    sharers = order // cols // 8
    for told, core in ((same_core, lax.axis_index("core")), (other_core, 1 - lax.axis_index("core"))):
        for i in range(half):
            target = pl.multiple_of((i % cols * sharers + (2 * (i // cols) + core) % sharers) * 8, 8)
            for j in range(order // 128):
                source = i * each + HEAD + 8 * j
                inverse[pl.ds(target, 8), 128 * j : 128 * j + 128] = told[source : source + 8, :]

    def row_of_all(p):
        return jnp.concatenate([x[pl.ds(p, half, stride=each), :] for x in (same_core, other_core)], axis=0)

    maps = row_of_all(9).astype(jnp.int32)
    lane = lax.broadcasted_iota(jnp.int32, (2 * half, order), 1)
    chosen = [(maps[:, p : p + 1] == lane).astype(F32) for p in range(8)]
    chosen = jnp.concatenate(chosen, axis=0).astype(BF16)
    rows = jnp.concatenate([row_of_all(p) for p in range(8)], axis=0)
    rhs = fold(dot_first(chosen, exact_pair(rows)))
    coarse = product(inverse[...], exact_pair(rhs))
    dots = jnp.sum(row_of_all(8), axis=0, keepdims=True)
    dots = dots + jnp.sum(rhs * coarse, axis=0, keepdims=True)
    precond_dot[...] = dots
    beta = dots / prev_dot[...]
    wanted[...] = coarse

    lane = lax.broadcasted_iota(jnp.int32, (8, order), 1)
    own = (mapped(primal_map, (8, 128), 0)[:, 0:1] == lane).astype(F32).astype(BF16)
    own_back = back(basis[...], fold(dot(own, exact_pair(coarse))))
    slots_by_block(faces, slot, (2, 0, 1))
    add_faces((got_2, got_0, got_1), coarse, added)
    previous_copy.wait()
    for b in range(count):
        mine = local[b] + own_back[b * 128 : (b + 1) * 128] * weight_of(multiplicity, b)
        started[b] = mine + added[slot[b]] + beta * previous[b]
def direction_kernel(
    faces, pattern, started, coarse, got_3, stacked,
    direction_hbm, direction, image, send_2, send_3, send_0, send_1, curvature,
    added, pairs, slot, direction_sem,
):
    count = started.shape[0]
    slots_by_block(faces, slot, (3,))
    add_faces((got_3,), coarse[...], added)
    for b in range(count):
        value = started[b] + added[slot[b]]
        direction[b] = value
        pairs[b] = exact_pair(value)
    direction_copy = pltpu.make_async_copy(direction, direction_hbm, direction_sem)
    direction_copy.start()
    total = jnp.zeros((8, 128), F32)
    for b in range(count):
        out = row_product(stacked[b], pattern, b, pairs)
        image[b] = out
        total += partial_rows(direction[b] * out)
    for f, sent in zip(partner_faces(), (send_0, send_1, send_2, send_3)):
        for k in range(SLOTS):
            sent[k * 128 : (k + 1) * 128, :] = image[jnp.minimum(faces[f, k], count - 1)]
    curvature[...] = jnp.broadcast_to(jnp.sum(total, axis=0, keepdims=True), curvature.shape)
    direction_copy.wait()


def update_kernel(
    faces, current, residual, direction, image, got_2, got_3, got_0, got_1, curvature, precond_dot,
    new_solution_hbm, new_residual_hbm,
    new_solution, new_residual, added, slot, solution_sems, residual_sems,
):
    count = current.shape[0]
    slots_by_block(faces, slot, (0, 1, 2, 3))
    step = precond_dot[...] / jnp.sum(curvature[...], axis=0, keepdims=True)
    copies = []

    def leave(c, value, value_hbm, sems):
        part = pl.ds(c * count // 4, count // 4)
        copies.append(pltpu.make_async_copy(value.at[part], value_hbm.at[part], sems.at[c]))
        copies[-1].start()

    for b in range(count):
        new_solution[b] = current[b] + step * direction[b]
        if (b + 1) % (count // 4) == 0:
            leave(b // (count // 4), new_solution, new_solution_hbm, solution_sems)
    for s, r in enumerate((got_0, got_1, got_2, got_3)):
        for k in range(SLOTS):
            added[s * SLOTS + k] = r[k * 128 : (k + 1) * 128, :]
    added[16] = jnp.zeros((128, 128), F32)
    for b in range(count):
        new_residual[b] = residual[b] - step * (image[b] + added[slot[b]])
        if (b + 1) % (count // 4) == 0:
            leave(b // (count // 4), new_residual, new_residual_hbm, residual_sems)
    for copy in copies:
        copy.wait()


def swap_pairs(x, axis, first):
    pairs = [(i, i + 1) for i in range(first, lax.axis_size(axis) - 1, 2)]
    return lax.ppermute(x, axis, pairs + [(j, i) for i, j in pairs])


def pass_kernel(*refs):
    pass


def passed(awaited, *arrays):
    return pl.pallas_call(
        pass_kernel,
        out_shape=[held(*x.shape) for x in arrays],
        in_specs=[ANY] * (len(awaited) + len(arrays)),
        out_specs=[ANY] * len(arrays),
        input_output_aliases={len(awaited) + i: i for i in range(len(arrays))},
        compiler_params=kernel_params(4),
        name="passed",
    )(*awaited, *arrays)


def from_all(x, axes):
    sent = x.reshape(lax.axis_size(axes), 1, -1)
    return lax.all_to_all(sent, axes, split_axis=0, concat_axis=0, tiled=True).reshape(x.shape)


def shape(*dims):
    return jax.ShapeDtypeStruct(dims, F32)


def held(*dims):
    return pltpu.VMEM(dims, F32)


def in_hbm(x):
    return pltpu.with_memory_space_constraint(x, pltpu.HBM)


def kernel_params(mib):
    return pltpu.CompilerParams(vmem_limit_bytes=mib << 20)


def per_device(
    solution,
    residual,
    prev_direction,
    prev_dot,
    face_lists,
    multiplicity,
    block_pattern,
    schur,
    neumann_inverse,
    coarse_basis,
    primal_map,
    coarse_inverse,
):
    current, residual, previous = solution[0, 0], residual[0, 0], prev_direction[0, 0]
    faces, multiplicity = face_lists[0, 0], multiplicity[0, 0]
    pattern = jnp.transpose(block_pattern, (0, 3, 1, 2))[0]
    schur, neumann = schur[0, 0], neumann_inverse[0, 0]
    basis, primal_map = coarse_basis[0, 0], primal_map[0, 0]
    count, dofs, cases = residual.shape

    everywhere = lax.axis_size(("y", "core", "col"))
    order = coarse_inverse.shape[1]
    told_rows = (HEAD + 8 * (order // cases)) * (everywhere // 2)

    face = held(SLOTS * dofs + 40, cases)
    indices = (faces, multiplicity, pattern, primal_map)
    local, send_2, told, send_3, send_0, send_1 = pl.pallas_call(
        local_kernel,
        out_shape=(held(count, dofs, cases), face, held(told_rows, cases), face, face, face),
        in_specs=[HBM] * 8,
        out_specs=(VMEM,) * 6,
        scratch_shapes=[pltpu.SMEM(x.shape, jnp.int32) for x in indices]
        + [
            pltpu.VMEM(residual.shape, F32),
            pltpu.VMEM(neumann.shape, F32),
            pltpu.VMEM(basis.shape, F32),
            pltpu.VMEM(coarse_inverse.shape, F32),
            pltpu.VMEM((count, dofs, 2 * cases), BF16),
            pltpu.SemaphoreType.DMA((4,)),
            pltpu.SemaphoreType.DMA((2,)),
            pltpu.SemaphoreType.DMA((4,)),
            pltpu.SemaphoreType.DMA((2,)),
        ],
        compiler_params=kernel_params(16),
        name="local_solve",
    )(*(in_hbm(x) for x in (*indices, residual, neumann, basis, coarse_inverse)))

    got_2 = swap_pairs(send_2, "col", 0)
    got_0 = swap_pairs(send_0, ("y", "core"), 0)
    got_1 = swap_pairs(send_1, ("y", "core"), 1)
    same_core = lax.cond(
        lax.axis_index("col") < lax.axis_size("col"), lambda x: from_all(x, ("y", "col")), lambda x: x, told
    )
    same_core, send_3 = passed((got_2, got_0, got_1), same_core, send_3)
    other_core = lax.ppermute(same_core, "core", [(0, 1), (1, 0)])
    got_3 = swap_pairs(send_3, "col", 1)

    stacked = pl.pallas_call(
        halving_kernel,
        out_shape=pltpu.VMEM((count, 2 * dofs, 3 * dofs), BF16),
        in_specs=[HBM],
        out_specs=VMEM,
        scratch_shapes=[pltpu.VMEM(schur.shape, F32), pltpu.SemaphoreType.DMA((4,))],
        compiler_params=kernel_params(12),
        name="halving",
    )(in_hbm(schur))

    started, coarse, precond_dot = pl.pallas_call(
        coarse_kernel,
        out_shape=(held(count, dofs, cases), held(order, cases), held(1, cases)),
        in_specs=[SMEM] * 3 + [VMEM] * 8 + [HBM],
        out_specs=(VMEM,) * 3,
        scratch_shapes=[
            pltpu.VMEM((order, order), F32),
            pltpu.VMEM((3 * SLOTS + 1, dofs, cases), F32),
            pltpu.SMEM((17,), jnp.int32),
            pltpu.VMEM(previous.shape, F32),
            pltpu.SemaphoreType.DMA,
        ],
        compiler_params=kernel_params(24),
        name="coarse_solve",
    )(
        faces, multiplicity, primal_map, local, same_core, other_core, got_2, got_0, got_1,
        basis, prev_dot.reshape(1, cases),
        in_hbm(previous),
    )

    direction, direction_held, image, send_2, send_3, send_0, send_1, curvature = pl.pallas_call(
        direction_kernel,
        out_shape=(shape(count, dofs, cases), held(count, dofs, cases), held(count, dofs, cases))
        + (held(SLOTS * dofs, cases),) * 4
        + (held(everywhere, cases),),
        in_specs=[SMEM] * 2 + [VMEM] * 4,
        out_specs=(HBM,) + (VMEM,) * 7,
        scratch_shapes=[
            pltpu.VMEM((SLOTS + 1, dofs, cases), F32),
            pltpu.VMEM((count, dofs, 2 * cases), BF16),
            pltpu.SMEM((17,), jnp.int32),
            pltpu.SemaphoreType.DMA,
        ],
        compiler_params=kernel_params(16),
        name="direction_image",
    )(faces, pattern, started, coarse, got_3, stacked)

    got_2 = swap_pairs(send_2, "col", 0)
    got_3 = swap_pairs(send_3, "col", 1)
    got_0 = swap_pairs(send_0, ("y", "core"), 0)
    got_1 = swap_pairs(send_1, ("y", "core"), 1)
    curvature = from_all(curvature, ("y", "core", "col"))

    new_solution, new_residual = pl.pallas_call(
        update_kernel,
        out_shape=(shape(count, dofs, cases),) * 2,
        in_specs=[SMEM] + [VMEM] * 10,
        out_specs=(HBM,) * 2,
        scratch_shapes=[
            pltpu.VMEM(residual.shape, F32),
            pltpu.VMEM(residual.shape, F32),
            pltpu.VMEM((17, dofs, cases), F32),
            pltpu.SMEM((17,), jnp.int32),
            pltpu.SemaphoreType.DMA((4,)),
            pltpu.SemaphoreType.DMA((4,)),
        ],
        compiler_params=kernel_params(16),
        name="update",
    )(
        faces, current, residual, direction_held, image, got_2, got_3, got_0, got_1, curvature, precond_dot
    )
    return (new_solution[None, None], new_residual[None, None], direction[None, None])


def solution(mesh):
    rows, cols = mesh.devices.shape
    mesh = jax.sharding.Mesh(mesh.devices.reshape(rows // 2, 2, cols), ("y", "core", "col"))
    split = lambda dims: P(("y", "core"), "col", *(None,) * dims)
    placed = (
        split(3), split(3), split(3), P(), split(2), split(1), split(2), split(4), split(4), split(2), split(1),
        P("col", None),
    )
    return jax.shard_map(
        per_device,
        mesh=mesh,
        in_specs=placed,
        out_specs=(split(3), split(3), split(3)),
        check_vma=False,
    )
```

```python
import jax
import jax.numpy as jnp
from jax import lax
from jax.experimental import pallas as pl
from jax.experimental.pallas import tpu as pltpu
from jax.sharding import PartitionSpec as P

F32 = jnp.float32
BF16 = jnp.bfloat16
SLOTS = 4
HEAD = 10
SMEM = pl.BlockSpec(memory_space=pltpu.SMEM)
VMEM = pl.BlockSpec(memory_space=pltpu.VMEM)
HBM = pl.BlockSpec(memory_space=pltpu.HBM)
ANY = pl.BlockSpec(memory_space=pl.ANY)


def halves(x):
    high = x.astype(BF16)
    return high, (x - high.astype(F32)).astype(BF16)


def dot(a, b):
    return jnp.dot(a, b, preferred_element_type=F32)


def dot_first(a, b):
    return lax.dot_general(a, b, (((0,), (0,)), ((), ())), preferred_element_type=F32)


def fold(x):
    width = x.shape[1] // 2
    return x[:, :width] + x[:, width:]


def product(matrix, pair):
    high, low = halves(matrix)
    return fold(dot(high, pair)) + dot(low, pair[:, : pair.shape[1] // 2])


def exact_pair(x):
    return jnp.concatenate(halves(x), axis=1)


def halved_rows(row_blocks):
    matrix = jnp.concatenate([row_blocks[k] for k in range(3)], axis=1)
    return jnp.concatenate(halves(matrix), axis=0)


def row_product(stacked, pattern, b, pairs):
    field = jnp.concatenate([pairs[pattern[k, 0, b]] for k in range(3)], axis=0)
    both = fold(dot(stacked, field))
    return both[:128] + both[128:]


def partial_rows(x):
    rows, cols = x.shape
    return jnp.sum(x.reshape(rows // 8, 8, cols), axis=0)


def weight_of(multiplicity, b):
    return 1.0 / jnp.full((1, 128), multiplicity[b].astype(F32))


def mapped(primal_map, shape, dim):
    place = lax.broadcasted_iota(jnp.int32, shape, dim)
    found = jnp.zeros(shape, jnp.int32)
    for p in range(8):
        found = jnp.where(place == p, primal_map[p], found)
    return found


def row_index():
    return 2 * lax.axis_index("y") + lax.axis_index("core")


def partner_faces():
    row, col = lax.axis_index("core"), lax.axis_index("col") % 2
    return 1 - row, row, 3 - col, 2 + col


def slots_by_block(faces, slot):
    for b in range(17):
        slot[b] = 16
    for s, f in enumerate(partner_faces()):
        for k in range(SLOTS):
            slot[faces[f, k]] = s * SLOTS + k


def local_kernel(
    faces_hbm, multiplicity_hbm, pattern_hbm, primal_map_hbm, residual_hbm, neumann_hbm, basis_hbm, inverse_hbm,
    local, send_2, told, send_3, send_0, send_1,
    faces, multiplicity, pattern, primal_map, residual, neumann, basis, inverse, pairs,
    index_sems, residual_sems, neumann_sems, basis_sems,
):
    count = residual.shape[0]
    index_copies = [
        pltpu.make_async_copy(source, target, index_sems.at[i])
        for i, (source, target) in enumerate(
            ((multiplicity_hbm, multiplicity), (pattern_hbm, pattern), (primal_map_hbm, primal_map), (faces_hbm, faces))
        )
    ]
    basis_copy = pltpu.make_async_copy(basis_hbm, basis, basis_sems.at[0])
    inverse_copy = pltpu.make_async_copy(inverse_hbm, inverse, basis_sems.at[1])
    copies = []
    for c in range(2):
        part = pl.ds(c * count // 2, count // 2)
        copies.append(pltpu.make_async_copy(residual_hbm.at[part], residual.at[part], residual_sems.at[c]))
    for c in range(4):
        part = pl.ds(c * count // 4, count // 4)
        copies.append(pltpu.make_async_copy(neumann_hbm.at[part], neumann.at[part], neumann_sems.at[c]))
    for copy in (*index_copies, *copies, basis_copy, inverse_copy):
        copy.start()
    for copy in index_copies:
        copy.wait()
    for b in range(count):
        if b % (count // 2) == 0:
            copies[b // (count // 2)].wait()
        pairs[b] = exact_pair(residual[b] * weight_of(multiplicity, b))
    total = jnp.zeros((8, 128), F32)
    for b in range(count):
        if b % (count // 4) == 0:
            copies[2 + b // (count // 4)].wait()
        weight = weight_of(multiplicity, b)
        out = row_product(halved_rows(neumann.at[b]), pattern, b, pairs) * weight
        local[b] = out
        total += partial_rows(residual[b] * out)
    basis_copy.wait()
    map_rows = mapped(primal_map, (8, 128), 0).astype(F32)
    for f, sent in zip(partner_faces(), (send_0, send_1, send_2, send_3)):
        for k in range(SLOTS):
            b = jnp.minimum(faces[f, k], count - 1)
            sent[k * 128 : (k + 1) * 128, :] = local[b]
            lanes = pl.ds(pl.multiple_of(b * 128, 128), 128)
            sent[512 + 8 * k : 520 + 8 * k, :] = basis[:, lanes] * weight_of(multiplicity, b)
        sent[544:552, :] = map_rows
    field = pairs[...].reshape(count * 128, 256)
    row = lax.broadcasted_iota(jnp.int32, (8, 128), 0)
    total = jnp.sum(total, axis=0, keepdims=True)
    map_row = mapped(primal_map, (8, 128), 1).astype(F32)
    inverse_copy.wait()
    sharers = inverse.shape[0] // 8
    mine = row_index() % sharers
    share = inverse[pl.ds(pl.multiple_of(mine * 8, 8), 8), :]
    rows = [product(basis[...], field), jnp.where(row == 0, total, map_row)[:2]]
    rows = jnp.concatenate(rows + [share[:, i : i + 128] for i in range(0, inverse.shape[1], 128)], axis=0)
    each = rows.shape[0]
    for i in range(told.shape[0] // each):
        told[each * i : each * i + each, :] = rows


def back(basis, own):
    bh, bl = (h.astype(F32) for h in halves(basis))
    oh, ol = (h.astype(F32) for h in halves(own))
    left = jnp.concatenate([bh, bl, bh, bl], axis=0).astype(BF16)
    right = jnp.concatenate([oh, oh, ol, ol], axis=0).astype(BF16)
    return dot_first(left, right)


def halving_kernel(schur_hbm, stacked, schur, sems):
    count = schur.shape[0]
    copies = []
    for c in range(4):
        part = pl.ds(c * count // 4, count // 4)
        copies.append(pltpu.make_async_copy(schur_hbm.at[part], schur.at[part], sems.at[c]))
        copies[c].start()
    for b in range(count):
        if b % (count // 4) == 0:
            copies[b // (count // 4)].wait()
        stacked[b] = halved_rows(schur.at[b])


def coarse_kernel(
    multiplicity, primal_map, local, same_core, other_core, basis, prev_dot, previous_hbm,
    started, wanted, precond_dot, inverse, previous, previous_sem,
):
    count = local.shape[0]
    previous_copy = pltpu.make_async_copy(previous_hbm, previous, previous_sem)
    previous_copy.start()

    order = inverse.shape[1]
    each = HEAD + 8 * (order // 128)
    half = same_core.shape[0] // each
    cols = lax.axis_size("col")
    sharers = order // cols // 8
    for told, core in ((same_core, lax.axis_index("core")), (other_core, 1 - lax.axis_index("core"))):
        for i in range(half):
            target = pl.multiple_of((i % cols * sharers + (2 * (i // cols) + core) % sharers) * 8, 8)
            for j in range(order // 128):
                source = i * each + HEAD + 8 * j
                inverse[pl.ds(target, 8), 128 * j : 128 * j + 128] = told[source : source + 8, :]

    def row_of_all(p):
        return jnp.concatenate([x[pl.ds(p, half, stride=each), :] for x in (same_core, other_core)], axis=0)

    maps = row_of_all(9).astype(jnp.int32)
    lane = lax.broadcasted_iota(jnp.int32, (2 * half, order), 1)
    chosen = [(maps[:, p : p + 1] == lane).astype(F32) for p in range(8)]
    chosen = jnp.concatenate(chosen, axis=0).astype(BF16)
    rows = jnp.concatenate([row_of_all(p) for p in range(8)], axis=0)
    rhs = fold(dot_first(chosen, exact_pair(rows)))
    coarse = product(inverse[...], exact_pair(rhs))
    dots = jnp.sum(row_of_all(8), axis=0, keepdims=True)
    dots = dots + jnp.sum(rhs * coarse, axis=0, keepdims=True)
    precond_dot[...] = dots
    beta = dots / prev_dot[...]
    wanted[...] = coarse

    lane = lax.broadcasted_iota(jnp.int32, (8, order), 1)
    own = (mapped(primal_map, (8, 128), 0)[:, 0:1] == lane).astype(F32).astype(BF16)
    own_back = back(basis[...], fold(dot(own, exact_pair(coarse))))
    previous_copy.wait()
    for b in range(count):
        mine = local[b] + own_back[b * 128 : (b + 1) * 128] * weight_of(multiplicity, b)
        started[b] = mine + beta * previous[b]
def direction_kernel(
    faces, pattern, started, coarse, got_2, got_3, got_0, got_1, stacked,
    direction_hbm, direction, image, send_2, send_3, send_0, send_1, curvature,
    added, pairs, slot, direction_sem,
):
    count = started.shape[0]
    order = coarse.shape[0]
    slots_by_block(faces, slot)
    received = (got_0, got_1, got_2, got_3)
    maps = jnp.concatenate([r[544:552, :] for r in received], axis=0).astype(jnp.int32)
    lane = lax.broadcasted_iota(jnp.int32, (32, order), 1)
    wanted = (maps[:, 0:1] == lane).astype(F32).astype(BF16)
    wanted = fold(dot(wanted, exact_pair(coarse[...])))
    for s, r in enumerate(received):
        face_basis = jnp.concatenate([r[512 + 8 * k : 520 + 8 * k, :] for k in range(SLOTS)], axis=1)
        face_back = back(face_basis, wanted[8 * s : 8 * s + 8])
        for k in range(SLOTS):
            part = slice(k * 128, (k + 1) * 128)
            added[s * SLOTS + k] = r[part, :] + face_back[part]
    added[16] = jnp.zeros((128, 128), F32)
    for b in range(count):
        value = started[b] + added[slot[b]]
        direction[b] = value
        pairs[b] = exact_pair(value)
    direction_copy = pltpu.make_async_copy(direction, direction_hbm, direction_sem)
    direction_copy.start()
    total = jnp.zeros((8, 128), F32)
    for b in range(count):
        out = row_product(stacked[b], pattern, b, pairs)
        image[b] = out
        total += partial_rows(direction[b] * out)
    for f, sent in zip(partner_faces(), (send_0, send_1, send_2, send_3)):
        for k in range(SLOTS):
            sent[k * 128 : (k + 1) * 128, :] = image[jnp.minimum(faces[f, k], count - 1)]
    curvature[...] = jnp.broadcast_to(jnp.sum(total, axis=0, keepdims=True), curvature.shape)
    direction_copy.wait()


def update_kernel(
    faces, current, residual, direction, image, got_2, got_3, got_0, got_1, curvature, precond_dot,
    new_solution_hbm, new_residual_hbm,
    new_solution, new_residual, added, slot, solution_sems, residual_sems,
):
    count = current.shape[0]
    slots_by_block(faces, slot)
    step = precond_dot[...] / jnp.sum(curvature[...], axis=0, keepdims=True)
    for s, r in enumerate((got_0, got_1, got_2, got_3)):
        for k in range(SLOTS):
            added[s * SLOTS + k] = r[k * 128 : (k + 1) * 128, :]
    added[16] = jnp.zeros((128, 128), F32)
    copies = []
    parts = solution_sems.shape[0]
    for c in range(parts):
        part = pl.ds(c * count // parts, count // parts)
        for b in range(c * count // parts, (c + 1) * count // parts):
            new_solution[b] = current[b] + step * direction[b]
            new_residual[b] = residual[b] - step * (image[b] + added[slot[b]])
        copies.append(pltpu.make_async_copy(new_solution.at[part], new_solution_hbm.at[part], solution_sems.at[c]))
        copies.append(pltpu.make_async_copy(new_residual.at[part], new_residual_hbm.at[part], residual_sems.at[c]))
        copies[-2].start()
        copies[-1].start()
    for copy in copies:
        copy.wait()


def swap_pairs(x, axis, first):
    pairs = [(i, i + 1) for i in range(first, lax.axis_size(axis) - 1, 2)]
    return lax.ppermute(x, axis, pairs + [(j, i) for i, j in pairs])


def from_all(x, axes):
    sent = x.reshape(lax.axis_size(axes), 1, -1)
    return lax.all_to_all(sent, axes, split_axis=0, concat_axis=0, tiled=True).reshape(x.shape)


def shape(*dims):
    return jax.ShapeDtypeStruct(dims, F32)


def held(*dims):
    return pltpu.VMEM(dims, F32)


def in_hbm(x):
    return pltpu.with_memory_space_constraint(x, pltpu.HBM)


def kernel_params(mib):
    return pltpu.CompilerParams(vmem_limit_bytes=mib << 20)


def per_device(
    solution,
    residual,
    prev_direction,
    prev_dot,
    face_lists,
    multiplicity,
    block_pattern,
    schur,
    neumann_inverse,
    coarse_basis,
    primal_map,
    coarse_inverse,
):
    current, residual, previous = solution[0, 0], residual[0, 0], prev_direction[0, 0]
    faces, multiplicity = face_lists[0, 0], multiplicity[0, 0]
    pattern = jnp.transpose(block_pattern, (0, 3, 1, 2))[0]
    schur, neumann = schur[0, 0], neumann_inverse[0, 0]
    basis, primal_map = coarse_basis[0, 0], primal_map[0, 0]
    count, dofs, cases = residual.shape

    everywhere = lax.axis_size(("y", "core", "col"))
    order = coarse_inverse.shape[1]
    told_rows = (HEAD + 8 * (order // cases)) * (everywhere // 2)

    face = held(SLOTS * dofs + 40, cases)
    indices = (faces, multiplicity, pattern, primal_map)
    local, send_2, told, send_3, send_0, send_1 = pl.pallas_call(
        local_kernel,
        out_shape=(held(count, dofs, cases), face, held(told_rows, cases), face, face, face),
        in_specs=[HBM] * 8,
        out_specs=(VMEM,) * 6,
        scratch_shapes=[pltpu.SMEM(x.shape, jnp.int32) for x in indices]
        + [
            pltpu.VMEM(residual.shape, F32),
            pltpu.VMEM(neumann.shape, F32),
            pltpu.VMEM(basis.shape, F32),
            pltpu.VMEM(coarse_inverse.shape, F32),
            pltpu.VMEM((count, dofs, 2 * cases), BF16),
            pltpu.SemaphoreType.DMA((4,)),
            pltpu.SemaphoreType.DMA((2,)),
            pltpu.SemaphoreType.DMA((4,)),
            pltpu.SemaphoreType.DMA((2,)),
        ],
        compiler_params=kernel_params(16),
        name="local_solve",
    )(*(in_hbm(x) for x in (*indices, residual, neumann, basis, coarse_inverse)))

    same_core = from_all(told, ("y", "col"))
    other_core = lax.ppermute(same_core, "core", [(0, 1), (1, 0)])
    got_2 = swap_pairs(send_2, "col", 0)
    got_3 = swap_pairs(send_3, "col", 1)
    got_0 = swap_pairs(send_0, ("y", "core"), 0)
    got_1 = swap_pairs(send_1, ("y", "core"), 1)

    stacked = pl.pallas_call(
        halving_kernel,
        out_shape=pltpu.VMEM((count, 2 * dofs, 3 * dofs), BF16),
        in_specs=[HBM],
        out_specs=VMEM,
        scratch_shapes=[pltpu.VMEM(schur.shape, F32), pltpu.SemaphoreType.DMA((4,))],
        compiler_params=kernel_params(12),
        name="halving",
    )(in_hbm(schur))

    started, coarse, precond_dot = pl.pallas_call(
        coarse_kernel,
        out_shape=(held(count, dofs, cases), held(order, cases), held(1, cases)),
        in_specs=[SMEM] * 2 + [VMEM] * 5 + [HBM],
        out_specs=(VMEM,) * 3,
        scratch_shapes=[
            pltpu.VMEM((order, order), F32),
            pltpu.VMEM(previous.shape, F32),
            pltpu.SemaphoreType.DMA,
        ],
        compiler_params=kernel_params(24),
        name="coarse_solve",
    )(
        multiplicity, primal_map, local, same_core, other_core, basis, prev_dot.reshape(1, cases),
        in_hbm(previous),
    )

    direction, direction_held, image, send_2, send_3, send_0, send_1, curvature = pl.pallas_call(
        direction_kernel,
        out_shape=(shape(count, dofs, cases), held(count, dofs, cases), held(count, dofs, cases))
        + (held(SLOTS * dofs, cases),) * 4
        + (held(everywhere, cases),),
        in_specs=[SMEM] * 2 + [VMEM] * 7,
        out_specs=(HBM,) + (VMEM,) * 7,
        scratch_shapes=[
            pltpu.VMEM((17, dofs, cases), F32),
            pltpu.VMEM((count, dofs, 2 * cases), BF16),
            pltpu.SMEM((17,), jnp.int32),
            pltpu.SemaphoreType.DMA,
        ],
        compiler_params=kernel_params(16),
        name="direction_image",
    )(faces, pattern, started, coarse, got_2, got_3, got_0, got_1, stacked)

    got_2 = swap_pairs(send_2, "col", 0)
    got_3 = swap_pairs(send_3, "col", 1)
    got_0 = swap_pairs(send_0, ("y", "core"), 0)
    got_1 = swap_pairs(send_1, ("y", "core"), 1)
    curvature = from_all(curvature, ("y", "core", "col"))

    new_solution, new_residual = pl.pallas_call(
        update_kernel,
        out_shape=(shape(count, dofs, cases),) * 2,
        in_specs=[SMEM] + [VMEM] * 10,
        out_specs=(HBM,) * 2,
        scratch_shapes=[
            pltpu.VMEM(residual.shape, F32),
            pltpu.VMEM(residual.shape, F32),
            pltpu.VMEM((17, dofs, cases), F32),
            pltpu.SMEM((17,), jnp.int32),
            pltpu.SemaphoreType.DMA((8,)),
            pltpu.SemaphoreType.DMA((8,)),
        ],
        compiler_params=kernel_params(16),
        name="update",
    )(
        faces, current, residual, direction_held, image, got_2, got_3, got_0, got_1, curvature, precond_dot
    )
    return (new_solution[None, None], new_residual[None, None], direction[None, None])


def solution(mesh):
    rows, cols = mesh.devices.shape
    mesh = jax.sharding.Mesh(mesh.devices.reshape(rows // 2, 2, cols), ("y", "core", "col"))
    split = lambda dims: P(("y", "core"), "col", *(None,) * dims)
    placed = (
        split(3), split(3), split(3), P(), split(2), split(1), split(2), split(4), split(4), split(2), split(1),
        P("col", None),
    )
    return jax.shard_map(
        per_device,
        mesh=mesh,
        in_specs=placed,
        out_specs=(split(3), split(3), split(3)),
        check_vma=False,
    )
```

```python
import jax
import jax.numpy as jnp
from jax import lax
from jax.experimental import pallas as pl
from jax.experimental.pallas import tpu as pltpu
from jax.sharding import PartitionSpec as P

F32 = jnp.float32
BF16 = jnp.bfloat16
SLOTS = 4
HEAD = 10
SMEM = pl.BlockSpec(memory_space=pltpu.SMEM)
VMEM = pl.BlockSpec(memory_space=pltpu.VMEM)
HBM = pl.BlockSpec(memory_space=pltpu.HBM)
ANY = pl.BlockSpec(memory_space=pl.ANY)


def halves(x):
    high = x.astype(BF16)
    return high, (x - high.astype(F32)).astype(BF16)


def dot(a, b):
    return jnp.dot(a, b, preferred_element_type=F32)


def dot_first(a, b):
    return lax.dot_general(a, b, (((0,), (0,)), ((), ())), preferred_element_type=F32)


def fold(x):
    width = x.shape[1] // 2
    return x[:, :width] + x[:, width:]


def product(matrix, pair):
    high, low = halves(matrix)
    return fold(dot(high, pair)) + dot(low, pair[:, : pair.shape[1] // 2])


def exact_pair(x):
    return jnp.concatenate(halves(x), axis=1)


def halved_rows(row_blocks):
    matrix = jnp.concatenate([row_blocks[k] for k in range(3)], axis=1)
    return jnp.concatenate(halves(matrix), axis=0)


def row_product(stacked, pattern, b, pairs):
    field = jnp.concatenate([pairs[pattern[k, 0, b]] for k in range(3)], axis=0)
    both = fold(dot(stacked, field))
    return both[:128] + both[128:]


def partial_rows(x):
    rows, cols = x.shape
    return jnp.sum(x.reshape(rows // 8, 8, cols), axis=0)


def weight_of(multiplicity, b):
    return 1.0 / jnp.full((1, 128), multiplicity[b].astype(F32))


def mapped(primal_map, shape, dim):
    place = lax.broadcasted_iota(jnp.int32, shape, dim)
    found = jnp.zeros(shape, jnp.int32)
    for p in range(8):
        found = jnp.where(place == p, primal_map[p], found)
    return found


def row_index():
    return 2 * lax.axis_index("y") + lax.axis_index("core")


def partner_faces():
    row, col = lax.axis_index("core"), lax.axis_index("col") % 2
    return 1 - row, row, 3 - col, 2 + col


def slots_by_block(faces, slot):
    for b in range(17):
        slot[b] = 16
    for s, f in enumerate(partner_faces()):
        for k in range(SLOTS):
            slot[faces[f, k]] = s * SLOTS + k


def local_kernel(
    faces_hbm, multiplicity_hbm, pattern_hbm, primal_map_hbm, residual_hbm, neumann_hbm, basis_hbm, inverse_hbm,
    local, send_2, told, send_3, send_0, send_1,
    faces, multiplicity, pattern, primal_map, residual, neumann, basis, inverse, pairs,
    index_sems, residual_sems, neumann_sems, basis_sems,
):
    count = residual.shape[0]
    index_copies = [
        pltpu.make_async_copy(source, target, index_sems.at[i])
        for i, (source, target) in enumerate(
            ((multiplicity_hbm, multiplicity), (pattern_hbm, pattern), (primal_map_hbm, primal_map), (faces_hbm, faces))
        )
    ]
    basis_copy = pltpu.make_async_copy(basis_hbm, basis, basis_sems.at[0])
    inverse_copy = pltpu.make_async_copy(inverse_hbm, inverse, basis_sems.at[1])
    copies = []
    for c in range(2):
        part = pl.ds(c * count // 2, count // 2)
        copies.append(pltpu.make_async_copy(residual_hbm.at[part], residual.at[part], residual_sems.at[c]))
    for c in range(4):
        part = pl.ds(c * count // 4, count // 4)
        copies.append(pltpu.make_async_copy(neumann_hbm.at[part], neumann.at[part], neumann_sems.at[c]))
    for copy in (*index_copies, *copies, basis_copy, inverse_copy):
        copy.start()
    for copy in index_copies:
        copy.wait()
    for b in range(count):
        if b % (count // 2) == 0:
            copies[b // (count // 2)].wait()
        pairs[b] = exact_pair(residual[b] * weight_of(multiplicity, b))
    total = jnp.zeros((8, 128), F32)
    for b in range(count):
        if b % (count // 4) == 0:
            copies[2 + b // (count // 4)].wait()
        weight = weight_of(multiplicity, b)
        out = row_product(halved_rows(neumann.at[b]), pattern, b, pairs) * weight
        local[b] = out
        total += partial_rows(residual[b] * out)
    basis_copy.wait()
    for f, sent in zip(partner_faces(), (send_0, send_1, send_2, send_3)):
        for k in range(SLOTS):
            b = jnp.minimum(faces[f, k], count - 1)
            sent[k * 128 : (k + 1) * 128, :] = local[b]
            lanes = pl.ds(pl.multiple_of(b * 128, 128), 128)
            sent[512 + 8 * k : 520 + 8 * k, :] = basis[:, lanes] * weight_of(multiplicity, b)
    field = pairs[...].reshape(count * 128, 256)
    row = lax.broadcasted_iota(jnp.int32, (8, 128), 0)
    total = jnp.sum(total, axis=0, keepdims=True)
    map_row = mapped(primal_map, (8, 128), 1).astype(F32)
    inverse_copy.wait()
    sharers = inverse.shape[0] // 8
    mine = row_index() % sharers
    share = inverse[pl.ds(pl.multiple_of(mine * 8, 8), 8), :]
    rows = [product(basis[...], field), jnp.where(row == 0, total, map_row)[:2]]
    rows = jnp.concatenate(rows + [share[:, i : i + 128] for i in range(0, inverse.shape[1], 128)], axis=0)
    each = rows.shape[0]
    for i in range(told.shape[0] // each):
        told[each * i : each * i + each, :] = rows


def back(basis, own):
    bh, bl = (h.astype(F32) for h in halves(basis))
    oh, ol = (h.astype(F32) for h in halves(own))
    left = jnp.concatenate([bh, bl, bh, bl], axis=0).astype(BF16)
    right = jnp.concatenate([oh, oh, ol, ol], axis=0).astype(BF16)
    return dot_first(left, right)


def halving_kernel(schur_hbm, stacked, schur, sems):
    count = schur.shape[0]
    copies = []
    for c in range(4):
        part = pl.ds(c * count // 4, count // 4)
        copies.append(pltpu.make_async_copy(schur_hbm.at[part], schur.at[part], sems.at[c]))
        copies[c].start()
    for b in range(count):
        if b % (count // 4) == 0:
            copies[b // (count // 4)].wait()
        stacked[b] = halved_rows(schur.at[b])


def coarse_kernel(
    multiplicity, primal_map, local, same_core, other_core, basis, prev_dot, previous_hbm,
    started, wanted, precond_dot, inverse, previous, previous_sem,
):
    count = local.shape[0]
    previous_copy = pltpu.make_async_copy(previous_hbm, previous, previous_sem)
    previous_copy.start()

    order = inverse.shape[1]
    each = HEAD + 8 * (order // 128)
    half = same_core.shape[0] // each
    cols = lax.axis_size("col")
    sharers = order // cols // 8
    for told, core in ((same_core, lax.axis_index("core")), (other_core, 1 - lax.axis_index("core"))):
        for i in range(half):
            target = pl.multiple_of((i % cols * sharers + (2 * (i // cols) + core) % sharers) * 8, 8)
            for j in range(order // 128):
                source = i * each + HEAD + 8 * j
                inverse[pl.ds(target, 8), 128 * j : 128 * j + 128] = told[source : source + 8, :]

    def row_of_all(p):
        return jnp.concatenate([x[pl.ds(p, half, stride=each), :] for x in (same_core, other_core)], axis=0)

    maps = row_of_all(9).astype(jnp.int32)
    lane = lax.broadcasted_iota(jnp.int32, (2 * half, order), 1)
    chosen = [(maps[:, p : p + 1] == lane).astype(F32) for p in range(8)]
    chosen = jnp.concatenate(chosen, axis=0).astype(BF16)
    rows = jnp.concatenate([row_of_all(p) for p in range(8)], axis=0)
    rhs = fold(dot_first(chosen, exact_pair(rows)))
    coarse = product(inverse[...], exact_pair(rhs))
    dots = jnp.sum(row_of_all(8), axis=0, keepdims=True)
    dots = dots + jnp.sum(rhs * coarse, axis=0, keepdims=True)
    precond_dot[...] = dots
    beta = dots / prev_dot[...]
    y, core, col = (lax.axis_index(name) for name in ("y", "core", "col"))
    odd = col % 2
    partners = (
        (other_core, y * cols + col),
        (other_core, jnp.clip(y + 2 * core - 1, 0, lax.axis_size("y") - 1) * cols + col),
        (same_core, y * cols + (col + 1 - 2 * odd)),
        (same_core, y * cols + jnp.clip(col + 2 * odd - 1, 0, cols - 1)),
    )
    map_rows = [x[pl.ds(i * each + 9, 1), :] for x, i in partners]
    map_rows = jnp.concatenate([jnp.broadcast_to(row, (8, 128)) for row in map_rows], axis=0)
    on_diagonal = lax.broadcasted_iota(jnp.int32, (32, 128), 0) % 8 == lax.broadcasted_iota(jnp.int32, (32, 128), 1)
    maps = jnp.sum(jnp.where(on_diagonal, map_rows, 0.0), axis=1, keepdims=True).astype(jnp.int32)
    maps = jnp.concatenate([mapped(primal_map, (8, 128), 0)[:, 0:1], maps], axis=0)
    lane = lax.broadcasted_iota(jnp.int32, (40, order), 1)
    picked = fold(dot((maps == lane).astype(F32).astype(BF16), exact_pair(coarse)))
    wanted[...] = picked[8:40]
    own_back = back(basis[...], picked[0:8])
    previous_copy.wait()
    for b in range(count):
        mine = local[b] + own_back[b * 128 : (b + 1) * 128] * weight_of(multiplicity, b)
        started[b] = mine + beta * previous[b]
def direction_kernel(
    faces, pattern, started, wanted, got_2, got_3, got_0, got_1, stacked,
    direction_hbm, direction, image, send_2, send_3, send_0, send_1, curvature,
    added, pairs, slot, direction_sem,
):
    count = started.shape[0]
    slots_by_block(faces, slot)
    for s, r in enumerate((got_0, got_1, got_2, got_3)):
        face_basis = jnp.concatenate([r[512 + 8 * k : 520 + 8 * k, :] for k in range(SLOTS)], axis=1)
        face_back = back(face_basis, wanted[8 * s : 8 * s + 8, :])
        for k in range(SLOTS):
            part = slice(k * 128, (k + 1) * 128)
            added[s * SLOTS + k] = r[part, :] + face_back[part]
    added[16] = jnp.zeros((128, 128), F32)
    for b in range(count):
        value = started[b] + added[slot[b]]
        direction[b] = value
        pairs[b] = exact_pair(value)
    direction_copy = pltpu.make_async_copy(direction, direction_hbm, direction_sem)
    direction_copy.start()
    total = jnp.zeros((8, 128), F32)
    for b in range(count):
        out = row_product(stacked[b], pattern, b, pairs)
        image[b] = out
        total += partial_rows(direction[b] * out)
    for f, sent in zip(partner_faces(), (send_0, send_1, send_2, send_3)):
        for k in range(SLOTS):
            sent[k * 128 : (k + 1) * 128, :] = image[jnp.minimum(faces[f, k], count - 1)]
    curvature[...] = jnp.broadcast_to(jnp.sum(total, axis=0, keepdims=True), curvature.shape)
    direction_copy.wait()


def update_kernel(
    faces, current, residual, direction, image, got_2, got_3, got_0, got_1, curvature, precond_dot,
    new_solution_hbm, new_residual_hbm,
    new_solution, new_residual, added, slot, solution_sems, residual_sems,
):
    count = current.shape[0]
    slots_by_block(faces, slot)
    step = precond_dot[...] / jnp.sum(curvature[...], axis=0, keepdims=True)
    copies = []

    def leave(c, value, value_hbm, sems):
        part = pl.ds(c * count // 4, count // 4)
        copies.append(pltpu.make_async_copy(value.at[part], value_hbm.at[part], sems.at[c]))
        copies[-1].start()

    for b in range(count):
        new_solution[b] = current[b] + step * direction[b]
        if (b + 1) % (count // 4) == 0:
            leave(b // (count // 4), new_solution, new_solution_hbm, solution_sems)
    for s, r in enumerate((got_0, got_1, got_2, got_3)):
        for k in range(SLOTS):
            added[s * SLOTS + k] = r[k * 128 : (k + 1) * 128, :]
    added[16] = jnp.zeros((128, 128), F32)
    for b in range(count):
        new_residual[b] = residual[b] - step * (image[b] + added[slot[b]])
        if (b + 1) % (count // 4) == 0:
            leave(b // (count // 4), new_residual, new_residual_hbm, residual_sems)
    for copy in copies:
        copy.wait()


def swap_pairs(x, axis, first):
    pairs = [(i, i + 1) for i in range(first, lax.axis_size(axis) - 1, 2)]
    return lax.ppermute(x, axis, pairs + [(j, i) for i, j in pairs])


def pass_kernel(*refs):
    pass


def passed(*arrays):
    return pl.pallas_call(
        pass_kernel,
        out_shape=[held(*x.shape) for x in arrays],
        in_specs=[ANY] * len(arrays),
        out_specs=[ANY] * len(arrays),
        input_output_aliases={i: i for i in range(len(arrays))},
        compiler_params=kernel_params(4),
        name="passed",
    )(*arrays)


def from_all(x, axes):
    sent = x.reshape(lax.axis_size(axes), 1, -1)
    return lax.all_to_all(sent, axes, split_axis=0, concat_axis=0, tiled=True).reshape(x.shape)


def shape(*dims):
    return jax.ShapeDtypeStruct(dims, F32)


def held(*dims):
    return pltpu.VMEM(dims, F32)


def in_hbm(x):
    return pltpu.with_memory_space_constraint(x, pltpu.HBM)


def kernel_params(mib):
    return pltpu.CompilerParams(vmem_limit_bytes=mib << 20)


def per_device(
    solution,
    residual,
    prev_direction,
    prev_dot,
    face_lists,
    multiplicity,
    block_pattern,
    schur,
    neumann_inverse,
    coarse_basis,
    primal_map,
    coarse_inverse,
):
    current, residual, previous = solution[0, 0], residual[0, 0], prev_direction[0, 0]
    faces, multiplicity = face_lists[0, 0], multiplicity[0, 0]
    pattern = jnp.transpose(block_pattern, (0, 3, 1, 2))[0]
    schur, neumann = schur[0, 0], neumann_inverse[0, 0]
    basis, primal_map = coarse_basis[0, 0], primal_map[0, 0]
    count, dofs, cases = residual.shape

    everywhere = lax.axis_size(("y", "core", "col"))
    order = coarse_inverse.shape[1]
    told_rows = (HEAD + 8 * (order // cases)) * (everywhere // 2)

    face = held(SLOTS * dofs + 32, cases)
    indices = (faces, multiplicity, pattern, primal_map)
    local, send_2, told, send_3, send_0, send_1 = pl.pallas_call(
        local_kernel,
        out_shape=(held(count, dofs, cases), face, held(told_rows, cases), face, face, face),
        in_specs=[HBM] * 8,
        out_specs=(VMEM,) * 6,
        scratch_shapes=[pltpu.SMEM(x.shape, jnp.int32) for x in indices]
        + [
            pltpu.VMEM(residual.shape, F32),
            pltpu.VMEM(neumann.shape, F32),
            pltpu.VMEM(basis.shape, F32),
            pltpu.VMEM(coarse_inverse.shape, F32),
            pltpu.VMEM((count, dofs, 2 * cases), BF16),
            pltpu.SemaphoreType.DMA((4,)),
            pltpu.SemaphoreType.DMA((2,)),
            pltpu.SemaphoreType.DMA((4,)),
            pltpu.SemaphoreType.DMA((2,)),
        ],
        compiler_params=kernel_params(16),
        name="local_solve",
    )(*(in_hbm(x) for x in (*indices, residual, neumann, basis, coarse_inverse)))

    same_core = lax.cond(
        lax.axis_index("col") < lax.axis_size("col"), lambda x: from_all(x, ("y", "col")), lambda x: x, told
    )
    same_core, send_2, send_3, send_0, send_1 = passed(same_core, send_2, send_3, send_0, send_1)
    other_core = lax.ppermute(same_core, "core", [(0, 1), (1, 0)])
    got_2 = swap_pairs(send_2, "col", 0)
    got_3 = swap_pairs(send_3, "col", 1)
    got_0 = swap_pairs(send_0, ("y", "core"), 0)
    got_1 = swap_pairs(send_1, ("y", "core"), 1)

    stacked = pl.pallas_call(
        halving_kernel,
        out_shape=pltpu.VMEM((count, 2 * dofs, 3 * dofs), BF16),
        in_specs=[HBM],
        out_specs=VMEM,
        scratch_shapes=[pltpu.VMEM(schur.shape, F32), pltpu.SemaphoreType.DMA((4,))],
        compiler_params=kernel_params(12),
        name="halving",
    )(in_hbm(schur))

    started, wanted, precond_dot = pl.pallas_call(
        coarse_kernel,
        out_shape=(held(count, dofs, cases), held(32, cases), held(1, cases)),
        in_specs=[SMEM] * 2 + [VMEM] * 5 + [HBM],
        out_specs=(VMEM,) * 3,
        scratch_shapes=[
            pltpu.VMEM((order, order), F32),
            pltpu.VMEM(previous.shape, F32),
            pltpu.SemaphoreType.DMA,
        ],
        compiler_params=kernel_params(24),
        name="coarse_solve",
    )(
        multiplicity, primal_map, local, same_core, other_core, basis, prev_dot.reshape(1, cases),
        in_hbm(previous),
    )

    direction, direction_held, image, send_2, send_3, send_0, send_1, curvature = pl.pallas_call(
        direction_kernel,
        out_shape=(shape(count, dofs, cases), held(count, dofs, cases), held(count, dofs, cases))
        + (held(SLOTS * dofs, cases),) * 4
        + (held(everywhere, cases),),
        in_specs=[SMEM] * 2 + [VMEM] * 7,
        out_specs=(HBM,) + (VMEM,) * 7,
        scratch_shapes=[
            pltpu.VMEM((17, dofs, cases), F32),
            pltpu.VMEM((count, dofs, 2 * cases), BF16),
            pltpu.SMEM((17,), jnp.int32),
            pltpu.SemaphoreType.DMA,
        ],
        compiler_params=kernel_params(16),
        name="direction_image",
    )(faces, pattern, started, wanted, got_2, got_3, got_0, got_1, stacked)

    got_2 = swap_pairs(send_2, "col", 0)
    got_3 = swap_pairs(send_3, "col", 1)
    got_0 = swap_pairs(send_0, ("y", "core"), 0)
    got_1 = swap_pairs(send_1, ("y", "core"), 1)
    curvature = from_all(curvature, ("y", "core", "col"))

    new_solution, new_residual = pl.pallas_call(
        update_kernel,
        out_shape=(shape(count, dofs, cases),) * 2,
        in_specs=[SMEM] + [VMEM] * 10,
        out_specs=(HBM,) * 2,
        scratch_shapes=[
            pltpu.VMEM(residual.shape, F32),
            pltpu.VMEM(residual.shape, F32),
            pltpu.VMEM((17, dofs, cases), F32),
            pltpu.SMEM((17,), jnp.int32),
            pltpu.SemaphoreType.DMA((4,)),
            pltpu.SemaphoreType.DMA((4,)),
        ],
        compiler_params=kernel_params(16),
        name="update",
    )(
        faces, current, residual, direction_held, image, got_2, got_3, got_0, got_1, curvature, precond_dot
    )
    return (new_solution[None, None], new_residual[None, None], direction[None, None])


def solution(mesh):
    rows, cols = mesh.devices.shape
    mesh = jax.sharding.Mesh(mesh.devices.reshape(rows // 2, 2, cols), ("y", "core", "col"))
    split = lambda dims: P(("y", "core"), "col", *(None,) * dims)
    placed = (
        split(3), split(3), split(3), P(), split(2), split(1), split(2), split(4), split(4), split(2), split(1),
        P("col", None),
    )
    return jax.shard_map(
        per_device,
        mesh=mesh,
        in_specs=placed,
        out_specs=(split(3), split(3), split(3)),
        check_vma=False,
    )
```

```python
import jax
import jax.numpy as jnp
from jax import lax
from jax.experimental import pallas as pl
from jax.experimental.pallas import tpu as pltpu
from jax.sharding import PartitionSpec as P

F32 = jnp.float32
BF16 = jnp.bfloat16
SLOTS = 4
HEAD = 10
SMEM = pl.BlockSpec(memory_space=pltpu.SMEM)
VMEM = pl.BlockSpec(memory_space=pltpu.VMEM)
HBM = pl.BlockSpec(memory_space=pltpu.HBM)


def halves(x):
    high = x.astype(BF16)
    return high, (x - high.astype(F32)).astype(BF16)


def dot(a, b):
    return jnp.dot(a, b, preferred_element_type=F32)


def dot_first(a, b):
    return lax.dot_general(a, b, (((0,), (0,)), ((), ())), preferred_element_type=F32)


def fold(x):
    width = x.shape[1] // 2
    return x[:, :width] + x[:, width:]


def product(matrix, pair):
    high, low = halves(matrix)
    return fold(dot(high, pair)) + dot(low, pair[:, : pair.shape[1] // 2])


def exact_pair(x):
    return jnp.concatenate(halves(x), axis=1)


def halved_rows(row_blocks):
    matrix = jnp.concatenate([row_blocks[k] for k in range(3)], axis=1)
    return jnp.concatenate(halves(matrix), axis=0)


def row_product(stacked, pattern, b, pairs):
    field = jnp.concatenate([pairs[pattern[k, 0, b]] for k in range(3)], axis=0)
    both = fold(dot(stacked, field))
    return both[:128] + both[128:]


def partial_rows(x):
    rows, cols = x.shape
    return jnp.sum(x.reshape(rows // 8, 8, cols), axis=0)


def weight_of(multiplicity, b):
    return 1.0 / jnp.full((1, 128), multiplicity[b].astype(F32))


def mapped(primal_map, shape, dim):
    place = lax.broadcasted_iota(jnp.int32, shape, dim)
    found = jnp.zeros(shape, jnp.int32)
    for p in range(8):
        found = jnp.where(place == p, primal_map[p], found)
    return found


def row_index():
    return 2 * lax.axis_index("y") + lax.axis_index("core")


def partner_faces():
    row, col = lax.axis_index("core"), lax.axis_index("col") % 2
    return 1 - row, row, 3 - col, 2 + col


def slots_by_block(faces, slot):
    for b in range(17):
        slot[b] = 16
    for s, f in enumerate(partner_faces()):
        for k in range(SLOTS):
            slot[faces[f, k]] = s * SLOTS + k


def local_kernel(
    faces_hbm, multiplicity_hbm, pattern_hbm, primal_map_hbm, residual_hbm, neumann_hbm, basis_hbm, inverse_hbm,
    local, send_2, told_hbm, send_3, send_0, send_1,
    faces, multiplicity, pattern, primal_map, residual, neumann, basis, inverse, pairs, told,
    index_sems, residual_sems, neumann_sems, basis_sems, told_sem,
):
    count = residual.shape[0]
    index_copies = [
        pltpu.make_async_copy(source, target, index_sems.at[i])
        for i, (source, target) in enumerate(
            ((multiplicity_hbm, multiplicity), (pattern_hbm, pattern), (primal_map_hbm, primal_map), (faces_hbm, faces))
        )
    ]
    basis_copy = pltpu.make_async_copy(basis_hbm, basis, basis_sems.at[0])
    inverse_copy = pltpu.make_async_copy(inverse_hbm, inverse, basis_sems.at[1])
    copies = []
    for c in range(2):
        part = pl.ds(c * count // 2, count // 2)
        copies.append(pltpu.make_async_copy(residual_hbm.at[part], residual.at[part], residual_sems.at[c]))
    for c in range(4):
        part = pl.ds(c * count // 4, count // 4)
        copies.append(pltpu.make_async_copy(neumann_hbm.at[part], neumann.at[part], neumann_sems.at[c]))
    for copy in (*index_copies, *copies[:2], basis_copy, *copies[2:], inverse_copy):
        copy.start()
    for copy in index_copies:
        copy.wait()
    for b in range(count):
        if b % (count // 2) == 0:
            copies[b // (count // 2)].wait()
        pairs[b] = exact_pair(residual[b] * weight_of(multiplicity, b))
    basis_copy.wait()
    coarse_local = product(basis[...], pairs[...].reshape(count * 128, 256))
    total = jnp.zeros((8, 128), F32)
    for b in range(count):
        if b % (count // 4) == 0:
            copies[2 + b // (count // 4)].wait()
        weight = weight_of(multiplicity, b)
        out = row_product(halved_rows(neumann.at[b]), pattern, b, pairs) * weight
        local[b] = out
        total += partial_rows(residual[b] * out)
    row = lax.broadcasted_iota(jnp.int32, (8, 128), 0)
    total = jnp.sum(total, axis=0, keepdims=True)
    map_row = mapped(primal_map, (8, 128), 1).astype(F32)
    inverse_copy.wait()
    sharers = inverse.shape[0] // 8
    mine = row_index() % sharers
    share = inverse[pl.ds(pl.multiple_of(mine * 8, 8), 8), :]
    rows = [coarse_local, jnp.where(row == 0, total, map_row)[:2]]
    rows = jnp.concatenate(rows + [share[:, i : i + 128] for i in range(0, inverse.shape[1], 128)], axis=0)
    each = rows.shape[0]
    for i in range(told.shape[0] // each):
        told[each * i : each * i + each, :] = rows
    told_copy = pltpu.make_async_copy(told, told_hbm, told_sem)
    told_copy.start()
    for f, sent in zip(partner_faces(), (send_0, send_1, send_2, send_3)):
        for k in range(SLOTS):
            b = jnp.minimum(faces[f, k], count - 1)
            sent[k * 128 : (k + 1) * 128, :] = local[b]
            lanes = pl.ds(pl.multiple_of(b * 128, 128), 128)
            sent[512 + 8 * k : 520 + 8 * k, :] = basis[:, lanes] * weight_of(multiplicity, b)
    told_copy.wait()


def back(basis, own):
    bh, bl = (h.astype(F32) for h in halves(basis))
    oh, ol = (h.astype(F32) for h in halves(own))
    left = jnp.concatenate([bh, bl, bh, bl], axis=0).astype(BF16)
    right = jnp.concatenate([oh, oh, ol, ol], axis=0).astype(BF16)
    return dot_first(left, right)


def halving_kernel(schur_hbm, stacked, schur, sems):
    count = schur.shape[0]
    copies = []
    for c in range(4):
        part = pl.ds(c * count // 4, count // 4)
        copies.append(pltpu.make_async_copy(schur_hbm.at[part], schur.at[part], sems.at[c]))
        copies[c].start()
    for b in range(count):
        if b % (count // 4) == 0:
            copies[b // (count // 4)].wait()
        stacked[b] = halved_rows(schur.at[b])


def coarse_kernel(
    multiplicity, primal_map, local, same_core, other_core, basis, prev_dot, previous_hbm,
    started, wanted, precond_dot, inverse, previous, previous_sem,
):
    count = local.shape[0]
    previous_copy = pltpu.make_async_copy(previous_hbm, previous, previous_sem)
    previous_copy.start()

    order = inverse.shape[1]
    each = HEAD + 8 * (order // 128)
    half = same_core.shape[0] // each
    cols = lax.axis_size("col")
    sharers = order // cols // 8
    for told, core in ((same_core, lax.axis_index("core")), (other_core, 1 - lax.axis_index("core"))):
        for i in range(half):
            target = pl.multiple_of((i % cols * sharers + (2 * (i // cols) + core) % sharers) * 8, 8)
            for j in range(order // 128):
                source = i * each + HEAD + 8 * j
                inverse[pl.ds(target, 8), 128 * j : 128 * j + 128] = told[source : source + 8, :]

    def row_of_all(p):
        return jnp.concatenate([x[pl.ds(p, half, stride=each), :] for x in (same_core, other_core)], axis=0)

    maps = row_of_all(9).astype(jnp.int32)
    lane = lax.broadcasted_iota(jnp.int32, (2 * half, order), 1)
    chosen = [(maps[:, p : p + 1] == lane).astype(F32) for p in range(8)]
    chosen = jnp.concatenate(chosen, axis=0).astype(BF16)
    rows = jnp.concatenate([row_of_all(p) for p in range(8)], axis=0)
    rhs = fold(dot_first(chosen, exact_pair(rows)))
    coarse = product(inverse[...], exact_pair(rhs))
    dots = jnp.sum(row_of_all(8), axis=0, keepdims=True)
    dots = dots + jnp.sum(rhs * coarse, axis=0, keepdims=True)
    precond_dot[...] = dots
    beta = dots / prev_dot[...]
    y, core, col = (lax.axis_index(name) for name in ("y", "core", "col"))
    odd = col % 2
    partners = (
        (other_core, y * cols + col),
        (other_core, jnp.clip(y + 2 * core - 1, 0, lax.axis_size("y") - 1) * cols + col),
        (same_core, y * cols + (col + 1 - 2 * odd)),
        (same_core, y * cols + jnp.clip(col + 2 * odd - 1, 0, cols - 1)),
    )
    map_rows = [x[pl.ds(i * each + 9, 1), :] for x, i in partners]
    map_rows = jnp.concatenate([jnp.broadcast_to(row, (8, 128)) for row in map_rows], axis=0)
    on_diagonal = lax.broadcasted_iota(jnp.int32, (32, 128), 0) % 8 == lax.broadcasted_iota(jnp.int32, (32, 128), 1)
    maps = jnp.sum(jnp.where(on_diagonal, map_rows, 0.0), axis=1, keepdims=True).astype(jnp.int32)
    maps = jnp.concatenate([mapped(primal_map, (8, 128), 0)[:, 0:1], maps], axis=0)
    lane = lax.broadcasted_iota(jnp.int32, (40, order), 1)
    picked = fold(dot((maps == lane).astype(F32).astype(BF16), exact_pair(coarse)))
    wanted[...] = picked[8:40]
    own_back = back(basis[...], picked[0:8])
    previous_copy.wait()
    for b in range(count):
        mine = local[b] + own_back[b * 128 : (b + 1) * 128] * weight_of(multiplicity, b)
        started[b] = mine + beta * previous[b]
def direction_kernel(
    faces, pattern, started, wanted, got_2, got_3, got_0, got_1, stacked,
    direction_hbm, direction, image, send_2, send_3, send_0, send_1, curvature,
    added, pairs, slot, direction_sem,
):
    count = started.shape[0]
    slots_by_block(faces, slot)
    for s, r in enumerate((got_0, got_1, got_2, got_3)):
        face_basis = jnp.concatenate([r[512 + 8 * k : 520 + 8 * k, :] for k in range(SLOTS)], axis=1)
        face_back = back(face_basis, wanted[8 * s : 8 * s + 8, :])
        for k in range(SLOTS):
            part = slice(k * 128, (k + 1) * 128)
            added[s * SLOTS + k] = r[part, :] + face_back[part]
    added[16] = jnp.zeros((128, 128), F32)
    for b in range(count):
        value = started[b] + added[slot[b]]
        direction[b] = value
        pairs[b] = exact_pair(value)
    direction_copy = pltpu.make_async_copy(direction, direction_hbm, direction_sem)
    direction_copy.start()
    total = jnp.zeros((8, 128), F32)
    for b in range(count):
        out = row_product(stacked[b], pattern, b, pairs)
        image[b] = out
        total += partial_rows(direction[b] * out)
    for f, sent in zip(partner_faces(), (send_0, send_1, send_2, send_3)):
        for k in range(SLOTS):
            sent[k * 128 : (k + 1) * 128, :] = image[jnp.minimum(faces[f, k], count - 1)]
    curvature[...] = jnp.broadcast_to(jnp.sum(total, axis=0, keepdims=True), curvature.shape)
    direction_copy.wait()


def update_kernel(
    faces, current, residual, direction, image, got_2, got_3, got_0, got_1, curvature, precond_dot,
    new_solution_hbm, new_residual_hbm,
    new_solution, new_residual, added, slot, solution_sems, residual_sems,
):
    count = current.shape[0]
    slots_by_block(faces, slot)
    step = precond_dot[...] / jnp.sum(curvature[...], axis=0, keepdims=True)
    copies = []

    def leave(c, value, value_hbm, sems):
        part = pl.ds(c * count // 4, count // 4)
        copies.append(pltpu.make_async_copy(value.at[part], value_hbm.at[part], sems.at[c]))
        copies[-1].start()

    for b in range(count):
        new_solution[b] = current[b] + step * direction[b]
        if (b + 1) % (count // 4) == 0:
            leave(b // (count // 4), new_solution, new_solution_hbm, solution_sems)
    for s, r in enumerate((got_0, got_1, got_2, got_3)):
        for k in range(SLOTS):
            added[s * SLOTS + k] = r[k * 128 : (k + 1) * 128, :]
    added[16] = jnp.zeros((128, 128), F32)
    for b in range(count):
        new_residual[b] = residual[b] - step * (image[b] + added[slot[b]])
        if (b + 1) % (count // 4) == 0:
            leave(b // (count // 4), new_residual, new_residual_hbm, residual_sems)
    for copy in copies:
        copy.wait()


def swap_pairs(x, axis, first):
    pairs = [(i, i + 1) for i in range(first, lax.axis_size(axis) - 1, 2)]
    return lax.ppermute(x, axis, pairs + [(j, i) for i, j in pairs])


def from_all(x, axes):
    sent = x.reshape(lax.axis_size(axes), 1, -1)
    return lax.all_to_all(sent, axes, split_axis=0, concat_axis=0, tiled=True).reshape(x.shape)


def shape(*dims):
    return jax.ShapeDtypeStruct(dims, F32)


def held(*dims):
    return pltpu.VMEM(dims, F32)


def in_hbm(x):
    return pltpu.with_memory_space_constraint(x, pltpu.HBM)


def kernel_params(mib):
    return pltpu.CompilerParams(vmem_limit_bytes=mib << 20)


def per_device(
    solution,
    residual,
    prev_direction,
    prev_dot,
    face_lists,
    multiplicity,
    block_pattern,
    schur,
    neumann_inverse,
    coarse_basis,
    primal_map,
    coarse_inverse,
):
    current, residual, previous = solution[0, 0], residual[0, 0], prev_direction[0, 0]
    faces, multiplicity = face_lists[0, 0], multiplicity[0, 0]
    pattern = jnp.transpose(block_pattern, (0, 3, 1, 2))[0]
    schur, neumann = schur[0, 0], neumann_inverse[0, 0]
    basis, primal_map = coarse_basis[0, 0], primal_map[0, 0]
    count, dofs, cases = residual.shape

    everywhere = lax.axis_size(("y", "core", "col"))
    order = coarse_inverse.shape[1]
    told_rows = (HEAD + 8 * (order // cases)) * (everywhere // 2)

    face = held(SLOTS * dofs + 32, cases)
    indices = (faces, multiplicity, pattern, primal_map)
    local, send_2, told, send_3, send_0, send_1 = pl.pallas_call(
        local_kernel,
        out_shape=(held(count, dofs, cases), face, shape(told_rows, cases), face, face, face),
        in_specs=[HBM] * 8,
        out_specs=(VMEM, VMEM, HBM, VMEM, VMEM, VMEM),
        scratch_shapes=[pltpu.SMEM(x.shape, jnp.int32) for x in indices]
        + [
            pltpu.VMEM(residual.shape, F32),
            pltpu.VMEM(neumann.shape, F32),
            pltpu.VMEM(basis.shape, F32),
            pltpu.VMEM(coarse_inverse.shape, F32),
            pltpu.VMEM((count, dofs, 2 * cases), BF16),
            pltpu.VMEM((told_rows, cases), F32),
            pltpu.SemaphoreType.DMA((4,)),
            pltpu.SemaphoreType.DMA((2,)),
            pltpu.SemaphoreType.DMA((4,)),
            pltpu.SemaphoreType.DMA((2,)),
            pltpu.SemaphoreType.DMA,
        ],
        compiler_params=kernel_params(16),
        name="local_solve",
    )(*(in_hbm(x) for x in (*indices, residual, neumann, basis, coarse_inverse)))

    same_core = from_all(told, ("y", "col"))
    other_core = lax.ppermute(same_core, "core", [(0, 1), (1, 0)])
    got_2 = swap_pairs(send_2, "col", 0)
    got_3 = swap_pairs(send_3, "col", 1)
    got_0 = swap_pairs(send_0, ("y", "core"), 0)
    got_1 = swap_pairs(send_1, ("y", "core"), 1)

    stacked = pl.pallas_call(
        halving_kernel,
        out_shape=pltpu.VMEM((count, 2 * dofs, 3 * dofs), BF16),
        in_specs=[HBM],
        out_specs=VMEM,
        scratch_shapes=[pltpu.VMEM(schur.shape, F32), pltpu.SemaphoreType.DMA((4,))],
        compiler_params=kernel_params(12),
        name="halving",
    )(in_hbm(schur))

    started, wanted, precond_dot = pl.pallas_call(
        coarse_kernel,
        out_shape=(held(count, dofs, cases), held(32, cases), held(1, cases)),
        in_specs=[SMEM] * 2 + [VMEM] * 5 + [HBM],
        out_specs=(VMEM,) * 3,
        scratch_shapes=[
            pltpu.VMEM((order, order), F32),
            pltpu.VMEM(previous.shape, F32),
            pltpu.SemaphoreType.DMA,
        ],
        compiler_params=kernel_params(24),
        name="coarse_solve",
    )(
        multiplicity, primal_map, local, same_core, other_core, basis, prev_dot.reshape(1, cases),
        in_hbm(previous),
    )

    direction, direction_held, image, send_2, send_3, send_0, send_1, curvature = pl.pallas_call(
        direction_kernel,
        out_shape=(shape(count, dofs, cases), held(count, dofs, cases), held(count, dofs, cases))
        + (held(SLOTS * dofs, cases),) * 4
        + (held(everywhere, cases),),
        in_specs=[SMEM] * 2 + [VMEM] * 7,
        out_specs=(HBM,) + (VMEM,) * 7,
        scratch_shapes=[
            pltpu.VMEM((17, dofs, cases), F32),
            pltpu.VMEM((count, dofs, 2 * cases), BF16),
            pltpu.SMEM((17,), jnp.int32),
            pltpu.SemaphoreType.DMA,
        ],
        compiler_params=kernel_params(16),
        name="direction_image",
    )(faces, pattern, started, wanted, got_2, got_3, got_0, got_1, stacked)

    got_2 = swap_pairs(send_2, "col", 0)
    got_3 = swap_pairs(send_3, "col", 1)
    got_0 = swap_pairs(send_0, ("y", "core"), 0)
    got_1 = swap_pairs(send_1, ("y", "core"), 1)
    curvature = from_all(curvature, ("y", "core", "col"))

    new_solution, new_residual = pl.pallas_call(
        update_kernel,
        out_shape=(shape(count, dofs, cases),) * 2,
        in_specs=[SMEM] + [VMEM] * 10,
        out_specs=(HBM,) * 2,
        scratch_shapes=[
            pltpu.VMEM(residual.shape, F32),
            pltpu.VMEM(residual.shape, F32),
            pltpu.VMEM((17, dofs, cases), F32),
            pltpu.SMEM((17,), jnp.int32),
            pltpu.SemaphoreType.DMA((4,)),
            pltpu.SemaphoreType.DMA((4,)),
        ],
        compiler_params=kernel_params(16),
        name="update",
    )(
        faces, current, residual, direction_held, image, got_2, got_3, got_0, got_1, curvature, precond_dot
    )
    return (new_solution[None, None], new_residual[None, None], direction[None, None])


def solution(mesh):
    rows, cols = mesh.devices.shape
    mesh = jax.sharding.Mesh(mesh.devices.reshape(rows // 2, 2, cols), ("y", "core", "col"))
    split = lambda dims: P(("y", "core"), "col", *(None,) * dims)
    placed = (
        split(3), split(3), split(3), P(), split(2), split(1), split(2), split(4), split(4), split(2), split(1),
        P("col", None),
    )
    return jax.shard_map(
        per_device,
        mesh=mesh,
        in_specs=placed,
        out_specs=(split(3), split(3), split(3)),
        check_vma=False,
    )
```

```python
import jax
import jax.numpy as jnp
from jax import lax
from jax.experimental import pallas as pl
from jax.experimental.pallas import tpu as pltpu
from jax.sharding import PartitionSpec as P

F32 = jnp.float32
BF16 = jnp.bfloat16
SLOTS = 4
HEAD = 10
SMEM = pl.BlockSpec(memory_space=pltpu.SMEM)
VMEM = pl.BlockSpec(memory_space=pltpu.VMEM)
HBM = pl.BlockSpec(memory_space=pltpu.HBM)
ANY = pl.BlockSpec(memory_space=pl.ANY)


def halves(x):
    high = x.astype(BF16)
    return high, (x - high.astype(F32)).astype(BF16)


def dot(a, b):
    return jnp.dot(a, b, preferred_element_type=F32)


def dot_first(a, b):
    return lax.dot_general(a, b, (((0,), (0,)), ((), ())), preferred_element_type=F32)


def fold(x):
    width = x.shape[1] // 2
    return x[:, :width] + x[:, width:]


def product(matrix, pair):
    high, low = halves(matrix)
    return fold(dot(high, pair)) + dot(low, pair[:, : pair.shape[1] // 2])


def exact_pair(x):
    return jnp.concatenate(halves(x), axis=1)


def halved_rows(row_blocks):
    matrix = jnp.concatenate([row_blocks[k] for k in range(3)], axis=1)
    return jnp.concatenate(halves(matrix), axis=0)


def row_product(stacked, pattern, b, pairs):
    field = jnp.concatenate([pairs[pattern[k, 0, b]] for k in range(3)], axis=0)
    both = fold(dot(stacked, field))
    return both[:128] + both[128:]


def partial_rows(x):
    rows, cols = x.shape
    return jnp.sum(x.reshape(rows // 8, 8, cols), axis=0)


def weight_of(multiplicity, b):
    return 1.0 / jnp.full((1, 128), multiplicity[b].astype(F32))


def mapped(primal_map, shape, dim):
    place = lax.broadcasted_iota(jnp.int32, shape, dim)
    found = jnp.zeros(shape, jnp.int32)
    for p in range(8):
        found = jnp.where(place == p, primal_map[p], found)
    return found


def row_index():
    return 2 * lax.axis_index("y") + lax.axis_index("core")


def partner_faces():
    row, col = lax.axis_index("core"), lax.axis_index("col") % 2
    return 1 - row, row, 3 - col, 2 + col


def slots_by_block(faces, slot):
    for b in range(17):
        slot[b] = 16
    for s, f in enumerate(partner_faces()):
        for k in range(SLOTS):
            slot[faces[f, k]] = s * SLOTS + k


def local_kernel(
    faces_hbm, multiplicity_hbm, pattern_hbm, primal_map_hbm, residual_hbm, neumann_hbm, basis_hbm, inverse_hbm,
    local, send_2, told_hbm, send_3, send_0, send_1,
    faces, multiplicity, pattern, primal_map, residual, neumann, basis, inverse, pairs, told,
    index_sems, residual_sems, neumann_sems, basis_sems, told_sem,
):
    count = residual.shape[0]
    index_copies = [
        pltpu.make_async_copy(source, target, index_sems.at[i])
        for i, (source, target) in enumerate(
            ((multiplicity_hbm, multiplicity), (pattern_hbm, pattern), (primal_map_hbm, primal_map), (faces_hbm, faces))
        )
    ]
    basis_copy = pltpu.make_async_copy(basis_hbm, basis, basis_sems.at[0])
    inverse_copy = pltpu.make_async_copy(inverse_hbm, inverse, basis_sems.at[1])
    copies = []
    for c in range(2):
        part = pl.ds(c * count // 2, count // 2)
        copies.append(pltpu.make_async_copy(residual_hbm.at[part], residual.at[part], residual_sems.at[c]))
    for c in range(4):
        part = pl.ds(c * count // 4, count // 4)
        copies.append(pltpu.make_async_copy(neumann_hbm.at[part], neumann.at[part], neumann_sems.at[c]))
    for copy in (*index_copies, *copies[:2], basis_copy, *copies[2:], inverse_copy):
        copy.start()
    for copy in index_copies:
        copy.wait()
    for b in range(count):
        if b % (count // 2) == 0:
            copies[b // (count // 2)].wait()
        pairs[b] = exact_pair(residual[b] * weight_of(multiplicity, b))
    basis_copy.wait()
    coarse_local = product(basis[...], pairs[...].reshape(count * 128, 256))
    total = jnp.zeros((8, 128), F32)
    for b in range(count):
        if b % (count // 4) == 0:
            copies[2 + b // (count // 4)].wait()
        weight = weight_of(multiplicity, b)
        out = row_product(halved_rows(neumann.at[b]), pattern, b, pairs) * weight
        local[b] = out
        total += partial_rows(residual[b] * out)
    row = lax.broadcasted_iota(jnp.int32, (8, 128), 0)
    total = jnp.sum(total, axis=0, keepdims=True)
    map_row = mapped(primal_map, (8, 128), 1).astype(F32)
    inverse_copy.wait()
    sharers = inverse.shape[0] // 8
    mine = row_index() % sharers
    share = inverse[pl.ds(pl.multiple_of(mine * 8, 8), 8), :]
    rows = [coarse_local, jnp.where(row == 0, total, map_row)[:2]]
    rows = jnp.concatenate(rows + [share[:, i : i + 128] for i in range(0, inverse.shape[1], 128)], axis=0)
    each = rows.shape[0]
    for i in range(told.shape[0] // each):
        told[each * i : each * i + each, :] = rows
    told_copy = pltpu.make_async_copy(told, told_hbm, told_sem)
    told_copy.start()
    for f, sent in zip(partner_faces(), (send_0, send_1, send_2, send_3)):
        for k in range(SLOTS):
            b = jnp.minimum(faces[f, k], count - 1)
            sent[k * 128 : (k + 1) * 128, :] = local[b]
            lanes = pl.ds(pl.multiple_of(b * 128, 128), 128)
            sent[512 + 8 * k : 520 + 8 * k, :] = basis[:, lanes] * weight_of(multiplicity, b)
    told_copy.wait()


def back(basis, own):
    bh, bl = (h.astype(F32) for h in halves(basis))
    oh, ol = (h.astype(F32) for h in halves(own))
    left = jnp.concatenate([bh, bl, bh, bl], axis=0).astype(BF16)
    right = jnp.concatenate([oh, oh, ol, ol], axis=0).astype(BF16)
    return dot_first(left, right)


def halving_kernel(schur_hbm, stacked, schur, sems):
    count = schur.shape[0]
    copies = []
    for c in range(4):
        part = pl.ds(c * count // 4, count // 4)
        copies.append(pltpu.make_async_copy(schur_hbm.at[part], schur.at[part], sems.at[c]))
        copies[c].start()
    for b in range(count):
        if b % (count // 4) == 0:
            copies[b // (count // 4)].wait()
        stacked[b] = halved_rows(schur.at[b])


def coarse_kernel(
    multiplicity, primal_map, local, same_core, other_core, basis, prev_dot, previous_hbm,
    started, wanted, precond_dot, inverse, previous, previous_sem,
):
    count = local.shape[0]
    previous_copy = pltpu.make_async_copy(previous_hbm, previous, previous_sem)
    previous_copy.start()

    order = inverse.shape[1]
    each = HEAD + 8 * (order // 128)
    half = same_core.shape[0] // each
    cols = lax.axis_size("col")
    sharers = order // cols // 8
    for told, core in ((same_core, lax.axis_index("core")), (other_core, 1 - lax.axis_index("core"))):
        for i in range(half):
            target = pl.multiple_of((i % cols * sharers + (2 * (i // cols) + core) % sharers) * 8, 8)
            for j in range(order // 128):
                source = i * each + HEAD + 8 * j
                inverse[pl.ds(target, 8), 128 * j : 128 * j + 128] = told[source : source + 8, :]

    def row_of_all(p):
        return jnp.concatenate([x[pl.ds(p, half, stride=each), :] for x in (same_core, other_core)], axis=0)

    maps = row_of_all(9).astype(jnp.int32)
    lane = lax.broadcasted_iota(jnp.int32, (2 * half, order), 1)
    chosen = [(maps[:, p : p + 1] == lane).astype(F32) for p in range(8)]
    chosen = jnp.concatenate(chosen, axis=0).astype(BF16)
    rows = jnp.concatenate([row_of_all(p) for p in range(8)], axis=0)
    rhs = fold(dot_first(chosen, exact_pair(rows)))
    coarse = product(inverse[...], exact_pair(rhs))
    dots = jnp.sum(row_of_all(8), axis=0, keepdims=True)
    dots = dots + jnp.sum(rhs * coarse, axis=0, keepdims=True)
    precond_dot[...] = dots
    beta = dots / prev_dot[...]
    y, core, col = (lax.axis_index(name) for name in ("y", "core", "col"))
    odd = col % 2
    partners = (
        (other_core, y * cols + col),
        (other_core, jnp.clip(y + 2 * core - 1, 0, lax.axis_size("y") - 1) * cols + col),
        (same_core, y * cols + (col + 1 - 2 * odd)),
        (same_core, y * cols + jnp.clip(col + 2 * odd - 1, 0, cols - 1)),
    )
    map_rows = [x[pl.ds(i * each + 9, 1), :] for x, i in partners]
    map_rows = jnp.concatenate([jnp.broadcast_to(row, (8, 128)) for row in map_rows], axis=0)
    on_diagonal = lax.broadcasted_iota(jnp.int32, (32, 128), 0) % 8 == lax.broadcasted_iota(jnp.int32, (32, 128), 1)
    maps = jnp.sum(jnp.where(on_diagonal, map_rows, 0.0), axis=1, keepdims=True).astype(jnp.int32)
    maps = jnp.concatenate([mapped(primal_map, (8, 128), 0)[:, 0:1], maps], axis=0)
    lane = lax.broadcasted_iota(jnp.int32, (40, order), 1)
    picked = fold(dot((maps == lane).astype(F32).astype(BF16), exact_pair(coarse)))
    wanted[...] = picked[8:40]
    own_back = back(basis[...], picked[0:8])
    previous_copy.wait()
    for b in range(count):
        mine = local[b] + own_back[b * 128 : (b + 1) * 128] * weight_of(multiplicity, b)
        started[b] = mine + beta * previous[b]
def direction_kernel(
    faces, pattern, started, wanted, got_2, got_3, got_0, got_1, stacked,
    direction_hbm, direction, image, send_2, send_3, send_0, send_1, curvature,
    added, pairs, slot, direction_sem,
):
    count = started.shape[0]
    slots_by_block(faces, slot)
    for s, r in enumerate((got_0, got_1, got_2, got_3)):
        face_basis = jnp.concatenate([r[512 + 8 * k : 520 + 8 * k, :] for k in range(SLOTS)], axis=1)
        face_back = back(face_basis, wanted[8 * s : 8 * s + 8, :])
        for k in range(SLOTS):
            part = slice(k * 128, (k + 1) * 128)
            added[s * SLOTS + k] = r[part, :] + face_back[part]
    added[16] = jnp.zeros((128, 128), F32)
    for b in range(count):
        value = started[b] + added[slot[b]]
        direction[b] = value
        pairs[b] = exact_pair(value)
    direction_copy = pltpu.make_async_copy(direction, direction_hbm, direction_sem)
    direction_copy.start()
    total = jnp.zeros((8, 128), F32)
    for b in range(count):
        out = row_product(stacked[b], pattern, b, pairs)
        image[b] = out
        total += partial_rows(direction[b] * out)
    for f, sent in zip(partner_faces(), (send_0, send_1, send_2, send_3)):
        for k in range(SLOTS):
            sent[k * 128 : (k + 1) * 128, :] = image[jnp.minimum(faces[f, k], count - 1)]
    curvature[...] = jnp.broadcast_to(jnp.sum(total, axis=0, keepdims=True), curvature.shape)
    direction_copy.wait()


def update_kernel(
    faces, current, residual, direction, image, got_2, got_3, got_0, got_1, curvature, precond_dot,
    new_solution_hbm, new_residual_hbm,
    new_solution, new_residual, added, slot, solution_sems, residual_sems,
):
    count = current.shape[0]
    slots_by_block(faces, slot)
    step = precond_dot[...] / jnp.sum(curvature[...], axis=0, keepdims=True)
    copies = []

    def leave(c, value, value_hbm, sems):
        part = pl.ds(c * count // 4, count // 4)
        copies.append(pltpu.make_async_copy(value.at[part], value_hbm.at[part], sems.at[c]))
        copies[-1].start()

    for b in range(count):
        new_solution[b] = current[b] + step * direction[b]
        if (b + 1) % (count // 4) == 0:
            leave(b // (count // 4), new_solution, new_solution_hbm, solution_sems)
    for s, r in enumerate((got_0, got_1, got_2, got_3)):
        for k in range(SLOTS):
            added[s * SLOTS + k] = r[k * 128 : (k + 1) * 128, :]
    added[16] = jnp.zeros((128, 128), F32)
    for b in range(count):
        new_residual[b] = residual[b] - step * (image[b] + added[slot[b]])
        if (b + 1) % (count // 4) == 0:
            leave(b // (count // 4), new_residual, new_residual_hbm, residual_sems)
    for copy in copies:
        copy.wait()


def swap_pairs(x, axis, first):
    pairs = [(i, i + 1) for i in range(first, lax.axis_size(axis) - 1, 2)]
    return lax.ppermute(x, axis, pairs + [(j, i) for i, j in pairs])


def pass_kernel(*refs):
    pass


def passed(*arrays):
    return pl.pallas_call(
        pass_kernel,
        out_shape=[held(*x.shape) for x in arrays],
        in_specs=[ANY] * len(arrays),
        out_specs=[ANY] * len(arrays),
        input_output_aliases={i: i for i in range(len(arrays))},
        compiler_params=kernel_params(4),
        name="passed",
    )(*arrays)


def from_all(x, axes):
    sent = x.reshape(lax.axis_size(axes), 1, -1)
    return lax.all_to_all(sent, axes, split_axis=0, concat_axis=0, tiled=True).reshape(x.shape)


def shape(*dims):
    return jax.ShapeDtypeStruct(dims, F32)


def held(*dims):
    return pltpu.VMEM(dims, F32)


def in_hbm(x):
    return pltpu.with_memory_space_constraint(x, pltpu.HBM)


def kernel_params(mib):
    return pltpu.CompilerParams(vmem_limit_bytes=mib << 20)


def per_device(
    solution,
    residual,
    prev_direction,
    prev_dot,
    face_lists,
    multiplicity,
    block_pattern,
    schur,
    neumann_inverse,
    coarse_basis,
    primal_map,
    coarse_inverse,
):
    current, residual, previous = solution[0, 0], residual[0, 0], prev_direction[0, 0]
    faces, multiplicity = face_lists[0, 0], multiplicity[0, 0]
    pattern = jnp.transpose(block_pattern, (0, 3, 1, 2))[0]
    schur, neumann = schur[0, 0], neumann_inverse[0, 0]
    basis, primal_map = coarse_basis[0, 0], primal_map[0, 0]
    count, dofs, cases = residual.shape

    everywhere = lax.axis_size(("y", "core", "col"))
    order = coarse_inverse.shape[1]
    told_rows = (HEAD + 8 * (order // cases)) * (everywhere // 2)

    face = held(SLOTS * dofs + 32, cases)
    indices = (faces, multiplicity, pattern, primal_map)
    local, send_2, told, send_3, send_0, send_1 = pl.pallas_call(
        local_kernel,
        out_shape=(held(count, dofs, cases), face, shape(told_rows, cases), face, face, face),
        in_specs=[HBM] * 8,
        out_specs=(VMEM, VMEM, HBM, VMEM, VMEM, VMEM),
        scratch_shapes=[pltpu.SMEM(x.shape, jnp.int32) for x in indices]
        + [
            pltpu.VMEM(residual.shape, F32),
            pltpu.VMEM(neumann.shape, F32),
            pltpu.VMEM(basis.shape, F32),
            pltpu.VMEM(coarse_inverse.shape, F32),
            pltpu.VMEM((count, dofs, 2 * cases), BF16),
            pltpu.VMEM((told_rows, cases), F32),
            pltpu.SemaphoreType.DMA((4,)),
            pltpu.SemaphoreType.DMA((2,)),
            pltpu.SemaphoreType.DMA((4,)),
            pltpu.SemaphoreType.DMA((2,)),
            pltpu.SemaphoreType.DMA,
        ],
        compiler_params=kernel_params(16),
        name="local_solve",
    )(*(in_hbm(x) for x in (*indices, residual, neumann, basis, coarse_inverse)))

    same_core = from_all(told, ("y", "col"))
    other_core = lax.ppermute(same_core, "core", [(0, 1), (1, 0)])
    got_2 = swap_pairs(send_2, "col", 0)
    got_3 = swap_pairs(send_3, "col", 1)
    got_0 = swap_pairs(send_0, ("y", "core"), 0)
    got_1 = swap_pairs(send_1, ("y", "core"), 1)

    stacked = pl.pallas_call(
        halving_kernel,
        out_shape=pltpu.VMEM((count, 2 * dofs, 3 * dofs), BF16),
        in_specs=[HBM],
        out_specs=VMEM,
        scratch_shapes=[pltpu.VMEM(schur.shape, F32), pltpu.SemaphoreType.DMA((4,))],
        compiler_params=kernel_params(12),
        name="halving",
    )(in_hbm(schur))

    started, wanted, precond_dot = pl.pallas_call(
        coarse_kernel,
        out_shape=(held(count, dofs, cases), held(32, cases), held(1, cases)),
        in_specs=[SMEM] * 2 + [VMEM] * 5 + [HBM],
        out_specs=(VMEM,) * 3,
        scratch_shapes=[
            pltpu.VMEM((order, order), F32),
            pltpu.VMEM(previous.shape, F32),
            pltpu.SemaphoreType.DMA,
        ],
        compiler_params=kernel_params(24),
        name="coarse_solve",
    )(
        multiplicity, primal_map, local, same_core, other_core, basis, prev_dot.reshape(1, cases),
        in_hbm(previous),
    )

    direction, direction_held, image, send_2, send_3, send_0, send_1, curvature = pl.pallas_call(
        direction_kernel,
        out_shape=(shape(count, dofs, cases), held(count, dofs, cases), held(count, dofs, cases))
        + (held(SLOTS * dofs, cases),) * 4
        + (held(everywhere, cases),),
        in_specs=[SMEM] * 2 + [VMEM] * 7,
        out_specs=(HBM,) + (VMEM,) * 7,
        scratch_shapes=[
            pltpu.VMEM((17, dofs, cases), F32),
            pltpu.VMEM((count, dofs, 2 * cases), BF16),
            pltpu.SMEM((17,), jnp.int32),
            pltpu.SemaphoreType.DMA,
        ],
        compiler_params=kernel_params(16),
        name="direction_image",
    )(faces, pattern, started, wanted, got_2, got_3, got_0, got_1, stacked)

    got_2 = swap_pairs(send_2, "col", 0)
    got_3 = swap_pairs(send_3, "col", 1)
    got_1 = swap_pairs(send_1, ("y", "core"), 1)
    curvature = from_all(curvature, ("y", "core", "col"))
    curvature, send_0 = passed(curvature, send_0)
    got_0 = swap_pairs(send_0, ("y", "core"), 0)

    new_solution, new_residual = pl.pallas_call(
        update_kernel,
        out_shape=(shape(count, dofs, cases),) * 2,
        in_specs=[SMEM] + [VMEM] * 10,
        out_specs=(HBM,) * 2,
        scratch_shapes=[
            pltpu.VMEM(residual.shape, F32),
            pltpu.VMEM(residual.shape, F32),
            pltpu.VMEM((17, dofs, cases), F32),
            pltpu.SMEM((17,), jnp.int32),
            pltpu.SemaphoreType.DMA((4,)),
            pltpu.SemaphoreType.DMA((4,)),
        ],
        compiler_params=kernel_params(16),
        name="update",
    )(
        faces, current, residual, direction_held, image, got_2, got_3, got_0, got_1, curvature, precond_dot
    )
    return (new_solution[None, None], new_residual[None, None], direction[None, None])


def solution(mesh):
    rows, cols = mesh.devices.shape
    mesh = jax.sharding.Mesh(mesh.devices.reshape(rows // 2, 2, cols), ("y", "core", "col"))
    split = lambda dims: P(("y", "core"), "col", *(None,) * dims)
    placed = (
        split(3), split(3), split(3), P(), split(2), split(1), split(2), split(4), split(4), split(2), split(1),
        P("col", None),
    )
    return jax.shard_map(
        per_device,
        mesh=mesh,
        in_specs=placed,
        out_specs=(split(3), split(3), split(3)),
        check_vma=False,
    )
```

```python
import jax
import jax.numpy as jnp
from jax import lax
from jax.experimental import pallas as pl
from jax.experimental.pallas import tpu as pltpu
from jax.sharding import PartitionSpec as P

F32 = jnp.float32
BF16 = jnp.bfloat16
SLOTS = 4
HEAD = 10
SMEM = pl.BlockSpec(memory_space=pltpu.SMEM)
VMEM = pl.BlockSpec(memory_space=pltpu.VMEM)
HBM = pl.BlockSpec(memory_space=pltpu.HBM)


def halves(x):
    high = x.astype(BF16)
    return high, (x - high.astype(F32)).astype(BF16)


def dot(a, b):
    return jnp.dot(a, b, preferred_element_type=F32)


def dot_first(a, b):
    return lax.dot_general(a, b, (((0,), (0,)), ((), ())), preferred_element_type=F32)


def fold(x):
    width = x.shape[1] // 2
    return x[:, :width] + x[:, width:]


def product(matrix, pair):
    high, low = halves(matrix)
    return fold(dot(high, pair)) + dot(low, pair[:, : pair.shape[1] // 2])


def exact_pair(x):
    return jnp.concatenate(halves(x), axis=1)


def halved_rows(row_blocks):
    matrix = jnp.concatenate([row_blocks[k] for k in range(3)], axis=1)
    return jnp.concatenate(halves(matrix), axis=0)


def row_product(stacked, pattern, b, pairs):
    field = jnp.concatenate([pairs[pattern[k, 0, b]] for k in range(3)], axis=0)
    both = fold(dot(stacked, field))
    return both[:128] + both[128:]


def partial_rows(x):
    rows, cols = x.shape
    return jnp.sum(x.reshape(rows // 8, 8, cols), axis=0)


def weight_of(multiplicity, b):
    return 1.0 / jnp.full((1, 128), multiplicity[b].astype(F32))


def mapped(primal_map, shape, dim):
    place = lax.broadcasted_iota(jnp.int32, shape, dim)
    found = jnp.zeros(shape, jnp.int32)
    for p in range(8):
        found = jnp.where(place == p, primal_map[p], found)
    return found


def row_index():
    return 2 * lax.axis_index("y") + lax.axis_index("core")


def partner_faces():
    row, col = lax.axis_index("core"), lax.axis_index("col") % 2
    return 1 - row, row, 3 - col, 2 + col


def slots_by_block(faces, slot):
    for b in range(17):
        slot[b] = 16
    for s, f in enumerate(partner_faces()):
        for k in range(SLOTS):
            slot[faces[f, k]] = s * SLOTS + k


def local_kernel(
    faces_hbm, multiplicity_hbm, pattern_hbm, primal_map_hbm, residual_hbm, neumann_hbm, basis_hbm, inverse_hbm,
    local, send_2, told_hbm, send_3, send_1, send_0,
    faces, multiplicity, pattern, primal_map, residual, neumann, basis, inverse, pairs, told,
    index_sems, residual_sems, neumann_sems, basis_sems, told_sem,
):
    count = residual.shape[0]
    index_copies = [
        pltpu.make_async_copy(source, target, index_sems.at[i])
        for i, (source, target) in enumerate(
            ((multiplicity_hbm, multiplicity), (pattern_hbm, pattern), (primal_map_hbm, primal_map), (faces_hbm, faces))
        )
    ]
    basis_copy = pltpu.make_async_copy(basis_hbm, basis, basis_sems.at[0])
    inverse_copy = pltpu.make_async_copy(inverse_hbm, inverse, basis_sems.at[1])
    copies = []
    for c in range(2):
        part = pl.ds(c * count // 2, count // 2)
        copies.append(pltpu.make_async_copy(residual_hbm.at[part], residual.at[part], residual_sems.at[c]))
    for c in range(4):
        part = pl.ds(c * count // 4, count // 4)
        copies.append(pltpu.make_async_copy(neumann_hbm.at[part], neumann.at[part], neumann_sems.at[c]))
    for copy in (*index_copies, *copies[:2], basis_copy, *copies[2:], inverse_copy):
        copy.start()
    for copy in index_copies:
        copy.wait()
    for b in range(count):
        if b % (count // 2) == 0:
            copies[b // (count // 2)].wait()
        pairs[b] = exact_pair(residual[b] * weight_of(multiplicity, b))
    basis_copy.wait()
    coarse_local = product(basis[...], pairs[...].reshape(count * 128, 256))
    total = jnp.zeros((8, 128), F32)
    for b in range(count):
        if b % (count // 4) == 0:
            copies[2 + b // (count // 4)].wait()
        weight = weight_of(multiplicity, b)
        out = row_product(halved_rows(neumann.at[b]), pattern, b, pairs) * weight
        local[b] = out
        total += partial_rows(residual[b] * out)
    row = lax.broadcasted_iota(jnp.int32, (8, 128), 0)
    total = jnp.sum(total, axis=0, keepdims=True)
    map_row = mapped(primal_map, (8, 128), 1).astype(F32)
    inverse_copy.wait()
    sharers = inverse.shape[0] // 8
    mine = row_index() % sharers
    share = inverse[pl.ds(pl.multiple_of(mine * 8, 8), 8), :]
    rows = [coarse_local, jnp.where(row == 0, total, map_row)[:2]]
    rows = jnp.concatenate(rows + [share[:, i : i + 128] for i in range(0, inverse.shape[1], 128)], axis=0)
    each = rows.shape[0]
    for i in range(told.shape[0] // each):
        told[each * i : each * i + each, :] = rows
    told_copy = pltpu.make_async_copy(told, told_hbm, told_sem)
    told_copy.start()
    for f, sent in zip(partner_faces(), (send_0, send_1, send_2, send_3)):
        for k in range(SLOTS):
            b = jnp.minimum(faces[f, k], count - 1)
            sent[k * 128 : (k + 1) * 128, :] = local[b]
            lanes = pl.ds(pl.multiple_of(b * 128, 128), 128)
            sent[512 + 8 * k : 520 + 8 * k, :] = basis[:, lanes] * weight_of(multiplicity, b)
    told_copy.wait()


def back(basis, own):
    bh, bl = (h.astype(F32) for h in halves(basis))
    oh, ol = (h.astype(F32) for h in halves(own))
    left = jnp.concatenate([bh, bl, bh, bl], axis=0).astype(BF16)
    right = jnp.concatenate([oh, oh, ol, ol], axis=0).astype(BF16)
    return dot_first(left, right)


def halving_kernel(schur_hbm, stacked, schur, sems):
    count = schur.shape[0]
    copies = []
    for c in range(4):
        part = pl.ds(c * count // 4, count // 4)
        copies.append(pltpu.make_async_copy(schur_hbm.at[part], schur.at[part], sems.at[c]))
        copies[c].start()
    for b in range(count):
        if b % (count // 4) == 0:
            copies[b // (count // 4)].wait()
        stacked[b] = halved_rows(schur.at[b])


def coarse_kernel(
    multiplicity, primal_map, local, same_core, other_core, basis, prev_dot, previous_hbm,
    started, wanted, precond_dot, inverse, previous, previous_sem,
):
    count = local.shape[0]
    previous_copy = pltpu.make_async_copy(previous_hbm, previous, previous_sem)
    previous_copy.start()

    order = inverse.shape[1]
    each = HEAD + 8 * (order // 128)
    half = same_core.shape[0] // each
    cols = lax.axis_size("col")
    sharers = order // cols // 8
    for told, core in ((same_core, lax.axis_index("core")), (other_core, 1 - lax.axis_index("core"))):
        for i in range(half):
            target = pl.multiple_of((i % cols * sharers + (2 * (i // cols) + core) % sharers) * 8, 8)
            for j in range(order // 128):
                source = i * each + HEAD + 8 * j
                inverse[pl.ds(target, 8), 128 * j : 128 * j + 128] = told[source : source + 8, :]

    def row_of_all(p):
        return jnp.concatenate([x[pl.ds(p, half, stride=each), :] for x in (same_core, other_core)], axis=0)

    maps = row_of_all(9).astype(jnp.int32)
    lane = lax.broadcasted_iota(jnp.int32, (2 * half, order), 1)
    chosen = [(maps[:, p : p + 1] == lane).astype(F32) for p in range(8)]
    chosen = jnp.concatenate(chosen, axis=0).astype(BF16)
    rows = jnp.concatenate([row_of_all(p) for p in range(8)], axis=0)
    rhs = fold(dot_first(chosen, exact_pair(rows)))
    coarse = product(inverse[...], exact_pair(rhs))
    dots = jnp.sum(row_of_all(8), axis=0, keepdims=True)
    dots = dots + jnp.sum(rhs * coarse, axis=0, keepdims=True)
    precond_dot[...] = dots
    beta = dots / prev_dot[...]
    y, core, col = (lax.axis_index(name) for name in ("y", "core", "col"))
    odd = col % 2
    partners = (
        (other_core, y * cols + col),
        (other_core, jnp.clip(y + 2 * core - 1, 0, lax.axis_size("y") - 1) * cols + col),
        (same_core, y * cols + (col + 1 - 2 * odd)),
        (same_core, y * cols + jnp.clip(col + 2 * odd - 1, 0, cols - 1)),
    )
    map_rows = [x[pl.ds(i * each + 9, 1), :] for x, i in partners]
    map_rows = jnp.concatenate([jnp.broadcast_to(row, (8, 128)) for row in map_rows], axis=0)
    on_diagonal = lax.broadcasted_iota(jnp.int32, (32, 128), 0) % 8 == lax.broadcasted_iota(jnp.int32, (32, 128), 1)
    maps = jnp.sum(jnp.where(on_diagonal, map_rows, 0.0), axis=1, keepdims=True).astype(jnp.int32)
    maps = jnp.concatenate([mapped(primal_map, (8, 128), 0)[:, 0:1], maps], axis=0)
    lane = lax.broadcasted_iota(jnp.int32, (40, order), 1)
    picked = fold(dot((maps == lane).astype(F32).astype(BF16), exact_pair(coarse)))
    wanted[...] = picked[8:40]
    own_back = back(basis[...], picked[0:8])
    previous_copy.wait()
    for b in range(count):
        mine = local[b] + own_back[b * 128 : (b + 1) * 128] * weight_of(multiplicity, b)
        started[b] = mine + beta * previous[b]
def direction_kernel(
    faces, pattern, started, wanted, got_2, got_3, got_1, got_0, stacked,
    direction_hbm, direction, image, send_2, send_3, send_1, send_0, curvature,
    added, pairs, slot, direction_sem,
):
    count = started.shape[0]
    slots_by_block(faces, slot)
    for s, r in enumerate((got_0, got_1, got_2, got_3)):
        face_basis = jnp.concatenate([r[512 + 8 * k : 520 + 8 * k, :] for k in range(SLOTS)], axis=1)
        face_back = back(face_basis, wanted[8 * s : 8 * s + 8, :])
        for k in range(SLOTS):
            part = slice(k * 128, (k + 1) * 128)
            added[s * SLOTS + k] = r[part, :] + face_back[part]
    added[16] = jnp.zeros((128, 128), F32)
    for b in range(count):
        value = started[b] + added[slot[b]]
        direction[b] = value
        pairs[b] = exact_pair(value)
    direction_copy = pltpu.make_async_copy(direction, direction_hbm, direction_sem)
    direction_copy.start()
    total = jnp.zeros((8, 128), F32)
    for b in range(count):
        out = row_product(stacked[b], pattern, b, pairs)
        image[b] = out
        total += partial_rows(direction[b] * out)
    for f, sent in zip(partner_faces(), (send_0, send_1, send_2, send_3)):
        for k in range(SLOTS):
            sent[k * 128 : (k + 1) * 128, :] = image[jnp.minimum(faces[f, k], count - 1)]
    curvature[...] = jnp.broadcast_to(jnp.sum(total, axis=0, keepdims=True), curvature.shape)
    direction_copy.wait()


def update_kernel(
    faces, current, residual, direction, image, got_2, got_3, got_1, got_0, curvature, precond_dot,
    new_solution_hbm, new_residual_hbm,
    new_solution, new_residual, added, slot, solution_sems, residual_sems,
):
    count = current.shape[0]
    slots_by_block(faces, slot)
    step = precond_dot[...] / jnp.sum(curvature[...], axis=0, keepdims=True)
    copies = []

    def leave(c, value, value_hbm, sems):
        part = pl.ds(c * count // 4, count // 4)
        copies.append(pltpu.make_async_copy(value.at[part], value_hbm.at[part], sems.at[c]))
        copies[-1].start()

    for b in range(count):
        new_solution[b] = current[b] + step * direction[b]
        if (b + 1) % (count // 4) == 0:
            leave(b // (count // 4), new_solution, new_solution_hbm, solution_sems)
    for s, r in enumerate((got_0, got_1, got_2, got_3)):
        for k in range(SLOTS):
            added[s * SLOTS + k] = r[k * 128 : (k + 1) * 128, :]
    added[16] = jnp.zeros((128, 128), F32)
    for b in range(count):
        new_residual[b] = residual[b] - step * (image[b] + added[slot[b]])
        if (b + 1) % (count // 4) == 0:
            leave(b // (count // 4), new_residual, new_residual_hbm, residual_sems)
    for copy in copies:
        copy.wait()


def swap_pairs(x, axis, first):
    pairs = [(i, i + 1) for i in range(first, lax.axis_size(axis) - 1, 2)]
    return lax.ppermute(x, axis, pairs + [(j, i) for i, j in pairs])


def from_all(x, axes):
    sent = x.reshape(lax.axis_size(axes), 1, -1)
    return lax.all_to_all(sent, axes, split_axis=0, concat_axis=0, tiled=True).reshape(x.shape)


def shape(*dims):
    return jax.ShapeDtypeStruct(dims, F32)


def held(*dims):
    return pltpu.VMEM(dims, F32)


def in_hbm(x):
    return pltpu.with_memory_space_constraint(x, pltpu.HBM)


def kernel_params(mib):
    return pltpu.CompilerParams(vmem_limit_bytes=mib << 20)


def per_device(
    solution,
    residual,
    prev_direction,
    prev_dot,
    face_lists,
    multiplicity,
    block_pattern,
    schur,
    neumann_inverse,
    coarse_basis,
    primal_map,
    coarse_inverse,
):
    current, residual, previous = solution[0, 0], residual[0, 0], prev_direction[0, 0]
    faces, multiplicity = face_lists[0, 0], multiplicity[0, 0]
    pattern = jnp.transpose(block_pattern, (0, 3, 1, 2))[0]
    schur, neumann = schur[0, 0], neumann_inverse[0, 0]
    basis, primal_map = coarse_basis[0, 0], primal_map[0, 0]
    count, dofs, cases = residual.shape

    everywhere = lax.axis_size(("y", "core", "col"))
    order = coarse_inverse.shape[1]
    told_rows = (HEAD + 8 * (order // cases)) * (everywhere // 2)

    face = held(SLOTS * dofs + 32, cases)
    indices = (faces, multiplicity, pattern, primal_map)
    local, send_2, told, send_3, send_1, send_0 = pl.pallas_call(
        local_kernel,
        out_shape=(held(count, dofs, cases), face, shape(told_rows, cases), face, face, face),
        in_specs=[HBM] * 8,
        out_specs=(VMEM, VMEM, HBM, VMEM, VMEM, VMEM),
        scratch_shapes=[pltpu.SMEM(x.shape, jnp.int32) for x in indices]
        + [
            pltpu.VMEM(residual.shape, F32),
            pltpu.VMEM(neumann.shape, F32),
            pltpu.VMEM(basis.shape, F32),
            pltpu.VMEM(coarse_inverse.shape, F32),
            pltpu.VMEM((count, dofs, 2 * cases), BF16),
            pltpu.VMEM((told_rows, cases), F32),
            pltpu.SemaphoreType.DMA((4,)),
            pltpu.SemaphoreType.DMA((2,)),
            pltpu.SemaphoreType.DMA((4,)),
            pltpu.SemaphoreType.DMA((2,)),
            pltpu.SemaphoreType.DMA,
        ],
        compiler_params=kernel_params(16),
        name="local_solve",
    )(*(in_hbm(x) for x in (*indices, residual, neumann, basis, coarse_inverse)))

    same_core = from_all(told, ("y", "col"))
    other_core = lax.ppermute(same_core, "core", [(0, 1), (1, 0)])
    got_2 = swap_pairs(send_2, "col", 0)
    got_3 = swap_pairs(send_3, "col", 1)
    got_1 = swap_pairs(send_1, ("y", "core"), 1)
    got_0 = swap_pairs(send_0, ("y", "core"), 0)

    stacked = pl.pallas_call(
        halving_kernel,
        out_shape=pltpu.VMEM((count, 2 * dofs, 3 * dofs), BF16),
        in_specs=[HBM],
        out_specs=VMEM,
        scratch_shapes=[pltpu.VMEM(schur.shape, F32), pltpu.SemaphoreType.DMA((4,))],
        compiler_params=kernel_params(12),
        name="halving",
    )(in_hbm(schur))

    started, wanted, precond_dot = pl.pallas_call(
        coarse_kernel,
        out_shape=(held(count, dofs, cases), held(32, cases), held(1, cases)),
        in_specs=[SMEM] * 2 + [VMEM] * 5 + [HBM],
        out_specs=(VMEM,) * 3,
        scratch_shapes=[
            pltpu.VMEM((order, order), F32),
            pltpu.VMEM(previous.shape, F32),
            pltpu.SemaphoreType.DMA,
        ],
        compiler_params=kernel_params(24),
        name="coarse_solve",
    )(
        multiplicity, primal_map, local, same_core, other_core, basis, prev_dot.reshape(1, cases),
        in_hbm(previous),
    )

    direction, direction_held, image, send_2, send_3, send_1, send_0, curvature = pl.pallas_call(
        direction_kernel,
        out_shape=(shape(count, dofs, cases), held(count, dofs, cases), held(count, dofs, cases))
        + (held(SLOTS * dofs, cases),) * 4
        + (held(everywhere, cases),),
        in_specs=[SMEM] * 2 + [VMEM] * 7,
        out_specs=(HBM,) + (VMEM,) * 7,
        scratch_shapes=[
            pltpu.VMEM((17, dofs, cases), F32),
            pltpu.VMEM((count, dofs, 2 * cases), BF16),
            pltpu.SMEM((17,), jnp.int32),
            pltpu.SemaphoreType.DMA,
        ],
        compiler_params=kernel_params(16),
        name="direction_image",
    )(faces, pattern, started, wanted, got_2, got_3, got_1, got_0, stacked)

    got_2 = swap_pairs(send_2, "col", 0)
    got_3 = swap_pairs(send_3, "col", 1)
    got_1 = swap_pairs(send_1, ("y", "core"), 1)
    got_0 = swap_pairs(send_0, ("y", "core"), 0)
    curvature = from_all(curvature, ("y", "core", "col"))

    new_solution, new_residual = pl.pallas_call(
        update_kernel,
        out_shape=(shape(count, dofs, cases),) * 2,
        in_specs=[SMEM] + [VMEM] * 10,
        out_specs=(HBM,) * 2,
        scratch_shapes=[
            pltpu.VMEM(residual.shape, F32),
            pltpu.VMEM(residual.shape, F32),
            pltpu.VMEM((17, dofs, cases), F32),
            pltpu.SMEM((17,), jnp.int32),
            pltpu.SemaphoreType.DMA((4,)),
            pltpu.SemaphoreType.DMA((4,)),
        ],
        compiler_params=kernel_params(16),
        name="update",
    )(
        faces, current, residual, direction_held, image, got_2, got_3, got_1, got_0, curvature, precond_dot
    )
    return (new_solution[None, None], new_residual[None, None], direction[None, None])


def solution(mesh):
    rows, cols = mesh.devices.shape
    mesh = jax.sharding.Mesh(mesh.devices.reshape(rows // 2, 2, cols), ("y", "core", "col"))
    split = lambda dims: P(("y", "core"), "col", *(None,) * dims)
    placed = (
        split(3), split(3), split(3), P(), split(2), split(1), split(2), split(4), split(4), split(2), split(1),
        P("col", None),
    )
    return jax.shard_map(
        per_device,
        mesh=mesh,
        in_specs=placed,
        out_specs=(split(3), split(3), split(3)),
        check_vma=False,
    )
```

```python
import jax
import jax.numpy as jnp
from jax import lax
from jax.experimental import pallas as pl
from jax.experimental.pallas import tpu as pltpu
from jax.sharding import PartitionSpec as P

F32 = jnp.float32
BF16 = jnp.bfloat16
SLOTS = 4
HEAD = 10
SMEM = pl.BlockSpec(memory_space=pltpu.SMEM)
VMEM = pl.BlockSpec(memory_space=pltpu.VMEM)
HBM = pl.BlockSpec(memory_space=pltpu.HBM)


def halves(x):
    high = x.astype(BF16)
    return high, (x - high.astype(F32)).astype(BF16)


def dot(a, b):
    return jnp.dot(a, b, preferred_element_type=F32)


def dot_first(a, b):
    return lax.dot_general(a, b, (((0,), (0,)), ((), ())), preferred_element_type=F32)


def fold(x):
    width = x.shape[1] // 2
    return x[:, :width] + x[:, width:]


def product(matrix, pair):
    high, low = halves(matrix)
    return fold(dot(high, pair)) + dot(low, pair[:, : pair.shape[1] // 2])


def exact_pair(x):
    return jnp.concatenate(halves(x), axis=1)


def halved_rows(row_blocks):
    matrix = jnp.concatenate([row_blocks[k] for k in range(3)], axis=1)
    return jnp.concatenate(halves(matrix), axis=0)


def row_product(stacked, pattern, b, pairs):
    field = jnp.concatenate([pairs[pattern[k, 0, b]] for k in range(3)], axis=0)
    both = fold(dot(stacked, field))
    return both[:128] + both[128:]


def partial_rows(x):
    rows, cols = x.shape
    return jnp.sum(x.reshape(rows // 8, 8, cols), axis=0)


def weight_of(multiplicity, b):
    return 1.0 / jnp.full((1, 128), multiplicity[b].astype(F32))


def mapped(primal_map, shape, dim):
    place = lax.broadcasted_iota(jnp.int32, shape, dim)
    found = jnp.zeros(shape, jnp.int32)
    for p in range(8):
        found = jnp.where(place == p, primal_map[p], found)
    return found


def row_index():
    return 2 * lax.axis_index("y") + lax.axis_index("core")


def partner_faces():
    row, col = lax.axis_index("core"), lax.axis_index("col") % 2
    return 1 - row, row, 3 - col, 2 + col


def slots_by_block(faces, slot):
    for b in range(17):
        slot[b] = 16
    for s, f in enumerate(partner_faces()):
        for k in range(SLOTS):
            slot[faces[f, k]] = s * SLOTS + k


def local_kernel(
    faces_hbm, multiplicity_hbm, pattern_hbm, primal_map_hbm, residual_hbm, neumann_hbm, basis_hbm, inverse_hbm,
    local, send_2, told_hbm, send_3, send_1, send_0,
    faces, multiplicity, pattern, primal_map, residual, neumann, basis, inverse, pairs, told,
    index_sems, residual_sem, neumann_sems, basis_sems, told_sem,
):
    count = residual.shape[0]
    index_copies = [
        pltpu.make_async_copy(source, target, index_sems.at[i])
        for i, (source, target) in enumerate(
            ((multiplicity_hbm, multiplicity), (pattern_hbm, pattern), (primal_map_hbm, primal_map), (faces_hbm, faces))
        )
    ]
    basis_copy = pltpu.make_async_copy(basis_hbm, basis, basis_sems.at[0])
    inverse_copy = pltpu.make_async_copy(inverse_hbm, inverse, basis_sems.at[1])
    residual_copy = pltpu.make_async_copy(residual_hbm, residual, residual_sem)
    neumann_copies = {}
    for c, (start, stop) in enumerate(((0, count // 4), (count // 4, count))):
        part = pl.ds(start, stop - start)
        neumann_copies[start] = pltpu.make_async_copy(neumann_hbm.at[part], neumann.at[part], neumann_sems.at[c])
    for copy in (*index_copies, residual_copy, basis_copy, *neumann_copies.values(), inverse_copy):
        copy.start()
    for copy in index_copies:
        copy.wait()
    residual_copy.wait()
    for b in range(count):
        pairs[b] = exact_pair(residual[b] * weight_of(multiplicity, b))
    basis_copy.wait()
    coarse_local = product(basis[...], pairs[...].reshape(count * 128, 256))
    total = jnp.zeros((8, 128), F32)
    for b in range(count):
        if b in neumann_copies:
            neumann_copies[b].wait()
        weight = weight_of(multiplicity, b)
        out = row_product(halved_rows(neumann.at[b]), pattern, b, pairs) * weight
        local[b] = out
        total += partial_rows(residual[b] * out)
    row = lax.broadcasted_iota(jnp.int32, (8, 128), 0)
    total = jnp.sum(total, axis=0, keepdims=True)
    map_row = mapped(primal_map, (8, 128), 1).astype(F32)
    inverse_copy.wait()
    sharers = inverse.shape[0] // 8
    mine = row_index() % sharers
    share = inverse[pl.ds(pl.multiple_of(mine * 8, 8), 8), :]
    rows = [coarse_local, jnp.where(row == 0, total, map_row)[:2]]
    rows = jnp.concatenate(rows + [share[:, i : i + 128] for i in range(0, inverse.shape[1], 128)], axis=0)
    each = rows.shape[0]
    for i in range(told.shape[0] // each):
        told[each * i : each * i + each, :] = rows
    told_copy = pltpu.make_async_copy(told, told_hbm, told_sem)
    told_copy.start()
    for f, sent in zip(partner_faces(), (send_0, send_1, send_2, send_3)):
        for k in range(SLOTS):
            b = jnp.minimum(faces[f, k], count - 1)
            sent[k * 128 : (k + 1) * 128, :] = local[b]
            lanes = pl.ds(pl.multiple_of(b * 128, 128), 128)
            sent[512 + 8 * k : 520 + 8 * k, :] = basis[:, lanes] * weight_of(multiplicity, b)
    told_copy.wait()


def back(basis, own):
    bh, bl = (h.astype(F32) for h in halves(basis))
    oh, ol = (h.astype(F32) for h in halves(own))
    left = jnp.concatenate([bh, bl, bh, bl], axis=0).astype(BF16)
    right = jnp.concatenate([oh, oh, ol, ol], axis=0).astype(BF16)
    return dot_first(left, right)


def halving_kernel(schur_hbm, stacked, schur, sems):
    count = schur.shape[0]
    copies = []
    for c in range(4):
        part = pl.ds(c * count // 4, count // 4)
        copies.append(pltpu.make_async_copy(schur_hbm.at[part], schur.at[part], sems.at[c]))
        copies[c].start()
    for b in range(count):
        if b % (count // 4) == 0:
            copies[b // (count // 4)].wait()
        stacked[b] = halved_rows(schur.at[b])


def coarse_kernel(
    multiplicity, primal_map, local, same_core, other_core, basis, prev_dot, previous_hbm,
    started, wanted, precond_dot, inverse, previous, previous_sem,
):
    count = local.shape[0]
    previous_copy = pltpu.make_async_copy(previous_hbm, previous, previous_sem)
    previous_copy.start()

    order = inverse.shape[1]
    each = HEAD + 8 * (order // 128)
    half = same_core.shape[0] // each
    cols = lax.axis_size("col")
    sharers = order // cols // 8
    for told, core in ((same_core, lax.axis_index("core")), (other_core, 1 - lax.axis_index("core"))):
        for i in range(half):
            target = pl.multiple_of((i % cols * sharers + (2 * (i // cols) + core) % sharers) * 8, 8)
            for j in range(order // 128):
                source = i * each + HEAD + 8 * j
                inverse[pl.ds(target, 8), 128 * j : 128 * j + 128] = told[source : source + 8, :]

    def row_of_all(p):
        return jnp.concatenate([x[pl.ds(p, half, stride=each), :] for x in (same_core, other_core)], axis=0)

    maps = row_of_all(9).astype(jnp.int32)
    lane = lax.broadcasted_iota(jnp.int32, (2 * half, order), 1)
    chosen = [(maps[:, p : p + 1] == lane).astype(F32) for p in range(8)]
    chosen = jnp.concatenate(chosen, axis=0).astype(BF16)
    rows = jnp.concatenate([row_of_all(p) for p in range(8)], axis=0)
    rhs = fold(dot_first(chosen, exact_pair(rows)))
    coarse = product(inverse[...], exact_pair(rhs))
    dots = jnp.sum(row_of_all(8), axis=0, keepdims=True)
    dots = dots + jnp.sum(rhs * coarse, axis=0, keepdims=True)
    precond_dot[...] = dots
    beta = dots / prev_dot[...]
    y, core, col = (lax.axis_index(name) for name in ("y", "core", "col"))
    odd = col % 2
    partners = (
        (other_core, y * cols + col),
        (other_core, jnp.clip(y + 2 * core - 1, 0, lax.axis_size("y") - 1) * cols + col),
        (same_core, y * cols + (col + 1 - 2 * odd)),
        (same_core, y * cols + jnp.clip(col + 2 * odd - 1, 0, cols - 1)),
    )
    map_rows = [x[pl.ds(i * each + 9, 1), :] for x, i in partners]
    map_rows = jnp.concatenate([jnp.broadcast_to(row, (8, 128)) for row in map_rows], axis=0)
    on_diagonal = lax.broadcasted_iota(jnp.int32, (32, 128), 0) % 8 == lax.broadcasted_iota(jnp.int32, (32, 128), 1)
    maps = jnp.sum(jnp.where(on_diagonal, map_rows, 0.0), axis=1, keepdims=True).astype(jnp.int32)
    maps = jnp.concatenate([mapped(primal_map, (8, 128), 0)[:, 0:1], maps], axis=0)
    lane = lax.broadcasted_iota(jnp.int32, (40, order), 1)
    picked = fold(dot((maps == lane).astype(F32).astype(BF16), exact_pair(coarse)))
    wanted[...] = picked[8:40]
    own_back = back(basis[...], picked[0:8])
    previous_copy.wait()
    for b in range(count):
        mine = local[b] + own_back[b * 128 : (b + 1) * 128] * weight_of(multiplicity, b)
        started[b] = mine + beta * previous[b]
def direction_kernel(
    faces, pattern, started, wanted, got_2, got_3, got_1, got_0, stacked,
    direction_hbm, direction, image, send_2, send_3, send_1, send_0, curvature,
    added, pairs, slot, direction_sem,
):
    count = started.shape[0]
    slots_by_block(faces, slot)
    for s, r in enumerate((got_0, got_1, got_2, got_3)):
        face_basis = jnp.concatenate([r[512 + 8 * k : 520 + 8 * k, :] for k in range(SLOTS)], axis=1)
        face_back = back(face_basis, wanted[8 * s : 8 * s + 8, :])
        for k in range(SLOTS):
            part = slice(k * 128, (k + 1) * 128)
            added[s * SLOTS + k] = r[part, :] + face_back[part]
    added[16] = jnp.zeros((128, 128), F32)
    for b in range(count):
        value = started[b] + added[slot[b]]
        direction[b] = value
        pairs[b] = exact_pair(value)
    direction_copy = pltpu.make_async_copy(direction, direction_hbm, direction_sem)
    direction_copy.start()
    total = jnp.zeros((8, 128), F32)
    for b in range(count):
        out = row_product(stacked[b], pattern, b, pairs)
        image[b] = out
        total += partial_rows(direction[b] * out)
    for f, sent in zip(partner_faces(), (send_0, send_1, send_2, send_3)):
        for k in range(SLOTS):
            sent[k * 128 : (k + 1) * 128, :] = image[jnp.minimum(faces[f, k], count - 1)]
    curvature[...] = jnp.broadcast_to(jnp.sum(total, axis=0, keepdims=True), curvature.shape)
    direction_copy.wait()


def update_kernel(
    faces, current, residual, direction, image, got_2, got_3, got_1, got_0, curvature, precond_dot,
    new_solution_hbm, new_residual_hbm,
    new_solution, new_residual, added, slot, solution_sems, residual_sems,
):
    count = current.shape[0]
    slots_by_block(faces, slot)
    step = precond_dot[...] / jnp.sum(curvature[...], axis=0, keepdims=True)
    copies = []

    def leave(c, value, value_hbm, sems):
        part = pl.ds(c * count // 4, count // 4)
        copies.append(pltpu.make_async_copy(value.at[part], value_hbm.at[part], sems.at[c]))
        copies[-1].start()

    for b in range(count):
        new_solution[b] = current[b] + step * direction[b]
        if (b + 1) % (count // 4) == 0:
            leave(b // (count // 4), new_solution, new_solution_hbm, solution_sems)
    for s, r in enumerate((got_0, got_1, got_2, got_3)):
        for k in range(SLOTS):
            added[s * SLOTS + k] = r[k * 128 : (k + 1) * 128, :]
    added[16] = jnp.zeros((128, 128), F32)
    for b in range(count):
        new_residual[b] = residual[b] - step * (image[b] + added[slot[b]])
        if (b + 1) % (count // 4) == 0:
            leave(b // (count // 4), new_residual, new_residual_hbm, residual_sems)
    for copy in copies:
        copy.wait()


def swap_pairs(x, axis, first):
    pairs = [(i, i + 1) for i in range(first, lax.axis_size(axis) - 1, 2)]
    return lax.ppermute(x, axis, pairs + [(j, i) for i, j in pairs])


def from_all(x, axes):
    sent = x.reshape(lax.axis_size(axes), 1, -1)
    return lax.all_to_all(sent, axes, split_axis=0, concat_axis=0, tiled=True).reshape(x.shape)


def shape(*dims):
    return jax.ShapeDtypeStruct(dims, F32)


def held(*dims):
    return pltpu.VMEM(dims, F32)


def in_hbm(x):
    return pltpu.with_memory_space_constraint(x, pltpu.HBM)


def kernel_params(mib):
    return pltpu.CompilerParams(vmem_limit_bytes=mib << 20)


def per_device(
    solution,
    residual,
    prev_direction,
    prev_dot,
    face_lists,
    multiplicity,
    block_pattern,
    schur,
    neumann_inverse,
    coarse_basis,
    primal_map,
    coarse_inverse,
):
    current, residual, previous = solution[0, 0], residual[0, 0], prev_direction[0, 0]
    faces, multiplicity = face_lists[0, 0], multiplicity[0, 0]
    pattern = jnp.transpose(block_pattern, (0, 3, 1, 2))[0]
    schur, neumann = schur[0, 0], neumann_inverse[0, 0]
    basis, primal_map = coarse_basis[0, 0], primal_map[0, 0]
    count, dofs, cases = residual.shape

    everywhere = lax.axis_size(("y", "core", "col"))
    order = coarse_inverse.shape[1]
    told_rows = (HEAD + 8 * (order // cases)) * (everywhere // 2)

    face = held(SLOTS * dofs + 32, cases)
    indices = (faces, multiplicity, pattern, primal_map)
    local, send_2, told, send_3, send_1, send_0 = pl.pallas_call(
        local_kernel,
        out_shape=(held(count, dofs, cases), face, shape(told_rows, cases), face, face, face),
        in_specs=[HBM] * 8,
        out_specs=(VMEM, VMEM, HBM, VMEM, VMEM, VMEM),
        scratch_shapes=[pltpu.SMEM(x.shape, jnp.int32) for x in indices]
        + [
            pltpu.VMEM(residual.shape, F32),
            pltpu.VMEM(neumann.shape, F32),
            pltpu.VMEM(basis.shape, F32),
            pltpu.VMEM(coarse_inverse.shape, F32),
            pltpu.VMEM((count, dofs, 2 * cases), BF16),
            pltpu.VMEM((told_rows, cases), F32),
            pltpu.SemaphoreType.DMA((4,)),
            pltpu.SemaphoreType.DMA,
            pltpu.SemaphoreType.DMA((2,)),
            pltpu.SemaphoreType.DMA((2,)),
            pltpu.SemaphoreType.DMA,
        ],
        compiler_params=kernel_params(16),
        name="local_solve",
    )(*(in_hbm(x) for x in (*indices, residual, neumann, basis, coarse_inverse)))

    same_core = from_all(told, ("y", "col"))
    other_core = lax.ppermute(same_core, "core", [(0, 1), (1, 0)])
    got_2 = swap_pairs(send_2, "col", 0)
    got_3 = swap_pairs(send_3, "col", 1)
    got_1 = swap_pairs(send_1, ("y", "core"), 1)
    got_0 = swap_pairs(send_0, ("y", "core"), 0)

    stacked = pl.pallas_call(
        halving_kernel,
        out_shape=pltpu.VMEM((count, 2 * dofs, 3 * dofs), BF16),
        in_specs=[HBM],
        out_specs=VMEM,
        scratch_shapes=[pltpu.VMEM(schur.shape, F32), pltpu.SemaphoreType.DMA((4,))],
        compiler_params=kernel_params(12),
        name="halving",
    )(in_hbm(schur))

    started, wanted, precond_dot = pl.pallas_call(
        coarse_kernel,
        out_shape=(held(count, dofs, cases), held(32, cases), held(1, cases)),
        in_specs=[SMEM] * 2 + [VMEM] * 5 + [HBM],
        out_specs=(VMEM,) * 3,
        scratch_shapes=[
            pltpu.VMEM((order, order), F32),
            pltpu.VMEM(previous.shape, F32),
            pltpu.SemaphoreType.DMA,
        ],
        compiler_params=kernel_params(24),
        name="coarse_solve",
    )(
        multiplicity, primal_map, local, same_core, other_core, basis, prev_dot.reshape(1, cases),
        in_hbm(previous),
    )

    direction, direction_held, image, send_2, send_3, send_1, send_0, curvature = pl.pallas_call(
        direction_kernel,
        out_shape=(shape(count, dofs, cases), held(count, dofs, cases), held(count, dofs, cases))
        + (held(SLOTS * dofs, cases),) * 4
        + (held(everywhere, cases),),
        in_specs=[SMEM] * 2 + [VMEM] * 7,
        out_specs=(HBM,) + (VMEM,) * 7,
        scratch_shapes=[
            pltpu.VMEM((17, dofs, cases), F32),
            pltpu.VMEM((count, dofs, 2 * cases), BF16),
            pltpu.SMEM((17,), jnp.int32),
            pltpu.SemaphoreType.DMA,
        ],
        compiler_params=kernel_params(16),
        name="direction_image",
    )(faces, pattern, started, wanted, got_2, got_3, got_1, got_0, stacked)

    got_2 = swap_pairs(send_2, "col", 0)
    got_3 = swap_pairs(send_3, "col", 1)
    got_1 = swap_pairs(send_1, ("y", "core"), 1)
    got_0 = swap_pairs(send_0, ("y", "core"), 0)
    curvature = from_all(curvature, ("y", "core", "col"))

    new_solution, new_residual = pl.pallas_call(
        update_kernel,
        out_shape=(shape(count, dofs, cases),) * 2,
        in_specs=[SMEM] + [VMEM] * 10,
        out_specs=(HBM,) * 2,
        scratch_shapes=[
            pltpu.VMEM(residual.shape, F32),
            pltpu.VMEM(residual.shape, F32),
            pltpu.VMEM((17, dofs, cases), F32),
            pltpu.SMEM((17,), jnp.int32),
            pltpu.SemaphoreType.DMA((4,)),
            pltpu.SemaphoreType.DMA((4,)),
        ],
        compiler_params=kernel_params(16),
        name="update",
    )(
        faces, current, residual, direction_held, image, got_2, got_3, got_1, got_0, curvature, precond_dot
    )
    return (new_solution[None, None], new_residual[None, None], direction[None, None])


def solution(mesh):
    rows, cols = mesh.devices.shape
    mesh = jax.sharding.Mesh(mesh.devices.reshape(rows // 2, 2, cols), ("y", "core", "col"))
    split = lambda dims: P(("y", "core"), "col", *(None,) * dims)
    placed = (
        split(3), split(3), split(3), P(), split(2), split(1), split(2), split(4), split(4), split(2), split(1),
        P("col", None),
    )
    return jax.shard_map(
        per_device,
        mesh=mesh,
        in_specs=placed,
        out_specs=(split(3), split(3), split(3)),
        check_vma=False,
    )
```

```python
import jax
import jax.numpy as jnp
from jax import lax
from jax.experimental import pallas as pl
from jax.experimental.pallas import tpu as pltpu
from jax.sharding import PartitionSpec as P

F32 = jnp.float32
BF16 = jnp.bfloat16
SLOTS = 4
HEAD = 10
SMEM = pl.BlockSpec(memory_space=pltpu.SMEM)
VMEM = pl.BlockSpec(memory_space=pltpu.VMEM)
HBM = pl.BlockSpec(memory_space=pltpu.HBM)
ANY = pl.BlockSpec(memory_space=pl.ANY)


def halves(x):
    high = x.astype(BF16)
    return high, (x - high.astype(F32)).astype(BF16)


def dot(a, b):
    return jnp.dot(a, b, preferred_element_type=F32)


def dot_first(a, b):
    return lax.dot_general(a, b, (((0,), (0,)), ((), ())), preferred_element_type=F32)


def fold(x):
    width = x.shape[1] // 2
    return x[:, :width] + x[:, width:]


def product(matrix, pair):
    high, low = halves(matrix)
    return fold(dot(high, pair)) + dot(low, pair[:, : pair.shape[1] // 2])


def exact_pair(x):
    return jnp.concatenate(halves(x), axis=1)


def halved_rows(row_blocks):
    matrix = jnp.concatenate([row_blocks[k] for k in range(3)], axis=1)
    return jnp.concatenate(halves(matrix), axis=0)


def row_product(stacked, pattern, b, pairs):
    field = jnp.concatenate([pairs[pattern[k, 0, b]] for k in range(3)], axis=0)
    both = fold(dot(stacked, field))
    return both[:128] + both[128:]


def partial_rows(x):
    rows, cols = x.shape
    return jnp.sum(x.reshape(rows // 8, 8, cols), axis=0)


def weight_of(multiplicity, b):
    return 1.0 / jnp.full((1, 128), multiplicity[b].astype(F32))


def mapped(primal_map, shape, dim):
    place = lax.broadcasted_iota(jnp.int32, shape, dim)
    found = jnp.zeros(shape, jnp.int32)
    for p in range(8):
        found = jnp.where(place == p, primal_map[p], found)
    return found


def row_index():
    return 2 * lax.axis_index("y") + lax.axis_index("core")


def partner_faces():
    row, col = lax.axis_index("core"), lax.axis_index("col") % 2
    return 1 - row, row, 3 - col, 2 + col


def slots_by_block(faces, slot):
    for b in range(17):
        slot[b] = 16
    for s, f in enumerate(partner_faces()):
        for k in range(SLOTS):
            slot[faces[f, k]] = s * SLOTS + k


def local_kernel(
    faces_hbm, multiplicity_hbm, pattern_hbm, primal_map_hbm, residual_hbm, neumann_hbm, basis_hbm, inverse_hbm,
    local, send_2, told_hbm, send_3, send_1, send_0,
    faces, multiplicity, pattern, primal_map, residual, neumann, basis, inverse, pairs, told,
    index_sems, residual_sem, neumann_sems, basis_sems, told_sem,
):
    count = residual.shape[0]
    index_copies = [
        pltpu.make_async_copy(source, target, index_sems.at[i])
        for i, (source, target) in enumerate(
            ((multiplicity_hbm, multiplicity), (pattern_hbm, pattern), (primal_map_hbm, primal_map), (faces_hbm, faces))
        )
    ]
    basis_copy = pltpu.make_async_copy(basis_hbm, basis, basis_sems.at[0])
    inverse_copy = pltpu.make_async_copy(inverse_hbm, inverse, basis_sems.at[1])
    residual_copy = pltpu.make_async_copy(residual_hbm, residual, residual_sem)
    neumann_copies = {}
    for c, (start, stop) in enumerate(((0, count // 4), (count // 4, count))):
        part = pl.ds(start, stop - start)
        neumann_copies[start] = pltpu.make_async_copy(neumann_hbm.at[part], neumann.at[part], neumann_sems.at[c])
    for copy in (*index_copies, residual_copy, basis_copy, *neumann_copies.values(), inverse_copy):
        copy.start()
    for copy in index_copies:
        copy.wait()
    residual_copy.wait()
    for b in range(count):
        pairs[b] = exact_pair(residual[b] * weight_of(multiplicity, b))
    basis_copy.wait()
    coarse_local = product(basis[...], pairs[...].reshape(count * 128, 256))
    total = jnp.zeros((8, 128), F32)
    for b in range(count):
        if b in neumann_copies:
            neumann_copies[b].wait()
        weight = weight_of(multiplicity, b)
        out = row_product(halved_rows(neumann.at[b]), pattern, b, pairs) * weight
        local[b] = out
        total += partial_rows(residual[b] * out)
    row = lax.broadcasted_iota(jnp.int32, (8, 128), 0)
    total = jnp.sum(total, axis=0, keepdims=True)
    map_row = mapped(primal_map, (8, 128), 1).astype(F32)
    inverse_copy.wait()
    sharers = inverse.shape[0] // 8
    mine = row_index() % sharers
    share = inverse[pl.ds(pl.multiple_of(mine * 8, 8), 8), :]
    rows = [coarse_local, jnp.where(row == 0, total, map_row)[:2]]
    rows = jnp.concatenate(rows + [share[:, i : i + 128] for i in range(0, inverse.shape[1], 128)], axis=0)
    each = rows.shape[0]
    for i in range(told.shape[0] // each):
        told[each * i : each * i + each, :] = rows
    told_copy = pltpu.make_async_copy(told, told_hbm, told_sem)
    told_copy.start()
    for f, sent in zip(partner_faces(), (send_0, send_1, send_2, send_3)):
        for k in range(SLOTS):
            b = jnp.minimum(faces[f, k], count - 1)
            sent[k * 128 : (k + 1) * 128, :] = local[b]
            lanes = pl.ds(pl.multiple_of(b * 128, 128), 128)
            sent[512 + 8 * k : 520 + 8 * k, :] = basis[:, lanes] * weight_of(multiplicity, b)
    told_copy.wait()


def back(basis, own):
    bh, bl = (h.astype(F32) for h in halves(basis))
    oh, ol = (h.astype(F32) for h in halves(own))
    left = jnp.concatenate([bh, bl, bh, bl], axis=0).astype(BF16)
    right = jnp.concatenate([oh, oh, ol, ol], axis=0).astype(BF16)
    return dot_first(left, right)


def halving_kernel(schur_hbm, stacked, schur, sems):
    count = schur.shape[0]
    copies = []
    for c in range(4):
        part = pl.ds(c * count // 4, count // 4)
        copies.append(pltpu.make_async_copy(schur_hbm.at[part], schur.at[part], sems.at[c]))
        copies[c].start()
    for b in range(count):
        if b % (count // 4) == 0:
            copies[b // (count // 4)].wait()
        stacked[b] = halved_rows(schur.at[b])


def coarse_kernel(
    multiplicity, primal_map, local, same_core, other_core, basis, prev_dot, previous_hbm,
    started, wanted, precond_dot, inverse, previous, previous_sem,
):
    count = local.shape[0]
    previous_copy = pltpu.make_async_copy(previous_hbm, previous, previous_sem)
    previous_copy.start()

    order = inverse.shape[1]
    each = HEAD + 8 * (order // 128)
    half = same_core.shape[0] // each
    cols = lax.axis_size("col")
    sharers = order // cols // 8
    for told, core in ((same_core, lax.axis_index("core")), (other_core, 1 - lax.axis_index("core"))):
        for i in range(half):
            target = pl.multiple_of((i % cols * sharers + (2 * (i // cols) + core) % sharers) * 8, 8)
            for j in range(order // 128):
                source = i * each + HEAD + 8 * j
                inverse[pl.ds(target, 8), 128 * j : 128 * j + 128] = told[source : source + 8, :]

    def row_of_all(p):
        return jnp.concatenate([x[pl.ds(p, half, stride=each), :] for x in (same_core, other_core)], axis=0)

    maps = row_of_all(9).astype(jnp.int32)
    lane = lax.broadcasted_iota(jnp.int32, (2 * half, order), 1)
    chosen = [(maps[:, p : p + 1] == lane).astype(F32) for p in range(8)]
    chosen = jnp.concatenate(chosen, axis=0).astype(BF16)
    rows = jnp.concatenate([row_of_all(p) for p in range(8)], axis=0)
    rhs = fold(dot_first(chosen, exact_pair(rows)))
    coarse = product(inverse[...], exact_pair(rhs))
    dots = jnp.sum(row_of_all(8), axis=0, keepdims=True)
    dots = dots + jnp.sum(rhs * coarse, axis=0, keepdims=True)
    precond_dot[...] = dots
    beta = dots / prev_dot[...]
    y, core, col = (lax.axis_index(name) for name in ("y", "core", "col"))
    odd = col % 2
    partners = (
        (other_core, y * cols + col),
        (other_core, jnp.clip(y + 2 * core - 1, 0, lax.axis_size("y") - 1) * cols + col),
        (same_core, y * cols + (col + 1 - 2 * odd)),
        (same_core, y * cols + jnp.clip(col + 2 * odd - 1, 0, cols - 1)),
    )
    map_rows = [x[pl.ds(i * each + 9, 1), :] for x, i in partners]
    map_rows = jnp.concatenate([jnp.broadcast_to(row, (8, 128)) for row in map_rows], axis=0)
    on_diagonal = lax.broadcasted_iota(jnp.int32, (32, 128), 0) % 8 == lax.broadcasted_iota(jnp.int32, (32, 128), 1)
    maps = jnp.sum(jnp.where(on_diagonal, map_rows, 0.0), axis=1, keepdims=True).astype(jnp.int32)
    maps = jnp.concatenate([mapped(primal_map, (8, 128), 0)[:, 0:1], maps], axis=0)
    lane = lax.broadcasted_iota(jnp.int32, (40, order), 1)
    picked = fold(dot((maps == lane).astype(F32).astype(BF16), exact_pair(coarse)))
    wanted[...] = picked[8:40]
    own_back = back(basis[...], picked[0:8])
    previous_copy.wait()
    for b in range(count):
        mine = local[b] + own_back[b * 128 : (b + 1) * 128] * weight_of(multiplicity, b)
        started[b] = mine + beta * previous[b]
def direction_kernel(
    faces_any, pattern_any, started, wanted, got_2, got_3, got_1, got_0, stacked,
    direction_hbm, direction, image, send_2, send_3, send_1, send_0, curvature,
    faces, pattern, added, pairs, slot, index_sems, direction_sem,
):
    count = started.shape[0]
    faces_copy = pltpu.make_async_copy(faces_any, faces, index_sems.at[0])
    pattern_copy = pltpu.make_async_copy(pattern_any, pattern, index_sems.at[1])
    faces_copy.start()
    pattern_copy.start()
    for s, r in enumerate((got_0, got_1, got_2, got_3)):
        face_basis = jnp.concatenate([r[512 + 8 * k : 520 + 8 * k, :] for k in range(SLOTS)], axis=1)
        face_back = back(face_basis, wanted[8 * s : 8 * s + 8, :])
        for k in range(SLOTS):
            part = slice(k * 128, (k + 1) * 128)
            added[s * SLOTS + k] = r[part, :] + face_back[part]
    added[16] = jnp.zeros((128, 128), F32)
    faces_copy.wait()
    pattern_copy.wait()
    slots_by_block(faces, slot)
    for b in range(count):
        value = started[b] + added[slot[b]]
        direction[b] = value
        pairs[b] = exact_pair(value)
    direction_copy = pltpu.make_async_copy(direction, direction_hbm, direction_sem)
    direction_copy.start()
    total = jnp.zeros((8, 128), F32)
    for b in range(count):
        out = row_product(stacked[b], pattern, b, pairs)
        image[b] = out
        total += partial_rows(direction[b] * out)
    for f, sent in zip(partner_faces(), (send_0, send_1, send_2, send_3)):
        for k in range(SLOTS):
            sent[k * 128 : (k + 1) * 128, :] = image[jnp.minimum(faces[f, k], count - 1)]
    curvature[...] = jnp.broadcast_to(jnp.sum(total, axis=0, keepdims=True), curvature.shape)
    direction_copy.wait()


def update_kernel(
    faces_any, current, residual, direction, image, got_2, got_3, got_1, got_0, curvature, precond_dot,
    new_solution_hbm, new_residual_hbm,
    faces, new_solution, new_residual, added, slot, faces_sem, solution_sems, residual_sems,
):
    count = current.shape[0]
    faces_copy = pltpu.make_async_copy(faces_any, faces, faces_sem)
    faces_copy.start()
    step = precond_dot[...] / jnp.sum(curvature[...], axis=0, keepdims=True)
    copies = []

    def leave(c, value, value_hbm, sems):
        part = pl.ds(c * count // 4, count // 4)
        copies.append(pltpu.make_async_copy(value.at[part], value_hbm.at[part], sems.at[c]))
        copies[-1].start()

    for b in range(count):
        new_solution[b] = current[b] + step * direction[b]
        if (b + 1) % (count // 4) == 0:
            leave(b // (count // 4), new_solution, new_solution_hbm, solution_sems)
    for s, r in enumerate((got_0, got_1, got_2, got_3)):
        for k in range(SLOTS):
            added[s * SLOTS + k] = r[k * 128 : (k + 1) * 128, :]
    added[16] = jnp.zeros((128, 128), F32)
    faces_copy.wait()
    slots_by_block(faces, slot)
    for b in range(count):
        new_residual[b] = residual[b] - step * (image[b] + added[slot[b]])
        if (b + 1) % (count // 4) == 0:
            leave(b // (count // 4), new_residual, new_residual_hbm, residual_sems)
    for copy in copies:
        copy.wait()


def swap_pairs(x, axis, first):
    pairs = [(i, i + 1) for i in range(first, lax.axis_size(axis) - 1, 2)]
    return lax.ppermute(x, axis, pairs + [(j, i) for i, j in pairs])


def from_all(x, axes):
    sent = x.reshape(lax.axis_size(axes), 1, -1)
    return lax.all_to_all(sent, axes, split_axis=0, concat_axis=0, tiled=True).reshape(x.shape)


def shape(*dims):
    return jax.ShapeDtypeStruct(dims, F32)


def held(*dims):
    return pltpu.VMEM(dims, F32)


def in_hbm(x):
    return pltpu.with_memory_space_constraint(x, pltpu.HBM)


def kernel_params(mib):
    return pltpu.CompilerParams(vmem_limit_bytes=mib << 20)


def per_device(
    solution,
    residual,
    prev_direction,
    prev_dot,
    face_lists,
    multiplicity,
    block_pattern,
    schur,
    neumann_inverse,
    coarse_basis,
    primal_map,
    coarse_inverse,
):
    current, residual, previous = solution[0, 0], residual[0, 0], prev_direction[0, 0]
    faces, multiplicity = face_lists[0, 0], multiplicity[0, 0]
    pattern = jnp.transpose(block_pattern, (0, 3, 1, 2))[0]
    schur, neumann = schur[0, 0], neumann_inverse[0, 0]
    basis, primal_map = coarse_basis[0, 0], primal_map[0, 0]
    count, dofs, cases = residual.shape

    everywhere = lax.axis_size(("y", "core", "col"))
    order = coarse_inverse.shape[1]
    told_rows = (HEAD + 8 * (order // cases)) * (everywhere // 2)

    face = held(SLOTS * dofs + 32, cases)
    indices = (faces, multiplicity, pattern, primal_map)
    local, send_2, told, send_3, send_1, send_0 = pl.pallas_call(
        local_kernel,
        out_shape=(held(count, dofs, cases), face, shape(told_rows, cases), face, face, face),
        in_specs=[HBM] * 8,
        out_specs=(VMEM, VMEM, HBM, VMEM, VMEM, VMEM),
        scratch_shapes=[pltpu.SMEM(x.shape, jnp.int32) for x in indices]
        + [
            pltpu.VMEM(residual.shape, F32),
            pltpu.VMEM(neumann.shape, F32),
            pltpu.VMEM(basis.shape, F32),
            pltpu.VMEM(coarse_inverse.shape, F32),
            pltpu.VMEM((count, dofs, 2 * cases), BF16),
            pltpu.VMEM((told_rows, cases), F32),
            pltpu.SemaphoreType.DMA((4,)),
            pltpu.SemaphoreType.DMA,
            pltpu.SemaphoreType.DMA((2,)),
            pltpu.SemaphoreType.DMA((2,)),
            pltpu.SemaphoreType.DMA,
        ],
        compiler_params=kernel_params(16),
        name="local_solve",
    )(*(in_hbm(x) for x in (*indices, residual, neumann, basis, coarse_inverse)))

    same_core = from_all(told, ("y", "col"))
    other_core = lax.ppermute(same_core, "core", [(0, 1), (1, 0)])
    got_2 = swap_pairs(send_2, "col", 0)
    got_3 = swap_pairs(send_3, "col", 1)
    got_1 = swap_pairs(send_1, ("y", "core"), 1)
    got_0 = swap_pairs(send_0, ("y", "core"), 0)

    stacked = pl.pallas_call(
        halving_kernel,
        out_shape=pltpu.VMEM((count, 2 * dofs, 3 * dofs), BF16),
        in_specs=[HBM],
        out_specs=VMEM,
        scratch_shapes=[pltpu.VMEM(schur.shape, F32), pltpu.SemaphoreType.DMA((4,))],
        compiler_params=kernel_params(12),
        name="halving",
    )(in_hbm(schur))

    started, wanted, precond_dot = pl.pallas_call(
        coarse_kernel,
        out_shape=(held(count, dofs, cases), held(32, cases), held(1, cases)),
        in_specs=[SMEM] * 2 + [VMEM] * 5 + [HBM],
        out_specs=(VMEM,) * 3,
        scratch_shapes=[
            pltpu.VMEM((order, order), F32),
            pltpu.VMEM(previous.shape, F32),
            pltpu.SemaphoreType.DMA,
        ],
        compiler_params=kernel_params(24),
        name="coarse_solve",
    )(
        multiplicity, primal_map, local, same_core, other_core, basis, prev_dot.reshape(1, cases),
        in_hbm(previous),
    )

    direction, direction_held, image, send_2, send_3, send_1, send_0, curvature = pl.pallas_call(
        direction_kernel,
        out_shape=(shape(count, dofs, cases), held(count, dofs, cases), held(count, dofs, cases))
        + (held(SLOTS * dofs, cases),) * 4
        + (held(everywhere, cases),),
        in_specs=[ANY] * 2 + [VMEM] * 7,
        out_specs=(HBM,) + (VMEM,) * 7,
        scratch_shapes=[
            pltpu.SMEM(faces.shape, jnp.int32),
            pltpu.SMEM(pattern.shape, jnp.int32),
            pltpu.VMEM((17, dofs, cases), F32),
            pltpu.VMEM((count, dofs, 2 * cases), BF16),
            pltpu.SMEM((17,), jnp.int32),
            pltpu.SemaphoreType.DMA((2,)),
            pltpu.SemaphoreType.DMA,
        ],
        compiler_params=kernel_params(16),
        name="direction_image",
    )(faces, pattern, started, wanted, got_2, got_3, got_1, got_0, stacked)

    got_2 = swap_pairs(send_2, "col", 0)
    got_3 = swap_pairs(send_3, "col", 1)
    got_1 = swap_pairs(send_1, ("y", "core"), 1)
    got_0 = swap_pairs(send_0, ("y", "core"), 0)
    curvature = from_all(curvature, ("y", "core", "col"))

    new_solution, new_residual = pl.pallas_call(
        update_kernel,
        out_shape=(shape(count, dofs, cases),) * 2,
        in_specs=[ANY] + [VMEM] * 10,
        out_specs=(HBM,) * 2,
        scratch_shapes=[
            pltpu.SMEM(faces.shape, jnp.int32),
            pltpu.VMEM(residual.shape, F32),
            pltpu.VMEM(residual.shape, F32),
            pltpu.VMEM((17, dofs, cases), F32),
            pltpu.SMEM((17,), jnp.int32),
            pltpu.SemaphoreType.DMA,
            pltpu.SemaphoreType.DMA((4,)),
            pltpu.SemaphoreType.DMA((4,)),
        ],
        compiler_params=kernel_params(16),
        name="update",
    )(
        faces, current, residual, direction_held, image, got_2, got_3, got_1, got_0, curvature, precond_dot
    )
    return (new_solution[None, None], new_residual[None, None], direction[None, None])


def solution(mesh):
    rows, cols = mesh.devices.shape
    mesh = jax.sharding.Mesh(mesh.devices.reshape(rows // 2, 2, cols), ("y", "core", "col"))
    split = lambda dims: P(("y", "core"), "col", *(None,) * dims)
    placed = (
        split(3), split(3), split(3), P(), split(2), split(1), split(2), split(4), split(4), split(2), split(1),
        P("col", None),
    )
    return jax.shard_map(
        per_device,
        mesh=mesh,
        in_specs=placed,
        out_specs=(split(3), split(3), split(3)),
        check_vma=False,
    )
```

```python
import jax
import jax.numpy as jnp
from jax import lax
from jax.experimental import pallas as pl
from jax.experimental.pallas import tpu as pltpu
from jax.sharding import PartitionSpec as P

F32 = jnp.float32
BF16 = jnp.bfloat16
SLOTS = 4
HEAD = 10
SMEM = pl.BlockSpec(memory_space=pltpu.SMEM)
VMEM = pl.BlockSpec(memory_space=pltpu.VMEM)
HBM = pl.BlockSpec(memory_space=pltpu.HBM)
ANY = pl.BlockSpec(memory_space=pl.ANY)


def halves(x):
    high = x.astype(BF16)
    return high, (x - high.astype(F32)).astype(BF16)


def dot(a, b):
    return jnp.dot(a, b, preferred_element_type=F32)


def dot_first(a, b):
    return lax.dot_general(a, b, (((0,), (0,)), ((), ())), preferred_element_type=F32)


def fold(x):
    width = x.shape[1] // 2
    return x[:, :width] + x[:, width:]


def product(matrix, pair):
    high, low = halves(matrix)
    return fold(dot(high, pair)) + dot(low, pair[:, : pair.shape[1] // 2])


def exact_pair(x):
    return jnp.concatenate(halves(x), axis=1)


def halved_rows(row_blocks):
    matrix = jnp.concatenate([row_blocks[k] for k in range(3)], axis=1)
    return jnp.concatenate(halves(matrix), axis=0)


def row_product(stacked, pattern, b, pairs):
    field = jnp.concatenate([pairs[pattern[k, 0, b]] for k in range(3)], axis=0)
    both = fold(dot(stacked, field))
    return both[:128] + both[128:]


def partial_rows(x):
    rows, cols = x.shape
    return jnp.sum(x.reshape(rows // 8, 8, cols), axis=0)


def weight_of(multiplicity, b):
    return 1.0 / jnp.full((1, 128), multiplicity[b].astype(F32))


def mapped(primal_map, shape, dim):
    place = lax.broadcasted_iota(jnp.int32, shape, dim)
    found = jnp.zeros(shape, jnp.int32)
    for p in range(8):
        found = jnp.where(place == p, primal_map[p], found)
    return found


def row_index():
    return 2 * lax.axis_index("y") + lax.axis_index("core")


def partner_faces():
    row, col = lax.axis_index("core"), lax.axis_index("col") % 2
    return 1 - row, row, 3 - col, 2 + col


def slots_by_block(faces, slot):
    for b in range(17):
        slot[b] = 16
    for s, f in enumerate(partner_faces()):
        for k in range(SLOTS):
            slot[faces[f, k]] = s * SLOTS + k


def local_kernel(
    faces_hbm, multiplicity_hbm, pattern_hbm, primal_map_hbm, residual_hbm, neumann_hbm, basis_hbm, inverse_hbm,
    local, send_2, told_hbm, send_3, send_1, send_0,
    faces, multiplicity, pattern, primal_map, residual, neumann, basis, inverse, pairs, told,
    index_sems, residual_sem, neumann_sems, basis_sems, told_sem,
):
    count = residual.shape[0]
    index_copies = [
        pltpu.make_async_copy(source, target, index_sems.at[i])
        for i, (source, target) in enumerate(
            ((multiplicity_hbm, multiplicity), (pattern_hbm, pattern), (primal_map_hbm, primal_map), (faces_hbm, faces))
        )
    ]
    basis_copy = pltpu.make_async_copy(basis_hbm, basis, basis_sems.at[0])
    inverse_copy = pltpu.make_async_copy(inverse_hbm, inverse, basis_sems.at[1])
    residual_copy = pltpu.make_async_copy(residual_hbm, residual, residual_sem)
    neumann_copies = {}
    for c, (start, stop) in enumerate(((0, count // 4), (count // 4, count))):
        part = pl.ds(start, stop - start)
        neumann_copies[start] = pltpu.make_async_copy(neumann_hbm.at[part], neumann.at[part], neumann_sems.at[c])
    for copy in (*index_copies, residual_copy, basis_copy, *neumann_copies.values(), inverse_copy):
        copy.start()
    for copy in index_copies:
        copy.wait()
    residual_copy.wait()
    basis_copy.wait()
    for b in range(count):
        pairs[b] = exact_pair(residual[b] * weight_of(multiplicity, b))
    total = jnp.zeros((8, 128), F32)
    for b in range(count):
        if b in neumann_copies:
            neumann_copies[b].wait()
        if b == count // 4:
            coarse_local = product(basis[...], pairs[...].reshape(count * 128, 256))
        weight = weight_of(multiplicity, b)
        out = row_product(halved_rows(neumann.at[b]), pattern, b, pairs) * weight
        local[b] = out
        total += partial_rows(residual[b] * out)
    row = lax.broadcasted_iota(jnp.int32, (8, 128), 0)
    total = jnp.sum(total, axis=0, keepdims=True)
    map_row = mapped(primal_map, (8, 128), 1).astype(F32)
    inverse_copy.wait()
    sharers = inverse.shape[0] // 8
    mine = row_index() % sharers
    share = inverse[pl.ds(pl.multiple_of(mine * 8, 8), 8), :]
    rows = [coarse_local, jnp.where(row == 0, total, map_row)[:2]]
    rows = jnp.concatenate(rows + [share[:, i : i + 128] for i in range(0, inverse.shape[1], 128)], axis=0)
    each = rows.shape[0]
    for i in range(told.shape[0] // each):
        told[each * i : each * i + each, :] = rows
    told_copy = pltpu.make_async_copy(told, told_hbm, told_sem)
    told_copy.start()
    for f, sent in zip(partner_faces(), (send_0, send_1, send_2, send_3)):
        for k in range(SLOTS):
            b = jnp.minimum(faces[f, k], count - 1)
            sent[k * 128 : (k + 1) * 128, :] = local[b]
            lanes = pl.ds(pl.multiple_of(b * 128, 128), 128)
            sent[512 + 8 * k : 520 + 8 * k, :] = basis[:, lanes] * weight_of(multiplicity, b)
    told_copy.wait()


def back(basis, own):
    bh, bl = (h.astype(F32) for h in halves(basis))
    oh, ol = (h.astype(F32) for h in halves(own))
    left = jnp.concatenate([bh, bl, bh, bl], axis=0).astype(BF16)
    right = jnp.concatenate([oh, oh, ol, ol], axis=0).astype(BF16)
    return dot_first(left, right)


def halving_kernel(schur_hbm, stacked, schur, sems):
    count = schur.shape[0]
    copies = []
    for c in range(4):
        part = pl.ds(c * count // 4, count // 4)
        copies.append(pltpu.make_async_copy(schur_hbm.at[part], schur.at[part], sems.at[c]))
        copies[c].start()
    for b in range(count):
        if b % (count // 4) == 0:
            copies[b // (count // 4)].wait()
        stacked[b] = halved_rows(schur.at[b])


def coarse_kernel(
    multiplicity, primal_map, local, same_core, other_core, basis, prev_dot, previous_hbm,
    started, wanted, precond_dot, inverse, previous, previous_sem,
):
    count = local.shape[0]
    previous_copy = pltpu.make_async_copy(previous_hbm, previous, previous_sem)
    previous_copy.start()

    order = inverse.shape[1]
    each = HEAD + 8 * (order // 128)
    half = same_core.shape[0] // each
    cols = lax.axis_size("col")
    sharers = order // cols // 8
    for told, core in ((same_core, lax.axis_index("core")), (other_core, 1 - lax.axis_index("core"))):
        for i in range(half):
            target = pl.multiple_of((i % cols * sharers + (2 * (i // cols) + core) % sharers) * 8, 8)
            for j in range(order // 128):
                source = i * each + HEAD + 8 * j
                inverse[pl.ds(target, 8), 128 * j : 128 * j + 128] = told[source : source + 8, :]

    def row_of_all(p):
        return jnp.concatenate([x[pl.ds(p, half, stride=each), :] for x in (same_core, other_core)], axis=0)

    maps = row_of_all(9).astype(jnp.int32)
    lane = lax.broadcasted_iota(jnp.int32, (2 * half, order), 1)
    chosen = [(maps[:, p : p + 1] == lane).astype(F32) for p in range(8)]
    chosen = jnp.concatenate(chosen, axis=0).astype(BF16)
    rows = jnp.concatenate([row_of_all(p) for p in range(8)], axis=0)
    rhs = fold(dot_first(chosen, exact_pair(rows)))
    coarse = product(inverse[...], exact_pair(rhs))
    dots = jnp.sum(row_of_all(8), axis=0, keepdims=True)
    dots = dots + jnp.sum(rhs * coarse, axis=0, keepdims=True)
    precond_dot[...] = dots
    beta = dots / prev_dot[...]
    y, core, col = (lax.axis_index(name) for name in ("y", "core", "col"))
    odd = col % 2
    partners = (
        (other_core, y * cols + col),
        (other_core, jnp.clip(y + 2 * core - 1, 0, lax.axis_size("y") - 1) * cols + col),
        (same_core, y * cols + (col + 1 - 2 * odd)),
        (same_core, y * cols + jnp.clip(col + 2 * odd - 1, 0, cols - 1)),
    )
    map_rows = [x[pl.ds(i * each + 9, 1), :] for x, i in partners]
    map_rows = jnp.concatenate([jnp.broadcast_to(row, (8, 128)) for row in map_rows], axis=0)
    on_diagonal = lax.broadcasted_iota(jnp.int32, (32, 128), 0) % 8 == lax.broadcasted_iota(jnp.int32, (32, 128), 1)
    maps = jnp.sum(jnp.where(on_diagonal, map_rows, 0.0), axis=1, keepdims=True).astype(jnp.int32)
    maps = jnp.concatenate([mapped(primal_map, (8, 128), 0)[:, 0:1], maps], axis=0)
    lane = lax.broadcasted_iota(jnp.int32, (40, order), 1)
    picked = fold(dot((maps == lane).astype(F32).astype(BF16), exact_pair(coarse)))
    wanted[...] = picked[8:40]
    own_back = back(basis[...], picked[0:8])
    previous_copy.wait()
    for b in range(count):
        mine = local[b] + own_back[b * 128 : (b + 1) * 128] * weight_of(multiplicity, b)
        started[b] = mine + beta * previous[b]
def direction_kernel(
    faces, pattern, started, wanted, got_2, got_3, got_1, got_0, stacked,
    direction_hbm, direction, image, send_2, send_3, send_1, send_0, curvature,
    added, pairs, slot, direction_sem,
):
    count = started.shape[0]
    slots_by_block(faces, slot)
    for s, r in enumerate((got_0, got_1, got_2, got_3)):
        face_basis = jnp.concatenate([r[512 + 8 * k : 520 + 8 * k, :] for k in range(SLOTS)], axis=1)
        face_back = back(face_basis, wanted[8 * s : 8 * s + 8, :])
        for k in range(SLOTS):
            part = slice(k * 128, (k + 1) * 128)
            added[s * SLOTS + k] = r[part, :] + face_back[part]
    added[16] = jnp.zeros((128, 128), F32)
    for b in range(count):
        value = started[b] + added[slot[b]]
        direction[b] = value
        pairs[b] = exact_pair(value)
    direction_copy = pltpu.make_async_copy(direction, direction_hbm, direction_sem)
    direction_copy.start()
    total = jnp.zeros((8, 128), F32)
    for b in range(count):
        out = row_product(stacked[b], pattern, b, pairs)
        image[b] = out
        total += partial_rows(direction[b] * out)
    for f, sent in zip(partner_faces(), (send_0, send_1, send_2, send_3)):
        for k in range(SLOTS):
            sent[k * 128 : (k + 1) * 128, :] = image[jnp.minimum(faces[f, k], count - 1)]
    curvature[...] = jnp.broadcast_to(jnp.sum(total, axis=0, keepdims=True), curvature.shape)
    direction_copy.wait()


def update_kernel(
    faces_any, current, residual, direction, image, got_2, got_3, got_1, got_0, curvature, precond_dot,
    new_solution_hbm, new_residual_hbm,
    faces, new_solution, new_residual, added, slot, faces_sem, solution_sems, residual_sems,
):
    count = current.shape[0]
    faces_copy = pltpu.make_async_copy(faces_any, faces, faces_sem)
    faces_copy.start()
    step = precond_dot[...] / jnp.sum(curvature[...], axis=0, keepdims=True)
    copies = []

    def leave(c, value, value_hbm, sems):
        part = pl.ds(c * count // 4, count // 4)
        copies.append(pltpu.make_async_copy(value.at[part], value_hbm.at[part], sems.at[c]))
        copies[-1].start()

    for b in range(count):
        new_solution[b] = current[b] + step * direction[b]
        if (b + 1) % (count // 4) == 0:
            leave(b // (count // 4), new_solution, new_solution_hbm, solution_sems)
    for s, r in enumerate((got_0, got_1, got_2, got_3)):
        for k in range(SLOTS):
            added[s * SLOTS + k] = r[k * 128 : (k + 1) * 128, :]
    added[16] = jnp.zeros((128, 128), F32)
    faces_copy.wait()
    slots_by_block(faces, slot)
    for b in range(count):
        new_residual[b] = residual[b] - step * (image[b] + added[slot[b]])
        if (b + 1) % (count // 4) == 0:
            leave(b // (count // 4), new_residual, new_residual_hbm, residual_sems)
    for copy in copies:
        copy.wait()


def swap_pairs(x, axis, first):
    pairs = [(i, i + 1) for i in range(first, lax.axis_size(axis) - 1, 2)]
    return lax.ppermute(x, axis, pairs + [(j, i) for i, j in pairs])


def from_all(x, axes):
    sent = x.reshape(lax.axis_size(axes), 1, -1)
    return lax.all_to_all(sent, axes, split_axis=0, concat_axis=0, tiled=True).reshape(x.shape)


def shape(*dims):
    return jax.ShapeDtypeStruct(dims, F32)


def held(*dims):
    return pltpu.VMEM(dims, F32)


def in_hbm(x):
    return pltpu.with_memory_space_constraint(x, pltpu.HBM)


def kernel_params(mib):
    return pltpu.CompilerParams(vmem_limit_bytes=mib << 20)


def per_device(
    solution,
    residual,
    prev_direction,
    prev_dot,
    face_lists,
    multiplicity,
    block_pattern,
    schur,
    neumann_inverse,
    coarse_basis,
    primal_map,
    coarse_inverse,
):
    current, residual, previous = solution[0, 0], residual[0, 0], prev_direction[0, 0]
    faces, multiplicity = face_lists[0, 0], multiplicity[0, 0]
    pattern = jnp.transpose(block_pattern, (0, 3, 1, 2))[0]
    schur, neumann = schur[0, 0], neumann_inverse[0, 0]
    basis, primal_map = coarse_basis[0, 0], primal_map[0, 0]
    count, dofs, cases = residual.shape

    everywhere = lax.axis_size(("y", "core", "col"))
    order = coarse_inverse.shape[1]
    told_rows = (HEAD + 8 * (order // cases)) * (everywhere // 2)

    face = held(SLOTS * dofs + 32, cases)
    indices = (faces, multiplicity, pattern, primal_map)
    local, send_2, told, send_3, send_1, send_0 = pl.pallas_call(
        local_kernel,
        out_shape=(held(count, dofs, cases), face, shape(told_rows, cases), face, face, face),
        in_specs=[HBM] * 8,
        out_specs=(VMEM, VMEM, HBM, VMEM, VMEM, VMEM),
        scratch_shapes=[pltpu.SMEM(x.shape, jnp.int32) for x in indices]
        + [
            pltpu.VMEM(residual.shape, F32),
            pltpu.VMEM(neumann.shape, F32),
            pltpu.VMEM(basis.shape, F32),
            pltpu.VMEM(coarse_inverse.shape, F32),
            pltpu.VMEM((count, dofs, 2 * cases), BF16),
            pltpu.VMEM((told_rows, cases), F32),
            pltpu.SemaphoreType.DMA((4,)),
            pltpu.SemaphoreType.DMA,
            pltpu.SemaphoreType.DMA((2,)),
            pltpu.SemaphoreType.DMA((2,)),
            pltpu.SemaphoreType.DMA,
        ],
        compiler_params=kernel_params(16),
        name="local_solve",
    )(*(in_hbm(x) for x in (*indices, residual, neumann, basis, coarse_inverse)))

    same_core = from_all(told, ("y", "col"))
    other_core = lax.ppermute(same_core, "core", [(0, 1), (1, 0)])
    got_2 = swap_pairs(send_2, "col", 0)
    got_3 = swap_pairs(send_3, "col", 1)
    got_1 = swap_pairs(send_1, ("y", "core"), 1)
    got_0 = swap_pairs(send_0, ("y", "core"), 0)

    stacked = pl.pallas_call(
        halving_kernel,
        out_shape=pltpu.VMEM((count, 2 * dofs, 3 * dofs), BF16),
        in_specs=[HBM],
        out_specs=VMEM,
        scratch_shapes=[pltpu.VMEM(schur.shape, F32), pltpu.SemaphoreType.DMA((4,))],
        compiler_params=kernel_params(12),
        name="halving",
    )(in_hbm(schur))

    started, wanted, precond_dot = pl.pallas_call(
        coarse_kernel,
        out_shape=(held(count, dofs, cases), held(32, cases), held(1, cases)),
        in_specs=[SMEM] * 2 + [VMEM] * 5 + [HBM],
        out_specs=(VMEM,) * 3,
        scratch_shapes=[
            pltpu.VMEM((order, order), F32),
            pltpu.VMEM(previous.shape, F32),
            pltpu.SemaphoreType.DMA,
        ],
        compiler_params=kernel_params(24),
        name="coarse_solve",
    )(
        multiplicity, primal_map, local, same_core, other_core, basis, prev_dot.reshape(1, cases),
        in_hbm(previous),
    )

    direction, direction_held, image, send_2, send_3, send_1, send_0, curvature = pl.pallas_call(
        direction_kernel,
        out_shape=(shape(count, dofs, cases), held(count, dofs, cases), held(count, dofs, cases))
        + (held(SLOTS * dofs, cases),) * 4
        + (held(everywhere, cases),),
        in_specs=[SMEM] * 2 + [VMEM] * 7,
        out_specs=(HBM,) + (VMEM,) * 7,
        scratch_shapes=[
            pltpu.VMEM((17, dofs, cases), F32),
            pltpu.VMEM((count, dofs, 2 * cases), BF16),
            pltpu.SMEM((17,), jnp.int32),
            pltpu.SemaphoreType.DMA,
        ],
        compiler_params=kernel_params(16),
        name="direction_image",
    )(faces, pattern, started, wanted, got_2, got_3, got_1, got_0, stacked)

    got_2 = swap_pairs(send_2, "col", 0)
    got_3 = swap_pairs(send_3, "col", 1)
    got_1 = swap_pairs(send_1, ("y", "core"), 1)
    got_0 = swap_pairs(send_0, ("y", "core"), 0)
    curvature = from_all(curvature, ("y", "core", "col"))

    new_solution, new_residual = pl.pallas_call(
        update_kernel,
        out_shape=(shape(count, dofs, cases),) * 2,
        in_specs=[ANY] + [VMEM] * 10,
        out_specs=(HBM,) * 2,
        scratch_shapes=[
            pltpu.SMEM(faces.shape, jnp.int32),
            pltpu.VMEM(residual.shape, F32),
            pltpu.VMEM(residual.shape, F32),
            pltpu.VMEM((17, dofs, cases), F32),
            pltpu.SMEM((17,), jnp.int32),
            pltpu.SemaphoreType.DMA,
            pltpu.SemaphoreType.DMA((4,)),
            pltpu.SemaphoreType.DMA((4,)),
        ],
        compiler_params=kernel_params(16),
        name="update",
    )(
        faces, current, residual, direction_held, image, got_2, got_3, got_1, got_0, curvature, precond_dot
    )
    return (new_solution[None, None], new_residual[None, None], direction[None, None])


def solution(mesh):
    rows, cols = mesh.devices.shape
    mesh = jax.sharding.Mesh(mesh.devices.reshape(rows // 2, 2, cols), ("y", "core", "col"))
    split = lambda dims: P(("y", "core"), "col", *(None,) * dims)
    placed = (
        split(3), split(3), split(3), P(), split(2), split(1), split(2), split(4), split(4), split(2), split(1),
        P("col", None),
    )
    return jax.shard_map(
        per_device,
        mesh=mesh,
        in_specs=placed,
        out_specs=(split(3), split(3), split(3)),
        check_vma=False,
    )
```

```python
import jax
import jax.numpy as jnp
from jax import lax
from jax.experimental import pallas as pl
from jax.experimental.pallas import tpu as pltpu
from jax.sharding import PartitionSpec as P

F32 = jnp.float32
BF16 = jnp.bfloat16
SLOTS = 4
HEAD = 10
SMEM = pl.BlockSpec(memory_space=pltpu.SMEM)
VMEM = pl.BlockSpec(memory_space=pltpu.VMEM)
HBM = pl.BlockSpec(memory_space=pltpu.HBM)
ANY = pl.BlockSpec(memory_space=pl.ANY)


def halves(x):
    high = x.astype(BF16)
    return high, (x - high.astype(F32)).astype(BF16)


def dot(a, b):
    return jnp.dot(a, b, preferred_element_type=F32)


def dot_first(a, b):
    return lax.dot_general(a, b, (((0,), (0,)), ((), ())), preferred_element_type=F32)


def fold(x):
    width = x.shape[1] // 2
    return x[:, :width] + x[:, width:]


def product(matrix, pair):
    high, low = halves(matrix)
    return fold(dot(high, pair)) + dot(low, pair[:, : pair.shape[1] // 2])


def exact_pair(x):
    return jnp.concatenate(halves(x), axis=1)


def halved_rows(row_blocks):
    matrix = jnp.concatenate([row_blocks[k] for k in range(3)], axis=1)
    return jnp.concatenate(halves(matrix), axis=0)


def row_product(stacked, pattern, b, pairs):
    field = jnp.concatenate([pairs[pattern[k, 0, b]] for k in range(3)], axis=0)
    both = fold(dot(stacked, field))
    return both[:128] + both[128:]


def partial_rows(x):
    rows, cols = x.shape
    return jnp.sum(x.reshape(rows // 8, 8, cols), axis=0)


def weight_of(multiplicity, b):
    return 1.0 / jnp.full((1, 128), multiplicity[b].astype(F32))


def mapped(primal_map, shape, dim):
    place = lax.broadcasted_iota(jnp.int32, shape, dim)
    found = jnp.zeros(shape, jnp.int32)
    for p in range(8):
        found = jnp.where(place == p, primal_map[p], found)
    return found


def row_index():
    return 2 * lax.axis_index("y") + lax.axis_index("core")


def partner_faces():
    row, col = lax.axis_index("core"), lax.axis_index("col") % 2
    return 1 - row, row, 3 - col, 2 + col


def slots_by_block(faces, slot):
    for b in range(17):
        slot[b] = 16
    for s, f in enumerate(partner_faces()):
        for k in range(SLOTS):
            slot[faces[f, k]] = s * SLOTS + k


def local_kernel(
    faces_hbm, multiplicity_hbm, pattern_hbm, primal_map_hbm, residual_hbm, neumann_hbm, basis_hbm, inverse_hbm,
    local, send_3, told_hbm, send_2, send_1, send_0,
    faces, multiplicity, pattern, primal_map, residual, neumann, basis, inverse, pairs, told,
    index_sems, residual_sem, neumann_sems, basis_sems, told_sem,
):
    count = residual.shape[0]
    index_copies = [
        pltpu.make_async_copy(source, target, index_sems.at[i])
        for i, (source, target) in enumerate(
            ((multiplicity_hbm, multiplicity), (pattern_hbm, pattern), (primal_map_hbm, primal_map), (faces_hbm, faces))
        )
    ]
    basis_copy = pltpu.make_async_copy(basis_hbm, basis, basis_sems.at[0])
    inverse_copy = pltpu.make_async_copy(inverse_hbm, inverse, basis_sems.at[1])
    residual_copy = pltpu.make_async_copy(residual_hbm, residual, residual_sem)
    neumann_copies = {}
    for c, (start, stop) in enumerate(((0, count // 4), (count // 4, count))):
        part = pl.ds(start, stop - start)
        neumann_copies[start] = pltpu.make_async_copy(neumann_hbm.at[part], neumann.at[part], neumann_sems.at[c])
    for copy in (*index_copies, residual_copy, basis_copy, *neumann_copies.values(), inverse_copy):
        copy.start()
    for copy in index_copies:
        copy.wait()
    residual_copy.wait()
    basis_copy.wait()
    for b in range(count):
        pairs[b] = exact_pair(residual[b] * weight_of(multiplicity, b))
    total = jnp.zeros((8, 128), F32)
    for b in range(count):
        if b in neumann_copies:
            neumann_copies[b].wait()
        if b == count // 4:
            coarse_local = product(basis[...], pairs[...].reshape(count * 128, 256))
        weight = weight_of(multiplicity, b)
        out = row_product(halved_rows(neumann.at[b]), pattern, b, pairs) * weight
        local[b] = out
        total += partial_rows(residual[b] * out)
    row = lax.broadcasted_iota(jnp.int32, (8, 128), 0)
    total = jnp.sum(total, axis=0, keepdims=True)
    map_row = mapped(primal_map, (8, 128), 1).astype(F32)
    inverse_copy.wait()
    sharers = inverse.shape[0] // 8
    mine = row_index() % sharers
    share = inverse[pl.ds(pl.multiple_of(mine * 8, 8), 8), :]
    rows = [coarse_local, jnp.where(row == 0, total, map_row)[:2]]
    rows = jnp.concatenate(rows + [share[:, i : i + 128] for i in range(0, inverse.shape[1], 128)], axis=0)
    each = rows.shape[0]
    for i in range(told.shape[0] // each):
        told[each * i : each * i + each, :] = rows
    told_copy = pltpu.make_async_copy(told, told_hbm, told_sem)
    told_copy.start()
    for f, sent in zip(partner_faces(), (send_0, send_1, send_2, send_3)):
        for k in range(SLOTS):
            b = jnp.minimum(faces[f, k], count - 1)
            sent[k * 128 : (k + 1) * 128, :] = local[b]
            lanes = pl.ds(pl.multiple_of(b * 128, 128), 128)
            sent[512 + 8 * k : 520 + 8 * k, :] = basis[:, lanes] * weight_of(multiplicity, b)
    told_copy.wait()


def back(basis, own):
    bh, bl = (h.astype(F32) for h in halves(basis))
    oh, ol = (h.astype(F32) for h in halves(own))
    left = jnp.concatenate([bh, bl, bh, bl], axis=0).astype(BF16)
    right = jnp.concatenate([oh, oh, ol, ol], axis=0).astype(BF16)
    return dot_first(left, right)


def halving_kernel(schur_hbm, stacked, schur, sems):
    count = schur.shape[0]
    copies = []
    for c in range(4):
        part = pl.ds(c * count // 4, count // 4)
        copies.append(pltpu.make_async_copy(schur_hbm.at[part], schur.at[part], sems.at[c]))
        copies[c].start()
    for b in range(count):
        if b % (count // 4) == 0:
            copies[b // (count // 4)].wait()
        stacked[b] = halved_rows(schur.at[b])


def coarse_kernel(
    multiplicity, primal_map, local, same_core, other_core, basis, prev_dot, previous_hbm,
    started, wanted, precond_dot, inverse, previous, previous_sem,
):
    count = local.shape[0]
    previous_copy = pltpu.make_async_copy(previous_hbm, previous, previous_sem)
    previous_copy.start()

    order = inverse.shape[1]
    each = HEAD + 8 * (order // 128)
    half = same_core.shape[0] // each
    cols = lax.axis_size("col")
    sharers = order // cols // 8
    for told, core in ((same_core, lax.axis_index("core")), (other_core, 1 - lax.axis_index("core"))):
        for i in range(half):
            target = pl.multiple_of((i % cols * sharers + (2 * (i // cols) + core) % sharers) * 8, 8)
            for j in range(order // 128):
                source = i * each + HEAD + 8 * j
                inverse[pl.ds(target, 8), 128 * j : 128 * j + 128] = told[source : source + 8, :]

    def row_of_all(p):
        return jnp.concatenate([x[pl.ds(p, half, stride=each), :] for x in (same_core, other_core)], axis=0)

    maps = row_of_all(9).astype(jnp.int32)
    lane = lax.broadcasted_iota(jnp.int32, (2 * half, order), 1)
    chosen = [(maps[:, p : p + 1] == lane).astype(F32) for p in range(8)]
    chosen = jnp.concatenate(chosen, axis=0).astype(BF16)
    rows = jnp.concatenate([row_of_all(p) for p in range(8)], axis=0)
    rhs = fold(dot_first(chosen, exact_pair(rows)))
    coarse = product(inverse[...], exact_pair(rhs))
    dots = jnp.sum(row_of_all(8), axis=0, keepdims=True)
    dots = dots + jnp.sum(rhs * coarse, axis=0, keepdims=True)
    precond_dot[...] = dots
    beta = dots / prev_dot[...]
    y, core, col = (lax.axis_index(name) for name in ("y", "core", "col"))
    odd = col % 2
    partners = (
        (other_core, y * cols + col),
        (other_core, jnp.clip(y + 2 * core - 1, 0, lax.axis_size("y") - 1) * cols + col),
        (same_core, y * cols + (col + 1 - 2 * odd)),
        (same_core, y * cols + jnp.clip(col + 2 * odd - 1, 0, cols - 1)),
    )
    map_rows = [x[pl.ds(i * each + 9, 1), :] for x, i in partners]
    map_rows = jnp.concatenate([jnp.broadcast_to(row, (8, 128)) for row in map_rows], axis=0)
    on_diagonal = lax.broadcasted_iota(jnp.int32, (32, 128), 0) % 8 == lax.broadcasted_iota(jnp.int32, (32, 128), 1)
    maps = jnp.sum(jnp.where(on_diagonal, map_rows, 0.0), axis=1, keepdims=True).astype(jnp.int32)
    maps = jnp.concatenate([mapped(primal_map, (8, 128), 0)[:, 0:1], maps], axis=0)
    lane = lax.broadcasted_iota(jnp.int32, (40, order), 1)
    picked = fold(dot((maps == lane).astype(F32).astype(BF16), exact_pair(coarse)))
    wanted[...] = picked[8:40]
    own_back = back(basis[...], picked[0:8])
    previous_copy.wait()
    for b in range(count):
        mine = local[b] + own_back[b * 128 : (b + 1) * 128] * weight_of(multiplicity, b)
        started[b] = mine + beta * previous[b]
def direction_kernel(
    faces, pattern, started, wanted, got_3, got_2, got_1, got_0, stacked,
    direction_hbm, direction, image, send_3, send_2, send_1, send_0, curvature,
    added, pairs, slot, direction_sem,
):
    count = started.shape[0]
    slots_by_block(faces, slot)
    for s, r in enumerate((got_0, got_1, got_2, got_3)):
        face_basis = jnp.concatenate([r[512 + 8 * k : 520 + 8 * k, :] for k in range(SLOTS)], axis=1)
        face_back = back(face_basis, wanted[8 * s : 8 * s + 8, :])
        for k in range(SLOTS):
            part = slice(k * 128, (k + 1) * 128)
            added[s * SLOTS + k] = r[part, :] + face_back[part]
    added[16] = jnp.zeros((128, 128), F32)
    for b in range(count):
        value = started[b] + added[slot[b]]
        direction[b] = value
        pairs[b] = exact_pair(value)
    direction_copy = pltpu.make_async_copy(direction, direction_hbm, direction_sem)
    direction_copy.start()
    total = jnp.zeros((8, 128), F32)
    for b in range(count):
        out = row_product(stacked[b], pattern, b, pairs)
        image[b] = out
        total += partial_rows(direction[b] * out)
    for f, sent in zip(partner_faces(), (send_0, send_1, send_2, send_3)):
        for k in range(SLOTS):
            sent[k * 128 : (k + 1) * 128, :] = image[jnp.minimum(faces[f, k], count - 1)]
    curvature[...] = jnp.broadcast_to(jnp.sum(total, axis=0, keepdims=True), curvature.shape)
    direction_copy.wait()


def update_kernel(
    faces_any, current, residual, direction, image, got_3, got_2, got_1, got_0, curvature, precond_dot,
    new_solution_hbm, new_residual_hbm,
    faces, new_solution, new_residual, added, slot, faces_sem, solution_sems, residual_sems,
):
    count = current.shape[0]
    faces_copy = pltpu.make_async_copy(faces_any, faces, faces_sem)
    faces_copy.start()
    step = precond_dot[...] / jnp.sum(curvature[...], axis=0, keepdims=True)
    copies = []

    def leave(c, value, value_hbm, sems):
        part = pl.ds(c * count // 4, count // 4)
        copies.append(pltpu.make_async_copy(value.at[part], value_hbm.at[part], sems.at[c]))
        copies[-1].start()

    for b in range(count):
        new_solution[b] = current[b] + step * direction[b]
        if (b + 1) % (count // 4) == 0:
            leave(b // (count // 4), new_solution, new_solution_hbm, solution_sems)
    for s, r in enumerate((got_0, got_1, got_2, got_3)):
        for k in range(SLOTS):
            added[s * SLOTS + k] = r[k * 128 : (k + 1) * 128, :]
    added[16] = jnp.zeros((128, 128), F32)
    faces_copy.wait()
    slots_by_block(faces, slot)
    for b in range(count):
        new_residual[b] = residual[b] - step * (image[b] + added[slot[b]])
        if (b + 1) % (count // 4) == 0:
            leave(b // (count // 4), new_residual, new_residual_hbm, residual_sems)
    for copy in copies:
        copy.wait()


def swap_pairs(x, axis, first):
    pairs = [(i, i + 1) for i in range(first, lax.axis_size(axis) - 1, 2)]
    return lax.ppermute(x, axis, pairs + [(j, i) for i, j in pairs])


def from_all(x, axes):
    sent = x.reshape(lax.axis_size(axes), 1, -1)
    return lax.all_to_all(sent, axes, split_axis=0, concat_axis=0, tiled=True).reshape(x.shape)


def shape(*dims):
    return jax.ShapeDtypeStruct(dims, F32)


def held(*dims):
    return pltpu.VMEM(dims, F32)


def in_hbm(x):
    return pltpu.with_memory_space_constraint(x, pltpu.HBM)


def kernel_params(mib):
    return pltpu.CompilerParams(vmem_limit_bytes=mib << 20)


def per_device(
    solution,
    residual,
    prev_direction,
    prev_dot,
    face_lists,
    multiplicity,
    block_pattern,
    schur,
    neumann_inverse,
    coarse_basis,
    primal_map,
    coarse_inverse,
):
    current, residual, previous = solution[0, 0], residual[0, 0], prev_direction[0, 0]
    faces, multiplicity = face_lists[0, 0], multiplicity[0, 0]
    pattern = jnp.transpose(block_pattern, (0, 3, 1, 2))[0]
    schur, neumann = schur[0, 0], neumann_inverse[0, 0]
    basis, primal_map = coarse_basis[0, 0], primal_map[0, 0]
    count, dofs, cases = residual.shape

    everywhere = lax.axis_size(("y", "core", "col"))
    order = coarse_inverse.shape[1]
    told_rows = (HEAD + 8 * (order // cases)) * (everywhere // 2)

    face = held(SLOTS * dofs + 32, cases)
    indices = (faces, multiplicity, pattern, primal_map)
    local, send_3, told, send_2, send_1, send_0 = pl.pallas_call(
        local_kernel,
        out_shape=(held(count, dofs, cases), face, shape(told_rows, cases), face, face, face),
        in_specs=[HBM] * 8,
        out_specs=(VMEM, VMEM, HBM, VMEM, VMEM, VMEM),
        scratch_shapes=[pltpu.SMEM(x.shape, jnp.int32) for x in indices]
        + [
            pltpu.VMEM(residual.shape, F32),
            pltpu.VMEM(neumann.shape, F32),
            pltpu.VMEM(basis.shape, F32),
            pltpu.VMEM(coarse_inverse.shape, F32),
            pltpu.VMEM((count, dofs, 2 * cases), BF16),
            pltpu.VMEM((told_rows, cases), F32),
            pltpu.SemaphoreType.DMA((4,)),
            pltpu.SemaphoreType.DMA,
            pltpu.SemaphoreType.DMA((2,)),
            pltpu.SemaphoreType.DMA((2,)),
            pltpu.SemaphoreType.DMA,
        ],
        compiler_params=kernel_params(16),
        name="local_solve",
    )(*(in_hbm(x) for x in (*indices, residual, neumann, basis, coarse_inverse)))

    same_core = from_all(told, ("y", "col"))
    other_core = lax.ppermute(same_core, "core", [(0, 1), (1, 0)])
    got_3 = swap_pairs(send_3, "col", 1)
    got_2 = swap_pairs(send_2, "col", 0)
    got_1 = swap_pairs(send_1, ("y", "core"), 1)
    got_0 = swap_pairs(send_0, ("y", "core"), 0)

    stacked = pl.pallas_call(
        halving_kernel,
        out_shape=pltpu.VMEM((count, 2 * dofs, 3 * dofs), BF16),
        in_specs=[HBM],
        out_specs=VMEM,
        scratch_shapes=[pltpu.VMEM(schur.shape, F32), pltpu.SemaphoreType.DMA((4,))],
        compiler_params=kernel_params(12),
        name="halving",
    )(in_hbm(schur))

    started, wanted, precond_dot = pl.pallas_call(
        coarse_kernel,
        out_shape=(held(count, dofs, cases), held(32, cases), held(1, cases)),
        in_specs=[SMEM] * 2 + [VMEM] * 5 + [HBM],
        out_specs=(VMEM,) * 3,
        scratch_shapes=[
            pltpu.VMEM((order, order), F32),
            pltpu.VMEM(previous.shape, F32),
            pltpu.SemaphoreType.DMA,
        ],
        compiler_params=kernel_params(24),
        name="coarse_solve",
    )(
        multiplicity, primal_map, local, same_core, other_core, basis, prev_dot.reshape(1, cases),
        in_hbm(previous),
    )

    direction, direction_held, image, send_3, send_2, send_1, send_0, curvature = pl.pallas_call(
        direction_kernel,
        out_shape=(shape(count, dofs, cases), held(count, dofs, cases), held(count, dofs, cases))
        + (held(SLOTS * dofs, cases),) * 4
        + (held(everywhere, cases),),
        in_specs=[SMEM] * 2 + [VMEM] * 7,
        out_specs=(HBM,) + (VMEM,) * 7,
        scratch_shapes=[
            pltpu.VMEM((17, dofs, cases), F32),
            pltpu.VMEM((count, dofs, 2 * cases), BF16),
            pltpu.SMEM((17,), jnp.int32),
            pltpu.SemaphoreType.DMA,
        ],
        compiler_params=kernel_params(16),
        name="direction_image",
    )(faces, pattern, started, wanted, got_3, got_2, got_1, got_0, stacked)

    got_3 = swap_pairs(send_3, "col", 1)
    got_2 = swap_pairs(send_2, "col", 0)
    got_1 = swap_pairs(send_1, ("y", "core"), 1)
    got_0 = swap_pairs(send_0, ("y", "core"), 0)
    curvature = from_all(curvature, ("y", "core", "col"))

    new_solution, new_residual = pl.pallas_call(
        update_kernel,
        out_shape=(shape(count, dofs, cases),) * 2,
        in_specs=[ANY] + [VMEM] * 10,
        out_specs=(HBM,) * 2,
        scratch_shapes=[
            pltpu.SMEM(faces.shape, jnp.int32),
            pltpu.VMEM(residual.shape, F32),
            pltpu.VMEM(residual.shape, F32),
            pltpu.VMEM((17, dofs, cases), F32),
            pltpu.SMEM((17,), jnp.int32),
            pltpu.SemaphoreType.DMA,
            pltpu.SemaphoreType.DMA((4,)),
            pltpu.SemaphoreType.DMA((4,)),
        ],
        compiler_params=kernel_params(16),
        name="update",
    )(
        faces, current, residual, direction_held, image, got_3, got_2, got_1, got_0, curvature, precond_dot
    )
    return (new_solution[None, None], new_residual[None, None], direction[None, None])


def solution(mesh):
    rows, cols = mesh.devices.shape
    mesh = jax.sharding.Mesh(mesh.devices.reshape(rows // 2, 2, cols), ("y", "core", "col"))
    split = lambda dims: P(("y", "core"), "col", *(None,) * dims)
    placed = (
        split(3), split(3), split(3), P(), split(2), split(1), split(2), split(4), split(4), split(2), split(1),
        P("col", None),
    )
    return jax.shard_map(
        per_device,
        mesh=mesh,
        in_specs=placed,
        out_specs=(split(3), split(3), split(3)),
        check_vma=False,
    )
```

```python
import jax
import jax.numpy as jnp
from jax import lax
from jax.experimental import pallas as pl
from jax.experimental.pallas import tpu as pltpu
from jax.sharding import PartitionSpec as P

F32 = jnp.float32
BF16 = jnp.bfloat16
SLOTS = 4
HEAD = 10
SMEM = pl.BlockSpec(memory_space=pltpu.SMEM)
VMEM = pl.BlockSpec(memory_space=pltpu.VMEM)
HBM = pl.BlockSpec(memory_space=pltpu.HBM)
ANY = pl.BlockSpec(memory_space=pl.ANY)


def halves(x):
    high = x.astype(BF16)
    return high, (x - high.astype(F32)).astype(BF16)


def dot(a, b):
    return jnp.dot(a, b, preferred_element_type=F32)


def dot_first(a, b):
    return lax.dot_general(a, b, (((0,), (0,)), ((), ())), preferred_element_type=F32)


def fold(x):
    width = x.shape[1] // 2
    return x[:, :width] + x[:, width:]


def product(matrix, pair):
    high, low = halves(matrix)
    return fold(dot(high, pair)) + dot(low, pair[:, : pair.shape[1] // 2])


def exact_pair(x):
    return jnp.concatenate(halves(x), axis=1)


def halved_rows(row_blocks):
    matrix = jnp.concatenate([row_blocks[k] for k in range(3)], axis=1)
    return jnp.concatenate(halves(matrix), axis=0)


def row_product(stacked, pattern, b, pairs):
    field = jnp.concatenate([pairs[pattern[k, 0, b]] for k in range(3)], axis=0)
    both = fold(dot(stacked, field))
    return both[:128] + both[128:]


def partial_rows(x):
    rows, cols = x.shape
    return jnp.sum(x.reshape(rows // 8, 8, cols), axis=0)


def weight_of(multiplicity, b):
    return 1.0 / jnp.full((1, 128), multiplicity[b].astype(F32))


def mapped(primal_map, shape, dim):
    place = lax.broadcasted_iota(jnp.int32, shape, dim)
    found = jnp.zeros(shape, jnp.int32)
    for p in range(8):
        found = jnp.where(place == p, primal_map[p], found)
    return found


def row_index():
    return 2 * lax.axis_index("y") + lax.axis_index("core")


def partner_faces():
    row, col = lax.axis_index("core"), lax.axis_index("col") % 2
    return 1 - row, row, 3 - col, 2 + col


def slots_by_block(faces, slot):
    for b in range(17):
        slot[b] = 16
    for s, f in enumerate(partner_faces()):
        for k in range(SLOTS):
            slot[faces[f, k]] = s * SLOTS + k


def local_kernel(
    faces_hbm, multiplicity_hbm, pattern_hbm, primal_map_hbm, residual_hbm, neumann_hbm, basis_hbm, inverse_hbm,
    local, send_2, told_hbm, send_1, send_0, send_3,
    faces, multiplicity, pattern, primal_map, residual, neumann, basis, inverse, pairs, told,
    index_sems, residual_sem, neumann_sems, basis_sems, told_sem,
):
    count = residual.shape[0]
    index_copies = [
        pltpu.make_async_copy(source, target, index_sems.at[i])
        for i, (source, target) in enumerate(
            ((multiplicity_hbm, multiplicity), (pattern_hbm, pattern), (primal_map_hbm, primal_map), (faces_hbm, faces))
        )
    ]
    basis_copy = pltpu.make_async_copy(basis_hbm, basis, basis_sems.at[0])
    inverse_copy = pltpu.make_async_copy(inverse_hbm, inverse, basis_sems.at[1])
    residual_copy = pltpu.make_async_copy(residual_hbm, residual, residual_sem)
    neumann_copies = {}
    for c, (start, stop) in enumerate(((0, count // 4), (count // 4, count))):
        part = pl.ds(start, stop - start)
        neumann_copies[start] = pltpu.make_async_copy(neumann_hbm.at[part], neumann.at[part], neumann_sems.at[c])
    for copy in (*index_copies, residual_copy, basis_copy, *neumann_copies.values(), inverse_copy):
        copy.start()
    for copy in index_copies:
        copy.wait()
    residual_copy.wait()
    basis_copy.wait()
    for b in range(count):
        pairs[b] = exact_pair(residual[b] * weight_of(multiplicity, b))
    total = jnp.zeros((8, 128), F32)
    for b in range(count):
        if b in neumann_copies:
            neumann_copies[b].wait()
        if b == count // 4:
            coarse_local = product(basis[...], pairs[...].reshape(count * 128, 256))
        weight = weight_of(multiplicity, b)
        out = row_product(halved_rows(neumann.at[b]), pattern, b, pairs) * weight
        local[b] = out
        total += partial_rows(residual[b] * out)
    row = lax.broadcasted_iota(jnp.int32, (8, 128), 0)
    total = jnp.sum(total, axis=0, keepdims=True)
    map_row = mapped(primal_map, (8, 128), 1).astype(F32)
    inverse_copy.wait()
    sharers = inverse.shape[0] // 8
    mine = row_index() % sharers
    share = inverse[pl.ds(pl.multiple_of(mine * 8, 8), 8), :]
    rows = [coarse_local, jnp.where(row == 0, total, map_row)[:2]]
    rows = jnp.concatenate(rows + [share[:, i : i + 128] for i in range(0, inverse.shape[1], 128)], axis=0)
    each = rows.shape[0]
    for i in range(told.shape[0] // each):
        told[each * i : each * i + each, :] = rows
    told_copy = pltpu.make_async_copy(told, told_hbm, told_sem)
    told_copy.start()
    for f, sent in zip(partner_faces(), (send_0, send_1, send_2, send_3)):
        for k in range(SLOTS):
            b = jnp.minimum(faces[f, k], count - 1)
            sent[k * 128 : (k + 1) * 128, :] = local[b]
            lanes = pl.ds(pl.multiple_of(b * 128, 128), 128)
            sent[512 + 8 * k : 520 + 8 * k, :] = basis[:, lanes] * weight_of(multiplicity, b)
    told_copy.wait()


def back(basis, own):
    bh, bl = (h.astype(F32) for h in halves(basis))
    oh, ol = (h.astype(F32) for h in halves(own))
    left = jnp.concatenate([bh, bl, bh, bl], axis=0).astype(BF16)
    right = jnp.concatenate([oh, oh, ol, ol], axis=0).astype(BF16)
    return dot_first(left, right)


def halving_kernel(schur_hbm, stacked, schur, sems):
    count = schur.shape[0]
    copies = []
    for c in range(4):
        part = pl.ds(c * count // 4, count // 4)
        copies.append(pltpu.make_async_copy(schur_hbm.at[part], schur.at[part], sems.at[c]))
        copies[c].start()
    for b in range(count):
        if b % (count // 4) == 0:
            copies[b // (count // 4)].wait()
        stacked[b] = halved_rows(schur.at[b])


def coarse_kernel(
    multiplicity, primal_map, local, same_core, other_core, basis, prev_dot, previous_hbm,
    started, wanted, precond_dot, inverse, previous, previous_sem,
):
    count = local.shape[0]
    previous_copy = pltpu.make_async_copy(previous_hbm, previous, previous_sem)
    previous_copy.start()

    order = inverse.shape[1]
    each = HEAD + 8 * (order // 128)
    half = same_core.shape[0] // each
    cols = lax.axis_size("col")
    sharers = order // cols // 8
    for told, core in ((same_core, lax.axis_index("core")), (other_core, 1 - lax.axis_index("core"))):
        for i in range(half):
            target = pl.multiple_of((i % cols * sharers + (2 * (i // cols) + core) % sharers) * 8, 8)
            for j in range(order // 128):
                source = i * each + HEAD + 8 * j
                inverse[pl.ds(target, 8), 128 * j : 128 * j + 128] = told[source : source + 8, :]

    def row_of_all(p):
        return jnp.concatenate([x[pl.ds(p, half, stride=each), :] for x in (same_core, other_core)], axis=0)

    maps = row_of_all(9).astype(jnp.int32)
    lane = lax.broadcasted_iota(jnp.int32, (2 * half, order), 1)
    chosen = [(maps[:, p : p + 1] == lane).astype(F32) for p in range(8)]
    chosen = jnp.concatenate(chosen, axis=0).astype(BF16)
    rows = jnp.concatenate([row_of_all(p) for p in range(8)], axis=0)
    rhs = fold(dot_first(chosen, exact_pair(rows)))
    coarse = product(inverse[...], exact_pair(rhs))
    dots = jnp.sum(row_of_all(8), axis=0, keepdims=True)
    dots = dots + jnp.sum(rhs * coarse, axis=0, keepdims=True)
    precond_dot[...] = dots
    beta = dots / prev_dot[...]
    y, core, col = (lax.axis_index(name) for name in ("y", "core", "col"))
    odd = col % 2
    partners = (
        (other_core, y * cols + col),
        (other_core, jnp.clip(y + 2 * core - 1, 0, lax.axis_size("y") - 1) * cols + col),
        (same_core, y * cols + (col + 1 - 2 * odd)),
        (same_core, y * cols + jnp.clip(col + 2 * odd - 1, 0, cols - 1)),
    )
    map_rows = [x[pl.ds(i * each + 9, 1), :] for x, i in partners]
    map_rows = jnp.concatenate([jnp.broadcast_to(row, (8, 128)) for row in map_rows], axis=0)
    on_diagonal = lax.broadcasted_iota(jnp.int32, (32, 128), 0) % 8 == lax.broadcasted_iota(jnp.int32, (32, 128), 1)
    maps = jnp.sum(jnp.where(on_diagonal, map_rows, 0.0), axis=1, keepdims=True).astype(jnp.int32)
    maps = jnp.concatenate([mapped(primal_map, (8, 128), 0)[:, 0:1], maps], axis=0)
    lane = lax.broadcasted_iota(jnp.int32, (40, order), 1)
    picked = fold(dot((maps == lane).astype(F32).astype(BF16), exact_pair(coarse)))
    wanted[...] = picked[8:40]
    own_back = back(basis[...], picked[0:8])
    previous_copy.wait()
    for b in range(count):
        mine = local[b] + own_back[b * 128 : (b + 1) * 128] * weight_of(multiplicity, b)
        started[b] = mine + beta * previous[b]
def direction_kernel(
    faces, pattern, started, wanted, got_2, got_1, got_0, got_3, stacked,
    direction_hbm, direction, image, send_2, send_1, send_0, send_3, curvature,
    added, pairs, slot, direction_sem,
):
    count = started.shape[0]
    slots_by_block(faces, slot)
    for s, r in enumerate((got_0, got_1, got_2, got_3)):
        face_basis = jnp.concatenate([r[512 + 8 * k : 520 + 8 * k, :] for k in range(SLOTS)], axis=1)
        face_back = back(face_basis, wanted[8 * s : 8 * s + 8, :])
        for k in range(SLOTS):
            part = slice(k * 128, (k + 1) * 128)
            added[s * SLOTS + k] = r[part, :] + face_back[part]
    added[16] = jnp.zeros((128, 128), F32)
    for b in range(count):
        value = started[b] + added[slot[b]]
        direction[b] = value
        pairs[b] = exact_pair(value)
    direction_copy = pltpu.make_async_copy(direction, direction_hbm, direction_sem)
    direction_copy.start()
    total = jnp.zeros((8, 128), F32)
    for b in range(count):
        out = row_product(stacked[b], pattern, b, pairs)
        image[b] = out
        total += partial_rows(direction[b] * out)
    for f, sent in zip(partner_faces(), (send_0, send_1, send_2, send_3)):
        for k in range(SLOTS):
            sent[k * 128 : (k + 1) * 128, :] = image[jnp.minimum(faces[f, k], count - 1)]
    curvature[...] = jnp.broadcast_to(jnp.sum(total, axis=0, keepdims=True), curvature.shape)
    direction_copy.wait()


def update_kernel(
    faces_any, current, residual, direction, image, got_2, got_1, got_0, got_3, curvature, precond_dot,
    new_solution_hbm, new_residual_hbm,
    faces, new_solution, new_residual, added, slot, faces_sem, solution_sems, residual_sems,
):
    count = current.shape[0]
    faces_copy = pltpu.make_async_copy(faces_any, faces, faces_sem)
    faces_copy.start()
    step = precond_dot[...] / jnp.sum(curvature[...], axis=0, keepdims=True)
    copies = []

    def leave(c, value, value_hbm, sems):
        part = pl.ds(c * count // 4, count // 4)
        copies.append(pltpu.make_async_copy(value.at[part], value_hbm.at[part], sems.at[c]))
        copies[-1].start()

    for b in range(count):
        new_solution[b] = current[b] + step * direction[b]
        if (b + 1) % (count // 4) == 0:
            leave(b // (count // 4), new_solution, new_solution_hbm, solution_sems)
    for s, r in enumerate((got_0, got_1, got_2, got_3)):
        for k in range(SLOTS):
            added[s * SLOTS + k] = r[k * 128 : (k + 1) * 128, :]
    added[16] = jnp.zeros((128, 128), F32)
    faces_copy.wait()
    slots_by_block(faces, slot)
    for b in range(count):
        new_residual[b] = residual[b] - step * (image[b] + added[slot[b]])
        if (b + 1) % (count // 4) == 0:
            leave(b // (count // 4), new_residual, new_residual_hbm, residual_sems)
    for copy in copies:
        copy.wait()


def swap_pairs(x, axis, first):
    pairs = [(i, i + 1) for i in range(first, lax.axis_size(axis) - 1, 2)]
    return lax.ppermute(x, axis, pairs + [(j, i) for i, j in pairs])


def from_all(x, axes):
    sent = x.reshape(lax.axis_size(axes), 1, -1)
    return lax.all_to_all(sent, axes, split_axis=0, concat_axis=0, tiled=True).reshape(x.shape)


def shape(*dims):
    return jax.ShapeDtypeStruct(dims, F32)


def held(*dims):
    return pltpu.VMEM(dims, F32)


def in_hbm(x):
    return pltpu.with_memory_space_constraint(x, pltpu.HBM)


def kernel_params(mib):
    return pltpu.CompilerParams(vmem_limit_bytes=mib << 20)


def per_device(
    solution,
    residual,
    prev_direction,
    prev_dot,
    face_lists,
    multiplicity,
    block_pattern,
    schur,
    neumann_inverse,
    coarse_basis,
    primal_map,
    coarse_inverse,
):
    current, residual, previous = solution[0, 0], residual[0, 0], prev_direction[0, 0]
    faces, multiplicity = face_lists[0, 0], multiplicity[0, 0]
    pattern = jnp.transpose(block_pattern, (0, 3, 1, 2))[0]
    schur, neumann = schur[0, 0], neumann_inverse[0, 0]
    basis, primal_map = coarse_basis[0, 0], primal_map[0, 0]
    count, dofs, cases = residual.shape

    everywhere = lax.axis_size(("y", "core", "col"))
    order = coarse_inverse.shape[1]
    told_rows = (HEAD + 8 * (order // cases)) * (everywhere // 2)

    face = held(SLOTS * dofs + 32, cases)
    indices = (faces, multiplicity, pattern, primal_map)
    local, send_2, told, send_1, send_0, send_3 = pl.pallas_call(
        local_kernel,
        out_shape=(held(count, dofs, cases), face, shape(told_rows, cases), face, face, face),
        in_specs=[HBM] * 8,
        out_specs=(VMEM, VMEM, HBM, VMEM, VMEM, VMEM),
        scratch_shapes=[pltpu.SMEM(x.shape, jnp.int32) for x in indices]
        + [
            pltpu.VMEM(residual.shape, F32),
            pltpu.VMEM(neumann.shape, F32),
            pltpu.VMEM(basis.shape, F32),
            pltpu.VMEM(coarse_inverse.shape, F32),
            pltpu.VMEM((count, dofs, 2 * cases), BF16),
            pltpu.VMEM((told_rows, cases), F32),
            pltpu.SemaphoreType.DMA((4,)),
            pltpu.SemaphoreType.DMA,
            pltpu.SemaphoreType.DMA((2,)),
            pltpu.SemaphoreType.DMA((2,)),
            pltpu.SemaphoreType.DMA,
        ],
        compiler_params=kernel_params(16),
        name="local_solve",
    )(*(in_hbm(x) for x in (*indices, residual, neumann, basis, coarse_inverse)))

    same_core = from_all(told, ("y", "col"))
    other_core = lax.ppermute(same_core, "core", [(0, 1), (1, 0)])
    got_2 = swap_pairs(send_2, "col", 0)
    got_1 = swap_pairs(send_1, ("y", "core"), 1)
    got_0 = swap_pairs(send_0, ("y", "core"), 0)
    got_3 = swap_pairs(send_3, "col", 1)

    stacked = pl.pallas_call(
        halving_kernel,
        out_shape=pltpu.VMEM((count, 2 * dofs, 3 * dofs), BF16),
        in_specs=[HBM],
        out_specs=VMEM,
        scratch_shapes=[pltpu.VMEM(schur.shape, F32), pltpu.SemaphoreType.DMA((4,))],
        compiler_params=kernel_params(12),
        name="halving",
    )(in_hbm(schur))

    started, wanted, precond_dot = pl.pallas_call(
        coarse_kernel,
        out_shape=(held(count, dofs, cases), held(32, cases), held(1, cases)),
        in_specs=[SMEM] * 2 + [VMEM] * 5 + [HBM],
        out_specs=(VMEM,) * 3,
        scratch_shapes=[
            pltpu.VMEM((order, order), F32),
            pltpu.VMEM(previous.shape, F32),
            pltpu.SemaphoreType.DMA,
        ],
        compiler_params=kernel_params(24),
        name="coarse_solve",
    )(
        multiplicity, primal_map, local, same_core, other_core, basis, prev_dot.reshape(1, cases),
        in_hbm(previous),
    )

    direction, direction_held, image, send_2, send_1, send_0, send_3, curvature = pl.pallas_call(
        direction_kernel,
        out_shape=(shape(count, dofs, cases), held(count, dofs, cases), held(count, dofs, cases))
        + (held(SLOTS * dofs, cases),) * 4
        + (held(everywhere, cases),),
        in_specs=[SMEM] * 2 + [VMEM] * 7,
        out_specs=(HBM,) + (VMEM,) * 7,
        scratch_shapes=[
            pltpu.VMEM((17, dofs, cases), F32),
            pltpu.VMEM((count, dofs, 2 * cases), BF16),
            pltpu.SMEM((17,), jnp.int32),
            pltpu.SemaphoreType.DMA,
        ],
        compiler_params=kernel_params(16),
        name="direction_image",
    )(faces, pattern, started, wanted, got_2, got_1, got_0, got_3, stacked)

    got_2 = swap_pairs(send_2, "col", 0)
    got_1 = swap_pairs(send_1, ("y", "core"), 1)
    got_0 = swap_pairs(send_0, ("y", "core"), 0)
    got_3 = swap_pairs(send_3, "col", 1)
    curvature = from_all(curvature, ("y", "core", "col"))

    new_solution, new_residual = pl.pallas_call(
        update_kernel,
        out_shape=(shape(count, dofs, cases),) * 2,
        in_specs=[ANY] + [VMEM] * 10,
        out_specs=(HBM,) * 2,
        scratch_shapes=[
            pltpu.SMEM(faces.shape, jnp.int32),
            pltpu.VMEM(residual.shape, F32),
            pltpu.VMEM(residual.shape, F32),
            pltpu.VMEM((17, dofs, cases), F32),
            pltpu.SMEM((17,), jnp.int32),
            pltpu.SemaphoreType.DMA,
            pltpu.SemaphoreType.DMA((4,)),
            pltpu.SemaphoreType.DMA((4,)),
        ],
        compiler_params=kernel_params(16),
        name="update",
    )(
        faces, current, residual, direction_held, image, got_2, got_1, got_0, got_3, curvature, precond_dot
    )
    return (new_solution[None, None], new_residual[None, None], direction[None, None])


def solution(mesh):
    rows, cols = mesh.devices.shape
    mesh = jax.sharding.Mesh(mesh.devices.reshape(rows // 2, 2, cols), ("y", "core", "col"))
    split = lambda dims: P(("y", "core"), "col", *(None,) * dims)
    placed = (
        split(3), split(3), split(3), P(), split(2), split(1), split(2), split(4), split(4), split(2), split(1),
        P("col", None),
    )
    return jax.shard_map(
        per_device,
        mesh=mesh,
        in_specs=placed,
        out_specs=(split(3), split(3), split(3)),
        check_vma=False,
    )
```

```python
import jax
import jax.numpy as jnp
from jax import lax
from jax.experimental import pallas as pl
from jax.experimental.pallas import tpu as pltpu
from jax.sharding import PartitionSpec as P

F32 = jnp.float32
BF16 = jnp.bfloat16
SLOTS = 4
HEAD = 10
SMEM = pl.BlockSpec(memory_space=pltpu.SMEM)
VMEM = pl.BlockSpec(memory_space=pltpu.VMEM)
HBM = pl.BlockSpec(memory_space=pltpu.HBM)
ANY = pl.BlockSpec(memory_space=pl.ANY)


def halves(x):
    high = x.astype(BF16)
    return high, (x - high.astype(F32)).astype(BF16)


def dot(a, b):
    return jnp.dot(a, b, preferred_element_type=F32)


def dot_first(a, b):
    return lax.dot_general(a, b, (((0,), (0,)), ((), ())), preferred_element_type=F32)


def fold(x):
    width = x.shape[1] // 2
    return x[:, :width] + x[:, width:]


def product(matrix, pair):
    high, low = halves(matrix)
    return fold(dot(high, pair)) + dot(low, pair[:, : pair.shape[1] // 2])


def exact_pair(x):
    return jnp.concatenate(halves(x), axis=1)


def halved_rows(row_blocks):
    matrix = jnp.concatenate([row_blocks[k] for k in range(3)], axis=1)
    return jnp.concatenate(halves(matrix), axis=0)


def row_product(stacked, pattern, b, pairs):
    field = jnp.concatenate([pairs[pattern[k, 0, b]] for k in range(3)], axis=0)
    both = fold(dot(stacked, field))
    return both[:128] + both[128:]


def partial_rows(x):
    rows, cols = x.shape
    return jnp.sum(x.reshape(rows // 8, 8, cols), axis=0)


def weight_of(multiplicity, b):
    return 1.0 / jnp.full((1, 128), multiplicity[b].astype(F32))


def mapped(primal_map, shape, dim):
    place = lax.broadcasted_iota(jnp.int32, shape, dim)
    found = jnp.zeros(shape, jnp.int32)
    for p in range(8):
        found = jnp.where(place == p, primal_map[p], found)
    return found


def row_index():
    return 2 * lax.axis_index("y") + lax.axis_index("core")


def partner_faces():
    row, col = lax.axis_index("core"), lax.axis_index("col") % 2
    return 1 - row, row, 3 - col, 2 + col


def slots_by_block(faces, slot):
    for b in range(17):
        slot[b] = 16
    for s, f in enumerate(partner_faces()):
        for k in range(SLOTS):
            slot[faces[f, k]] = s * SLOTS + k


def local_kernel(
    faces_hbm, multiplicity_hbm, pattern_hbm, primal_map_hbm, residual_hbm, neumann_hbm, basis_hbm, inverse_hbm,
    local, send_2, told_hbm, send_1, send_0, send_3,
    faces, multiplicity, pattern, primal_map, residual, neumann, basis, inverse, pairs, told,
    index_sems, residual_sem, neumann_sems, basis_sems, told_sem,
):
    count = residual.shape[0]
    index_copies = [
        pltpu.make_async_copy(source, target, index_sems.at[i])
        for i, (source, target) in enumerate(
            ((multiplicity_hbm, multiplicity), (pattern_hbm, pattern), (primal_map_hbm, primal_map), (faces_hbm, faces))
        )
    ]
    basis_copy = pltpu.make_async_copy(basis_hbm, basis, basis_sems.at[0])
    inverse_copy = pltpu.make_async_copy(inverse_hbm, inverse, basis_sems.at[1])
    residual_copy = pltpu.make_async_copy(residual_hbm, residual, residual_sem)
    neumann_copies = {}
    for c, (start, stop) in enumerate(((0, count // 4), (count // 4, count))):
        part = pl.ds(start, stop - start)
        neumann_copies[start] = pltpu.make_async_copy(neumann_hbm.at[part], neumann.at[part], neumann_sems.at[c])
    for copy in (*index_copies, residual_copy, basis_copy, inverse_copy, *neumann_copies.values()):
        copy.start()
    for copy in index_copies:
        copy.wait()
    residual_copy.wait()
    basis_copy.wait()
    for b in range(count):
        pairs[b] = exact_pair(residual[b] * weight_of(multiplicity, b))
    total = jnp.zeros((8, 128), F32)
    for b in range(count):
        if b in neumann_copies:
            neumann_copies[b].wait()
        if b == count // 4:
            inverse_copy.wait()
            coarse_local = product(basis[...], pairs[...].reshape(count * 128, 256))
        weight = weight_of(multiplicity, b)
        out = row_product(halved_rows(neumann.at[b]), pattern, b, pairs) * weight
        local[b] = out
        total += partial_rows(residual[b] * out)
    row = lax.broadcasted_iota(jnp.int32, (8, 128), 0)
    total = jnp.sum(total, axis=0, keepdims=True)
    map_row = mapped(primal_map, (8, 128), 1).astype(F32)
    sharers = inverse.shape[0] // 8
    mine = row_index() % sharers
    share = inverse[pl.ds(pl.multiple_of(mine * 8, 8), 8), :]
    rows = [coarse_local, jnp.where(row == 0, total, map_row)[:2]]
    rows = jnp.concatenate(rows + [share[:, i : i + 128] for i in range(0, inverse.shape[1], 128)], axis=0)
    each = rows.shape[0]
    for i in range(told.shape[0] // each):
        told[each * i : each * i + each, :] = rows
    told_copy = pltpu.make_async_copy(told, told_hbm, told_sem)
    told_copy.start()
    for f, sent in zip(partner_faces(), (send_0, send_1, send_2, send_3)):
        for k in range(SLOTS):
            b = jnp.minimum(faces[f, k], count - 1)
            sent[k * 128 : (k + 1) * 128, :] = local[b]
            lanes = pl.ds(pl.multiple_of(b * 128, 128), 128)
            sent[512 + 8 * k : 520 + 8 * k, :] = basis[:, lanes] * weight_of(multiplicity, b)
    told_copy.wait()


def back(basis, own):
    bh, bl = (h.astype(F32) for h in halves(basis))
    oh, ol = (h.astype(F32) for h in halves(own))
    left = jnp.concatenate([bh, bl, bh, bl], axis=0).astype(BF16)
    right = jnp.concatenate([oh, oh, ol, ol], axis=0).astype(BF16)
    return dot_first(left, right)


def halving_kernel(schur_hbm, stacked, schur, sems):
    count = schur.shape[0]
    copies = []
    for c in range(4):
        part = pl.ds(c * count // 4, count // 4)
        copies.append(pltpu.make_async_copy(schur_hbm.at[part], schur.at[part], sems.at[c]))
        copies[c].start()
    for b in range(count):
        if b % (count // 4) == 0:
            copies[b // (count // 4)].wait()
        stacked[b] = halved_rows(schur.at[b])


def coarse_kernel(
    multiplicity, primal_map, local, same_core, other_core, basis, prev_dot, previous_hbm,
    started, wanted, precond_dot, inverse, previous, previous_sem,
):
    count = local.shape[0]
    previous_copy = pltpu.make_async_copy(previous_hbm, previous, previous_sem)
    previous_copy.start()

    order = inverse.shape[1]
    each = HEAD + 8 * (order // 128)
    half = same_core.shape[0] // each
    cols = lax.axis_size("col")
    sharers = order // cols // 8
    for told, core in ((same_core, lax.axis_index("core")), (other_core, 1 - lax.axis_index("core"))):
        for i in range(half):
            target = pl.multiple_of((i % cols * sharers + (2 * (i // cols) + core) % sharers) * 8, 8)
            for j in range(order // 128):
                source = i * each + HEAD + 8 * j
                inverse[pl.ds(target, 8), 128 * j : 128 * j + 128] = told[source : source + 8, :]

    def row_of_all(p):
        return jnp.concatenate([x[pl.ds(p, half, stride=each), :] for x in (same_core, other_core)], axis=0)

    maps = row_of_all(9).astype(jnp.int32)
    lane = lax.broadcasted_iota(jnp.int32, (2 * half, order), 1)
    chosen = [(maps[:, p : p + 1] == lane).astype(F32) for p in range(8)]
    chosen = jnp.concatenate(chosen, axis=0).astype(BF16)
    rows = jnp.concatenate([row_of_all(p) for p in range(8)], axis=0)
    rhs = fold(dot_first(chosen, exact_pair(rows)))
    coarse = product(inverse[...], exact_pair(rhs))
    dots = jnp.sum(row_of_all(8), axis=0, keepdims=True)
    dots = dots + jnp.sum(rhs * coarse, axis=0, keepdims=True)
    precond_dot[...] = dots
    beta = dots / prev_dot[...]
    y, core, col = (lax.axis_index(name) for name in ("y", "core", "col"))
    odd = col % 2
    partners = (
        (other_core, y * cols + col),
        (other_core, jnp.clip(y + 2 * core - 1, 0, lax.axis_size("y") - 1) * cols + col),
        (same_core, y * cols + (col + 1 - 2 * odd)),
        (same_core, y * cols + jnp.clip(col + 2 * odd - 1, 0, cols - 1)),
    )
    map_rows = [x[pl.ds(i * each + 9, 1), :] for x, i in partners]
    map_rows = jnp.concatenate([jnp.broadcast_to(row, (8, 128)) for row in map_rows], axis=0)
    on_diagonal = lax.broadcasted_iota(jnp.int32, (32, 128), 0) % 8 == lax.broadcasted_iota(jnp.int32, (32, 128), 1)
    maps = jnp.sum(jnp.where(on_diagonal, map_rows, 0.0), axis=1, keepdims=True).astype(jnp.int32)
    maps = jnp.concatenate([mapped(primal_map, (8, 128), 0)[:, 0:1], maps], axis=0)
    lane = lax.broadcasted_iota(jnp.int32, (40, order), 1)
    picked = fold(dot((maps == lane).astype(F32).astype(BF16), exact_pair(coarse)))
    wanted[...] = picked[8:40]
    own_back = back(basis[...], picked[0:8])
    previous_copy.wait()
    for b in range(count):
        mine = local[b] + own_back[b * 128 : (b + 1) * 128] * weight_of(multiplicity, b)
        started[b] = mine + beta * previous[b]
def direction_kernel(
    faces, pattern, started, wanted, got_2, got_1, got_0, got_3, stacked,
    direction_hbm, direction, image, send_2, send_1, send_0, send_3, curvature,
    added, pairs, slot, direction_sem,
):
    count = started.shape[0]
    slots_by_block(faces, slot)
    for s, r in enumerate((got_0, got_1, got_2, got_3)):
        face_basis = jnp.concatenate([r[512 + 8 * k : 520 + 8 * k, :] for k in range(SLOTS)], axis=1)
        face_back = back(face_basis, wanted[8 * s : 8 * s + 8, :])
        for k in range(SLOTS):
            part = slice(k * 128, (k + 1) * 128)
            added[s * SLOTS + k] = r[part, :] + face_back[part]
    added[16] = jnp.zeros((128, 128), F32)
    for b in range(count):
        value = started[b] + added[slot[b]]
        direction[b] = value
        pairs[b] = exact_pair(value)
    direction_copy = pltpu.make_async_copy(direction, direction_hbm, direction_sem)
    direction_copy.start()
    total = jnp.zeros((8, 128), F32)
    for b in range(count):
        out = row_product(stacked[b], pattern, b, pairs)
        image[b] = out
        total += partial_rows(direction[b] * out)
    for f, sent in zip(partner_faces(), (send_0, send_1, send_2, send_3)):
        for k in range(SLOTS):
            sent[k * 128 : (k + 1) * 128, :] = image[jnp.minimum(faces[f, k], count - 1)]
    curvature[...] = jnp.broadcast_to(jnp.sum(total, axis=0, keepdims=True), curvature.shape)
    direction_copy.wait()


def update_kernel(
    faces_any, current, residual, direction, image, got_2, got_1, got_0, got_3, curvature, precond_dot,
    new_solution_hbm, new_residual_hbm,
    faces, new_solution, new_residual, added, slot, faces_sem, solution_sems, residual_sems,
):
    count = current.shape[0]
    faces_copy = pltpu.make_async_copy(faces_any, faces, faces_sem)
    faces_copy.start()
    step = precond_dot[...] / jnp.sum(curvature[...], axis=0, keepdims=True)
    copies = []

    def leave(c, value, value_hbm, sems):
        part = pl.ds(c * count // 4, count // 4)
        copies.append(pltpu.make_async_copy(value.at[part], value_hbm.at[part], sems.at[c]))
        copies[-1].start()

    for b in range(count):
        new_solution[b] = current[b] + step * direction[b]
        if (b + 1) % (count // 4) == 0:
            leave(b // (count // 4), new_solution, new_solution_hbm, solution_sems)
    for s, r in enumerate((got_0, got_1, got_2, got_3)):
        for k in range(SLOTS):
            added[s * SLOTS + k] = r[k * 128 : (k + 1) * 128, :]
    added[16] = jnp.zeros((128, 128), F32)
    faces_copy.wait()
    slots_by_block(faces, slot)
    for b in range(count):
        new_residual[b] = residual[b] - step * (image[b] + added[slot[b]])
        if (b + 1) % (count // 4) == 0:
            leave(b // (count // 4), new_residual, new_residual_hbm, residual_sems)
    for copy in copies:
        copy.wait()


def swap_pairs(x, axis, first):
    pairs = [(i, i + 1) for i in range(first, lax.axis_size(axis) - 1, 2)]
    return lax.ppermute(x, axis, pairs + [(j, i) for i, j in pairs])


def from_all(x, axes):
    sent = x.reshape(lax.axis_size(axes), 1, -1)
    return lax.all_to_all(sent, axes, split_axis=0, concat_axis=0, tiled=True).reshape(x.shape)


def shape(*dims):
    return jax.ShapeDtypeStruct(dims, F32)


def held(*dims):
    return pltpu.VMEM(dims, F32)


def in_hbm(x):
    return pltpu.with_memory_space_constraint(x, pltpu.HBM)


def kernel_params(mib):
    return pltpu.CompilerParams(vmem_limit_bytes=mib << 20)


def per_device(
    solution,
    residual,
    prev_direction,
    prev_dot,
    face_lists,
    multiplicity,
    block_pattern,
    schur,
    neumann_inverse,
    coarse_basis,
    primal_map,
    coarse_inverse,
):
    current, residual, previous = solution[0, 0], residual[0, 0], prev_direction[0, 0]
    faces, multiplicity = face_lists[0, 0], multiplicity[0, 0]
    pattern = jnp.transpose(block_pattern, (0, 3, 1, 2))[0]
    schur, neumann = schur[0, 0], neumann_inverse[0, 0]
    basis, primal_map = coarse_basis[0, 0], primal_map[0, 0]
    count, dofs, cases = residual.shape

    everywhere = lax.axis_size(("y", "core", "col"))
    order = coarse_inverse.shape[1]
    told_rows = (HEAD + 8 * (order // cases)) * (everywhere // 2)

    face = held(SLOTS * dofs + 32, cases)
    indices = (faces, multiplicity, pattern, primal_map)
    local, send_2, told, send_1, send_0, send_3 = pl.pallas_call(
        local_kernel,
        out_shape=(held(count, dofs, cases), face, shape(told_rows, cases), face, face, face),
        in_specs=[HBM] * 8,
        out_specs=(VMEM, VMEM, HBM, VMEM, VMEM, VMEM),
        scratch_shapes=[pltpu.SMEM(x.shape, jnp.int32) for x in indices]
        + [
            pltpu.VMEM(residual.shape, F32),
            pltpu.VMEM(neumann.shape, F32),
            pltpu.VMEM(basis.shape, F32),
            pltpu.VMEM(coarse_inverse.shape, F32),
            pltpu.VMEM((count, dofs, 2 * cases), BF16),
            pltpu.VMEM((told_rows, cases), F32),
            pltpu.SemaphoreType.DMA((4,)),
            pltpu.SemaphoreType.DMA,
            pltpu.SemaphoreType.DMA((2,)),
            pltpu.SemaphoreType.DMA((2,)),
            pltpu.SemaphoreType.DMA,
        ],
        compiler_params=kernel_params(16),
        name="local_solve",
    )(*(in_hbm(x) for x in (*indices, residual, neumann, basis, coarse_inverse)))

    same_core = from_all(told, ("y", "col"))
    other_core = lax.ppermute(same_core, "core", [(0, 1), (1, 0)])
    got_2 = swap_pairs(send_2, "col", 0)
    got_1 = swap_pairs(send_1, ("y", "core"), 1)
    got_0 = swap_pairs(send_0, ("y", "core"), 0)
    got_3 = swap_pairs(send_3, "col", 1)

    stacked = pl.pallas_call(
        halving_kernel,
        out_shape=pltpu.VMEM((count, 2 * dofs, 3 * dofs), BF16),
        in_specs=[HBM],
        out_specs=VMEM,
        scratch_shapes=[pltpu.VMEM(schur.shape, F32), pltpu.SemaphoreType.DMA((4,))],
        compiler_params=kernel_params(12),
        name="halving",
    )(in_hbm(schur))

    started, wanted, precond_dot = pl.pallas_call(
        coarse_kernel,
        out_shape=(held(count, dofs, cases), held(32, cases), held(1, cases)),
        in_specs=[SMEM] * 2 + [VMEM] * 5 + [HBM],
        out_specs=(VMEM,) * 3,
        scratch_shapes=[
            pltpu.VMEM((order, order), F32),
            pltpu.VMEM(previous.shape, F32),
            pltpu.SemaphoreType.DMA,
        ],
        compiler_params=kernel_params(24),
        name="coarse_solve",
    )(
        multiplicity, primal_map, local, same_core, other_core, basis, prev_dot.reshape(1, cases),
        in_hbm(previous),
    )

    direction, direction_held, image, send_2, send_1, send_0, send_3, curvature = pl.pallas_call(
        direction_kernel,
        out_shape=(shape(count, dofs, cases), held(count, dofs, cases), held(count, dofs, cases))
        + (held(SLOTS * dofs, cases),) * 4
        + (held(everywhere, cases),),
        in_specs=[SMEM] * 2 + [VMEM] * 7,
        out_specs=(HBM,) + (VMEM,) * 7,
        scratch_shapes=[
            pltpu.VMEM((17, dofs, cases), F32),
            pltpu.VMEM((count, dofs, 2 * cases), BF16),
            pltpu.SMEM((17,), jnp.int32),
            pltpu.SemaphoreType.DMA,
        ],
        compiler_params=kernel_params(16),
        name="direction_image",
    )(faces, pattern, started, wanted, got_2, got_1, got_0, got_3, stacked)

    got_2 = swap_pairs(send_2, "col", 0)
    got_1 = swap_pairs(send_1, ("y", "core"), 1)
    got_0 = swap_pairs(send_0, ("y", "core"), 0)
    got_3 = swap_pairs(send_3, "col", 1)
    curvature = from_all(curvature, ("y", "core", "col"))

    new_solution, new_residual = pl.pallas_call(
        update_kernel,
        out_shape=(shape(count, dofs, cases),) * 2,
        in_specs=[ANY] + [VMEM] * 10,
        out_specs=(HBM,) * 2,
        scratch_shapes=[
            pltpu.SMEM(faces.shape, jnp.int32),
            pltpu.VMEM(residual.shape, F32),
            pltpu.VMEM(residual.shape, F32),
            pltpu.VMEM((17, dofs, cases), F32),
            pltpu.SMEM((17,), jnp.int32),
            pltpu.SemaphoreType.DMA,
            pltpu.SemaphoreType.DMA((4,)),
            pltpu.SemaphoreType.DMA((4,)),
        ],
        compiler_params=kernel_params(16),
        name="update",
    )(
        faces, current, residual, direction_held, image, got_2, got_1, got_0, got_3, curvature, precond_dot
    )
    return (new_solution[None, None], new_residual[None, None], direction[None, None])


def solution(mesh):
    rows, cols = mesh.devices.shape
    mesh = jax.sharding.Mesh(mesh.devices.reshape(rows // 2, 2, cols), ("y", "core", "col"))
    split = lambda dims: P(("y", "core"), "col", *(None,) * dims)
    placed = (
        split(3), split(3), split(3), P(), split(2), split(1), split(2), split(4), split(4), split(2), split(1),
        P("col", None),
    )
    return jax.shard_map(
        per_device,
        mesh=mesh,
        in_specs=placed,
        out_specs=(split(3), split(3), split(3)),
        check_vma=False,
    )
```
